512 devices in a mesh: lon: 64 (over z, y_hi, core), lat: 8 (over x, y_lo).
Axes of the slice: x: 4, y: 8 (y_hi: 4, y_lo: 2; y = y_hi * 2 + y_lo), z: 8, core: 2. Of those that a mesh axis runs over, the one named last changes fastest.
Arguments:
- activations: bfloat16 [4, 48, 768, 512], P(None, 'lat', 'lon'), may hold values from -6 to 6
- cotangent: bfloat16 [4, 48, 768, 512], P(None, 'lat', 'lon'), may hold values from -6 to 6
- qkv_weight: bfloat16 [512, 1536], replicated, may hold values from -0.397747564 to 0.397747564, as said below
- proj_weight: bfloat16 [512, 512], replicated, may hold values from -0.25 to 0.25
Outputs:
- input_grad: bfloat16 [4, 48, 768, 512], P(None, 'lat', 'lon')
- qkv_weight_grad: bfloat16 [512, 1536], replicated
- proj_weight_grad: bfloat16 [512, 512], replicated
The draws below stay inside these ranges and needn't reach their ends.
Inputs may be any that keep to these rules, and one draw needn't show every extreme that they name: `qkv_weight`: most entries of order 512 ** -0.5; a few columns up to 9 times that.
All inputs are finite; a program needn't handle non-finite values.
Results may differ from the reference program's by a relative error of at most 0.01.
Values may be sent and summed in bfloat16 or wider, within the bound.
No kernel may reach another device: no remote copies, remote signals or barrier semaphores. Data moves between devices by JAX's collectives and lax.ppermute only.
A program may use at most 64 MiB of HBM per device.

```python
import jax
import jax.numpy as jnp
from jax import lax

D = 512
HEADS = 8
NL = 4
WIN_LEV = 2
WIN_LAT = 6
WIN_LON = 12
HEAD_DIM = 64
NLAT = 48
NLON = 768
TOKENS = 147456


def draw_qkv_weight(key, part):
    key = jax.random.fold_in(key, 7)
    base = jax.random.truncated_normal(key, -4.0, 4.0, (D, 3 * D), jnp.float32) * D ** (-0.5)
    return base.astype(jnp.bfloat16)


def steps_of(key, dims, cuts, least, largest):
    gain = 1.0
    for position, shards_of in cuts:
        heights = jax.random.uniform(jax.random.fold_in(jax.random.fold_in(key, 6), position), (shards_of,), jnp.float32, least / len(cuts), largest / len(cuts))
        gain = gain * jnp.repeat(jnp.exp(heights), dims[position] // shards_of).reshape((-1,) + (1,) * (len(dims) - 1 - position))
    return gain


def gaussian(rng, extent, scale, reach, shards=(), held_as=jnp.bfloat16):
    entries = jax.random.normal(rng, extent, jnp.float32) * scale
    if len(shards) > 0:
        entries = steps_of(rng, extent, shards, -0.22, 0.18) * entries
    return jnp.clip(entries, min=-reach, max=reach).astype(held_as)


def setup_inputs(seed: int = 0) -> dict:
    key_of = jax.random.split(jax.random.key(seed), 5)
    return {
        "activations": gaussian(key_of[0], (NL, NLAT, NLON, D), 1.0, 6.0, ((1, 8), (2, 64))),
        "cotangent": gaussian(key_of[1], (NL, NLAT, NLON, D), 1.0, 6.0, ((1, 8), (2, 64))),
        "qkv_weight": draw_qkv_weight(jax.random.fold_in(key_of[4], 71), 0),
        "proj_weight": gaussian(key_of[3], (D, D), D ** -0.5, 0.25),
    }


def to_windows(grid):
    levels, rows, cols, width = grid.shape
    blocks = grid.reshape(levels // WIN_LEV, WIN_LEV, rows // WIN_LAT, WIN_LAT, cols // WIN_LON, WIN_LON, width)
    blocks = blocks.transpose(0, 2, 4, 1, 3, 5, 6)
    return blocks.reshape(levels // WIN_LEV * (rows // WIN_LAT), cols // WIN_LON, WIN_LEV * WIN_LAT * WIN_LON, width)

def from_windows(blocks, levels, rows, cols):
    width = blocks.shape[-1]
    grid = blocks.reshape(levels // WIN_LEV, rows // WIN_LAT, cols // WIN_LON, WIN_LEV, WIN_LAT, WIN_LON, width)
    return grid.transpose(0, 3, 1, 4, 2, 5, 6).reshape(levels, rows, cols, width)

def attend(qkv_win, grad_win, same):
    scale = HEAD_DIM ** (-0.5)
    split = qkv_win.reshape(qkv_win.shape[:-1] + (3, HEADS, HEAD_DIM)).astype(jnp.float32)
    query = split[..., 0, :, :]
    keys = split[..., 1, :, :]
    values = split[..., 2, :, :]
    scores = jnp.einsum('bqhd,bkhd->bhqk', query, keys) * scale
    scores = jnp.where(same[:, None], scores, -1000000000.0)
    top = lax.optimization_barrier(jnp.max(scores, axis=-1, keepdims=True))
    expo = jnp.exp(scores - top)
    probs = expo / lax.optimization_barrier(jnp.sum(expo, axis=-1, keepdims=True))
    probs_low = probs.astype(jnp.bfloat16).astype(jnp.float32)
    attended = jnp.einsum('bhqk,bkhd->bqhd', probs_low, values).astype(jnp.bfloat16)
    upstream = grad_win.reshape(grad_win.shape[:-1] + (HEADS, HEAD_DIM)).astype(jnp.float32)
    prob_grad = jnp.einsum('bqhd,bkhd->bhqk', upstream, values)
    value_grad = jnp.einsum('bhqk,bqhd->bkhd', probs_low, upstream).astype(jnp.bfloat16)
    inner = lax.optimization_barrier(jnp.sum(probs * prob_grad, axis=-1, keepdims=True))
    score_grad = (probs * (prob_grad - inner) * scale).astype(jnp.bfloat16).astype(jnp.float32)
    query_grad = jnp.einsum('bhqk,bkhd->bqhd', score_grad, keys).astype(jnp.bfloat16)
    key_grad = jnp.einsum('bhqk,bqhd->bkhd', score_grad, query).astype(jnp.bfloat16)
    qkv_grad = jnp.stack([query_grad, key_grad, value_grad], axis=-3).reshape(qkv_win.shape)
    return (attended.reshape(grad_win.shape), qkv_grad)

def region(index, total, window):
    return jnp.where(index < total - window, 0, jnp.where(index < total - window // 2, 1, 2)).astype(jnp.int32)

def reference(activations, cotangent, qkv_weight, proj_weight):
    shifts = (-(WIN_LEV // 2), -(WIN_LAT // 2), -(WIN_LON // 2))
    rolled_input = jnp.roll(activations, shifts, axis=(0, 1, 2))
    rolled_cot = jnp.roll(cotangent, shifts, axis=(0, 1, 2))
    float_values = rolled_input.astype(jnp.float32)
    centered_input = lax.optimization_barrier(jnp.mean(float_values, axis=-1, keepdims=True))
    variance = lax.optimization_barrier(jnp.mean((float_values - centered_input) ** 2, axis=-1, keepdims=True))
    inverse_deviation = lax.rsqrt(variance + 1e-05)
    standardized_input = (float_values - centered_input) * inverse_deviation
    norm_output = standardized_input.astype(jnp.bfloat16)
    flat_normed = norm_output.reshape(-1, D)
    qkv = jnp.dot(flat_normed, qkv_weight, preferred_element_type=jnp.float32).astype(jnp.bfloat16)
    flat_cot = rolled_cot.reshape(-1, D)
    attended_grad = jnp.dot(flat_cot, proj_weight.T, preferred_element_type=jnp.float32).astype(jnp.bfloat16)
    level_label = region(jnp.arange(NL), NL, WIN_LEV)
    lat_label = region(jnp.arange(NLAT), NLAT, WIN_LAT)
    lon_label = region(jnp.arange(NLON), NLON, WIN_LON)
    labels = 9 * level_label[:, None, None, None] + 3 * lat_label[None, :, None, None] + lon_label[None, None, :, None]
    labels = jnp.broadcast_to(labels, (NL, NLAT, NLON, 1)).astype(jnp.int32)
    label_win = to_windows(labels)[..., 0]
    same = label_win[..., :, None] == label_win[..., None, :]
    qkv_win = to_windows(qkv.reshape(NL, NLAT, NLON, 3 * D))
    grad_win = to_windows(attended_grad.reshape(NL, NLAT, NLON, D))
    attended_win, qkv_grad_win = lax.map(lambda items: attend(items[0], items[1], items[2]), (qkv_win, grad_win, same))
    attended = from_windows(attended_win, NL, NLAT, NLON).reshape(-1, D)
    qkv_grad = from_windows(qkv_grad_win, NL, NLAT, NLON).reshape(-1, 3 * D)
    norm_output_gradient = jnp.dot(qkv_grad, qkv_weight.T, preferred_element_type=jnp.float32).reshape(NL, NLAT, NLON, D)
    average_gradient = lax.optimization_barrier(jnp.mean(norm_output_gradient, axis=-1, keepdims=True))
    average_product = lax.optimization_barrier(jnp.mean(norm_output_gradient * standardized_input, axis=-1, keepdims=True))
    residual_branch_gradient = (inverse_deviation * (norm_output_gradient - average_gradient - standardized_input * average_product)).astype(jnp.bfloat16)
    unrolled = jnp.roll(residual_branch_gradient, (WIN_LEV // 2, WIN_LAT // 2, WIN_LON // 2), axis=(0, 1, 2))
    input_grad = (cotangent.astype(jnp.float32) + unrolled.astype(jnp.float32)).astype(jnp.bfloat16)
    factor = TOKENS ** (-0.5)
    qkv_weight_grad = (jnp.dot(flat_normed.T, qkv_grad, preferred_element_type=jnp.float32) * factor).astype(jnp.bfloat16)
    proj_weight_grad = (jnp.dot(attended.T, flat_cot, preferred_element_type=jnp.float32) * factor).astype(jnp.bfloat16)
    return (input_grad, qkv_weight_grad, proj_weight_grad)
```

```python
import jax
import jax.numpy as jnp
from jax import lax
from jax.experimental import pallas as pl
from jax.experimental.pallas import tpu as pltpu
from jax.sharding import Mesh, PartitionSpec as P

D = 512
HEADS = 8
HEAD_DIM = 64
GROUP = 4
LEVELS = 4
HALF_LAT = 3
HALF_LON = 6
ROWS = 6
COLS = 12
PAIRS = ((1, 2), (3, 0))
QUARTER = 2 * HALF_LAT * HALF_LON
WINDOW = 4 * QUARTER
TOKENS = 2 * WINDOW

LON = ("z2", "z1", "z0", "y2", "y1", "core")
LAT = ("x1", "x0", "y0")
CORE = ("core",)
NEAR = ("z0", "y0", "x0")
MIDDLE = ("x1", "z2", "z1")
FAR = ("y2", "y1")


def dot(a, b, a_dim, b_dim):
    return lax.dot_general(a, b, (((a_dim,), (b_dim,)), ((), ())), preferred_element_type=jnp.float32)


def owner_of(kind, lat, lon):
    lat = lat + kind // 2
    return lat, lon + kind % 2 * (-1 if lat % 2 == 1 else 1)


def moved(value, kind, back):
    lons, lats = lax.axis_size(LON), lax.axis_size(LAT)
    pairs = []
    for lon in range(lons):
        for lat in range(lats):
            to_lat, to_lon = owner_of(kind, lat, lon)
            pair = (lon * lats + lat, to_lon % lons * lats + to_lat % lats)
            pairs.append(pair[::-1] if back else pair)
    return lax.ppermute(value, LON + LAT, pairs)


def token_labels(token, window, lat_edge, lon_edge):
    quarter = token // QUARTER
    level = token % QUARTER // (QUARTER // 2)
    return level * window + 2 * lat_edge * (quarter // 2) + 4 * lon_edge * (quarter % 2)


def pack_kernel(place, act_ref, cot_ref, own, lon, lat, both):
    pieces = {(row_half, col_half): [] for row_half in range(2) for col_half in range(2)}
    for ref in (act_ref, cot_ref):
        for pair in PAIRS:
            for level in pair:
                for row in range(ROWS):
                    line = ref[level, row].astype(jnp.float32)
                    for half in range(2):
                        cut = line[half * HALF_LON : half * HALF_LON + HALF_LON]
                        pieces[row // HALF_LAT, half].append(cut)
    whole = {at: jnp.concatenate(cuts, axis=0).astype(jnp.bfloat16) for at, cuts in pieces.items()}

    def put(parity):
        own[...] = whole[0, parity]
        lon[...] = whole[0, 1 - parity]
        lat[...] = whole[1, 1 - parity]
        both[...] = whole[1, parity]

    for parity in range(2):
        pl.when(place[0] == parity)(lambda parity=parity: put(parity))


def pack(place, activations, cotangent):
    whole = pl.BlockSpec(memory_space=pltpu.VMEM)
    return pl.pallas_call(
        pack_kernel,
        out_shape=(jax.ShapeDtypeStruct((4 * QUARTER, D), jnp.bfloat16),) * 4,
        in_specs=[pl.BlockSpec(memory_space=pltpu.SMEM)] + [whole] * 2,
        out_specs=(whole,) * 4,
        compiler_params=pltpu.CompilerParams(vmem_limit_bytes=32 * 2**20),
        cost_estimate=pl.CostEstimate(flops=0, bytes_accessed=1200000, transcendentals=0),
        name="pack",
    )(place, activations, cotangent)


def unpack_kernel(place, cot_ref, *refs):
    own, lon, lat, both = [ref[...].astype(jnp.float32) for ref in refs[:4]]
    out = refs[4]
    even = place[0] == 0
    whole = {
        (0, 0): jnp.where(even, own, lon),
        (0, 1): jnp.where(even, lon, own),
        (1, 0): jnp.where(even, both, lat),
        (1, 1): jnp.where(even, lat, both),
    }
    at = [0, 0]
    for pair in PAIRS:
        for level in pair:
            for row in range(ROWS):
                half = row // HALF_LAT
                cuts = [whole[half, col_half][at[half] : at[half] + HALF_LON] for col_half in range(2)]
                at[half] += HALF_LON
                line = cot_ref[level, row].astype(jnp.float32) + jnp.concatenate(cuts, axis=0)
                out[level, row] = line.astype(jnp.bfloat16)


def unpack(place, cotangent, quarters):
    whole = pl.BlockSpec(memory_space=pltpu.VMEM)
    return pl.pallas_call(
        unpack_kernel,
        out_shape=jax.ShapeDtypeStruct(cotangent.shape, jnp.bfloat16),
        in_specs=[pl.BlockSpec(memory_space=pltpu.SMEM)] + [whole] * 5,
        out_specs=whole,
        compiler_params=pltpu.CompilerParams(vmem_limit_bytes=32 * 2**20),
        cost_estimate=pl.CostEstimate(flops=0, bytes_accessed=900000, transcendentals=0),
        name="unpack",
    )(place, cotangent, *quarters)


def block_kernel(place, *refs):
    quarters, (qkv_weight, proj_weight), branch, (grads_ref, x_held, cot_held) = refs[:4], refs[4:6], refs[6:10], refs[10:13]
    normed, qkv, upstream, attended, qkv_grad = refs[13:]
    held = [ref[...].astype(jnp.float32) for ref in quarters]
    for kind, target in enumerate((x_held, cot_held)):
        chunks = [
            held[quarter][(2 * kind + window) * QUARTER : (2 * kind + window + 1) * QUARTER]
            for window in range(2)
            for quarter in range(4)
        ]
        target[...] = jnp.concatenate(chunks, axis=0).astype(jnp.bfloat16)
    x = x_held[...].astype(jnp.float32)
    centered = x - jnp.mean(x, axis=-1, keepdims=True)
    inverse = lax.rsqrt(jnp.mean(centered * centered, axis=-1, keepdims=True) + 1e-05)
    normed[...] = (centered * inverse).astype(jnp.bfloat16)

    @pl.loop(0, 3 * D // 256)
    def _(step):
        cols = pl.ds(pl.multiple_of(step * 256, 256), 256)
        gain = jnp.where(step < D // 256, HEAD_DIM ** (-0.5), 1.0)
        qkv[:, cols] = (dot(normed[...], qkv_weight[:, cols], 1, 0) * gain).astype(jnp.bfloat16)

    @pl.loop(0, D // 256)
    def _(step):
        cols = pl.ds(pl.multiple_of(step * 256, 256), 256)
        upstream[:, cols] = dot(cot_held[...], proj_weight[cols, :], 1, 1).astype(jnp.bfloat16)

    head_of = lax.broadcasted_iota(jnp.int32, (WINDOW, GROUP * HEAD_DIM), 1) // HEAD_DIM
    zero = jnp.zeros((WINDOW, GROUP * HEAD_DIM), jnp.bfloat16)

    def apart(slab):
        return jnp.concatenate([jnp.where(head_of == head, slab, zero) for head in range(GROUP)], axis=0)

    def together(tall):
        merged = tall[:WINDOW]
        for head in range(1, GROUP):
            merged = jnp.where(head_of == head, tall[head * WINDOW : (head + 1) * WINDOW], merged)
        return merged.astype(jnp.bfloat16)

    for window in range(2):
        rows = slice(window * WINDOW, (window + 1) * WINDOW)
        shape = (WINDOW, GROUP * WINDOW)
        key_label = token_labels(lax.broadcasted_iota(jnp.int32, shape, 0), window, place[1], place[2])
        query_label = token_labels(lax.broadcasted_iota(jnp.int32, shape, 1) % WINDOW, window, place[1], place[2])
        bias = jnp.where(key_label == query_label, 0.0, -1000000000.0)
        for group in range(HEADS // GROUP):
            cols = [slice(part * D + group * GROUP * HEAD_DIM, part * D + (group + 1) * GROUP * HEAD_DIM) for part in range(3)]
            query, keys, values = (qkv[rows, at] for at in cols)
            query, grad = apart(query), apart(upstream[rows, cols[0]])
            scores = dot(keys, query, 1, 1) + bias
            expo = jnp.exp(scores - jnp.max(scores, axis=0, keepdims=True))
            probs = expo * (1.0 / jnp.sum(expo, axis=0, keepdims=True))
            low = probs.astype(jnp.bfloat16)
            prob_grad = dot(values, grad, 1, 1)
            inner = jnp.sum(probs * prob_grad, axis=0, keepdims=True)
            score_grad = (probs * (prob_grad - inner)).astype(jnp.bfloat16)
            attended[rows, cols[0]] = together(dot(low, values, 0, 0))
            qkv_grad[rows, cols[0]] = together(dot(score_grad, keys, 0, 0) * HEAD_DIM ** (-0.5))
            qkv_grad[rows, cols[1]] = dot(score_grad, query, 1, 0).astype(jnp.bfloat16)
            qkv_grad[rows, cols[2]] = dot(low, grad, 1, 0).astype(jnp.bfloat16)

    normed_grad = dot(qkv_grad[...], qkv_weight[...], 1, 1)
    x = x_held[...].astype(jnp.float32)
    centered = x - jnp.mean(x, axis=-1, keepdims=True)
    inverse = lax.rsqrt(jnp.mean(centered * centered, axis=-1, keepdims=True) + 1e-05)
    xhat = centered * inverse
    average = jnp.mean(normed_grad, axis=-1, keepdims=True)
    product = jnp.mean(normed_grad * xhat, axis=-1, keepdims=True)
    dx = inverse * (normed_grad - average - xhat * product)
    for quarter in range(4):
        chunks = [dx[(4 * window + quarter) * QUARTER : (4 * window + quarter + 1) * QUARTER] for window in range(2)]
        branch[quarter][...] = jnp.concatenate(chunks, axis=0).astype(jnp.bfloat16)

    def put(step, block):
        block = block.astype(jnp.bfloat16)
        for half in range(2):
            grads_ref[:, 2 * step + half] = block[:, 128 * half : 128 * half + 128].reshape(D // 16, 16, 128)

    @pl.loop(0, 3 * D // 256)
    def _(step):
        cols = pl.ds(pl.multiple_of(step * 256, 256), 256)
        put(step, dot(normed[...], qkv_grad[:, cols], 0, 0))

    @pl.loop(0, D // 256)
    def _(step):
        cols = pl.ds(pl.multiple_of(step * 256, 256), 256)
        put(step + 3 * D // 256, dot(attended[...], cot_held[:, cols], 0, 0))


def block(place, quarters, qkv_weight, proj_weight):
    whole = pl.BlockSpec(memory_space=pltpu.VMEM)
    return pl.pallas_call(
        block_kernel,
        out_shape=(jax.ShapeDtypeStruct((2 * QUARTER, D), jnp.bfloat16),) * 4
        + (jax.ShapeDtypeStruct((D // 16, 4 * D // 128, 16, 128), jnp.bfloat16),),
        in_specs=[pl.BlockSpec(memory_space=pltpu.SMEM)] + [whole] * 6,
        out_specs=(whole,) * 5,
        scratch_shapes=[
            pltpu.VMEM((TOKENS, D), jnp.bfloat16),
            pltpu.VMEM((TOKENS, D), jnp.bfloat16),
            pltpu.VMEM((TOKENS, D), jnp.bfloat16),
            pltpu.VMEM((TOKENS, 3 * D), jnp.bfloat16),
            pltpu.VMEM((TOKENS, D), jnp.bfloat16),
            pltpu.VMEM((TOKENS, D), jnp.bfloat16),
            pltpu.VMEM((TOKENS, 3 * D), jnp.bfloat16),
        ],
        compiler_params=pltpu.CompilerParams(vmem_limit_bytes=48 * 2**20),
        cost_estimate=pl.CostEstimate(flops=2 * 10**9, bytes_accessed=6 * 10**6, transcendentals=6 * 10**5),
        name="block",
    )(place, *quarters, qkv_weight, proj_weight)


def added(arrived):
    total = arrived[0].astype(jnp.float32)
    for part in range(1, arrived.shape[0]):
        total = total + arrived[part].astype(jnp.float32)
    return total


def scattered_sum(tiles, axes):
    groups = lax.axis_size(axes)
    split = tiles.reshape((groups, tiles.shape[0] // groups) + tiles.shape[1:])
    return added(lax.all_to_all(split, axes, 0, 0))


def exchanged(tiles, axes):
    groups = lax.axis_size(axes)
    return lax.all_to_all(jnp.broadcast_to(tiles[None], (groups,) + tiles.shape), axes, 0, 0)


def summed_over_mesh(tiles, factor, branch):
    tiles = scattered_sum(tiles, CORE).astype(jnp.bfloat16)
    tiles, branch = lax.optimization_barrier((tiles, branch))
    tiles = scattered_sum(tiles, NEAR).astype(jnp.bfloat16)
    quarters = [branch[0]] + [moved(branch[kind], kind, True) for kind in range(1, 4)]
    tiles, quarters = lax.optimization_barrier((tiles, quarters))
    tiles = scattered_sum(tiles, MIDDLE).astype(jnp.bfloat16)
    tiles = (added(exchanged(tiles, FAR)) * factor).astype(jnp.bfloat16)
    tiles, quarters = lax.optimization_barrier((exchanged(tiles, MIDDLE), quarters))
    tiles = tiles.reshape((-1,) + tiles.shape[2:])
    for axes in (NEAR, CORE):
        tiles = exchanged(tiles, axes)
        tiles = tiles.reshape((-1,) + tiles.shape[2:])
    return tiles, quarters


def untile_kernel(tiles, qkv_out, proj_out):
    for col in range(4 * D // 128):
        strip = tiles[:, col].reshape(D, 128)
        if col < 3 * D // 128:
            qkv_out[:, 128 * col : 128 * col + 128] = strip
        else:
            proj_out[:, 128 * col - 3 * D : 128 * col - 3 * D + 128] = strip


def untile(tiles):
    whole = pl.BlockSpec(memory_space=pltpu.VMEM)
    return pl.pallas_call(
        untile_kernel,
        out_shape=(jax.ShapeDtypeStruct((D, 3 * D), jnp.bfloat16), jax.ShapeDtypeStruct((D, D), jnp.bfloat16)),
        in_specs=[whole],
        out_specs=(whole, whole),
        compiler_params=pltpu.CompilerParams(vmem_limit_bytes=32 * 2**20),
        cost_estimate=pl.CostEstimate(flops=0, bytes_accessed=4 * 2**20, transcendentals=0),
        name="untile",
    )(tiles)


def per_device(activations, cotangent, qkv_weight, proj_weight):
    lat, lon = lax.axis_index(LAT), lax.axis_index(LON)
    odd = lat % 2 == 1
    lon_edge = jnp.where(odd, lon == lax.axis_size(LON) - 1, lon == 0)
    place = jnp.stack([odd, lat == 0, lon_edge]).astype(jnp.int32)
    quarters = pack(place, activations, cotangent)
    quarters = [quarters[0]] + [moved(quarters[kind], kind, False) for kind in range(1, 4)]
    *branch, grads = block(place, quarters, qkv_weight, proj_weight)
    factor = (LEVELS * ROWS * COLS * lax.axis_size(LON + LAT)) ** (-0.5)
    tiles, quarters = summed_over_mesh(grads.reshape(-1, 16, 128), factor, branch)
    qkv_weight_grad, proj_weight_grad = untile(tiles.reshape(D // 16, 4 * D // 128, 16, 128))
    return (unpack(place, cotangent, quarters), qkv_weight_grad, proj_weight_grad)


def over(physical):
    spec = P(None, LAT, LON, None)
    return jax.shard_map(
        per_device,
        mesh=physical,
        in_specs=(spec, spec, P(), P()),
        out_specs=(spec, P(), P()),
        check_vma=False,
    )


def solution(mesh):
    return over(Mesh(mesh.devices.reshape((2,) * 9), LON + LAT))
```

```python
import jax
import jax.numpy as jnp
from jax import lax
from jax.experimental import pallas as pl
from jax.experimental.pallas import tpu as pltpu
from jax.sharding import Mesh, PartitionSpec as P

D = 512
HEADS = 8
HEAD_DIM = 64
GROUP = 4
LEVELS = 4
HALF_LAT = 3
HALF_LON = 6
ROWS = 6
COLS = 12
PAIRS = ((1, 2), (3, 0))
QUARTER = 2 * HALF_LAT * HALF_LON
WINDOW = 4 * QUARTER
TOKENS = 2 * WINDOW

LON = ("z", "y_hi", "core")
LAT = ("x", "y_lo")
ALL = LON + LAT


def dot(a, b, a_dim, b_dim):
    return lax.dot_general(a, b, (((a_dim,), (b_dim,)), ((), ())), preferred_element_type=jnp.float32)


def owner_of(kind, lat, lon):
    lat = lat + kind // 2
    return lat, lon + kind % 2 * (-1 if lat % 2 == 1 else 1)


def moved(value, kind, back):
    lons, lats = lax.axis_size(LON), lax.axis_size(LAT)
    pairs = []
    for lon in range(lons):
        for lat in range(lats):
            to_lat, to_lon = owner_of(kind, lat, lon)
            pair = (lon * lats + lat, to_lon % lons * lats + to_lat % lats)
            pairs.append(pair[::-1] if back else pair)
    return lax.ppermute(value, ALL, pairs)


def token_labels(token, window, lat_edge, lon_edge):
    quarter = token // QUARTER
    level = token % QUARTER // (QUARTER // 2)
    return level * window + 2 * lat_edge * (quarter // 2) + 4 * lon_edge * (quarter % 2)


def pack_kernel(place, act_ref, cot_ref, own, lon, lat, both):
    pieces = {(row_half, col_half): [] for row_half in range(2) for col_half in range(2)}
    for ref in (act_ref, cot_ref):
        for pair in PAIRS:
            for level in pair:
                for row in range(ROWS):
                    line = ref[level, row].astype(jnp.float32)
                    for half in range(2):
                        cut = line[half * HALF_LON : half * HALF_LON + HALF_LON]
                        pieces[row // HALF_LAT, half].append(cut)
    whole = {at: jnp.concatenate(cuts, axis=0).astype(jnp.bfloat16) for at, cuts in pieces.items()}

    def put(parity):
        own[...] = whole[0, parity]
        lon[...] = whole[0, 1 - parity]
        lat[...] = whole[1, 1 - parity]
        both[...] = whole[1, parity]

    for parity in range(2):
        pl.when(place[0] == parity)(lambda parity=parity: put(parity))


def pack(place, activations, cotangent):
    whole = pl.BlockSpec(memory_space=pltpu.VMEM)
    return pl.pallas_call(
        pack_kernel,
        out_shape=(jax.ShapeDtypeStruct((4 * QUARTER, D), jnp.bfloat16),) * 4,
        in_specs=[pl.BlockSpec(memory_space=pltpu.SMEM)] + [whole] * 2,
        out_specs=(whole,) * 4,
        compiler_params=pltpu.CompilerParams(vmem_limit_bytes=32 * 2**20),
        cost_estimate=pl.CostEstimate(flops=0, bytes_accessed=1200000, transcendentals=0),
        name="pack",
    )(place, activations, cotangent)


def unpack_kernel(place, cot_ref, *refs):
    own, lon, lat, both = [ref[...].astype(jnp.float32) for ref in refs[:4]]
    out = refs[4]
    even = place[0] == 0
    whole = {
        (0, 0): jnp.where(even, own, lon),
        (0, 1): jnp.where(even, lon, own),
        (1, 0): jnp.where(even, both, lat),
        (1, 1): jnp.where(even, lat, both),
    }
    at = [0, 0]
    for pair in PAIRS:
        for level in pair:
            for row in range(ROWS):
                half = row // HALF_LAT
                cuts = [whole[half, col_half][at[half] : at[half] + HALF_LON] for col_half in range(2)]
                at[half] += HALF_LON
                line = cot_ref[level, row].astype(jnp.float32) + jnp.concatenate(cuts, axis=0)
                out[level, row] = line.astype(jnp.bfloat16)


def unpack(place, cotangent, quarters):
    whole = pl.BlockSpec(memory_space=pltpu.VMEM)
    return pl.pallas_call(
        unpack_kernel,
        out_shape=jax.ShapeDtypeStruct(cotangent.shape, jnp.bfloat16),
        in_specs=[pl.BlockSpec(memory_space=pltpu.SMEM)] + [whole] * 5,
        out_specs=whole,
        compiler_params=pltpu.CompilerParams(vmem_limit_bytes=32 * 2**20),
        cost_estimate=pl.CostEstimate(flops=0, bytes_accessed=900000, transcendentals=0),
        name="unpack",
    )(place, cotangent, *quarters)


def block_kernel(place, *refs):
    quarters, (qkv_weight, proj_weight), branch, (grads_ref, x_held, cot_held) = refs[:4], refs[4:6], refs[6:10], refs[10:13]
    normed, qkv, upstream, attended, qkv_grad = refs[13:]
    held = [ref[...].astype(jnp.float32) for ref in quarters]
    for kind, target in enumerate((x_held, cot_held)):
        chunks = [
            held[quarter][(2 * kind + window) * QUARTER : (2 * kind + window + 1) * QUARTER]
            for window in range(2)
            for quarter in range(4)
        ]
        target[...] = jnp.concatenate(chunks, axis=0).astype(jnp.bfloat16)
    x = x_held[...].astype(jnp.float32)
    centered = x - jnp.mean(x, axis=-1, keepdims=True)
    inverse = lax.rsqrt(jnp.mean(centered * centered, axis=-1, keepdims=True) + 1e-05)
    normed[...] = (centered * inverse).astype(jnp.bfloat16)

    @pl.loop(0, 3 * D // 256)
    def _(step):
        cols = pl.ds(pl.multiple_of(step * 256, 256), 256)
        gain = jnp.where(step < D // 256, HEAD_DIM ** (-0.5), 1.0)
        qkv[:, cols] = (dot(normed[...], qkv_weight[:, cols], 1, 0) * gain).astype(jnp.bfloat16)

    @pl.loop(0, D // 256)
    def _(step):
        cols = pl.ds(pl.multiple_of(step * 256, 256), 256)
        upstream[:, cols] = dot(cot_held[...], proj_weight[cols, :], 1, 1).astype(jnp.bfloat16)

    head_of = lax.broadcasted_iota(jnp.int32, (WINDOW, GROUP * HEAD_DIM), 1) // HEAD_DIM
    zero = jnp.zeros((WINDOW, GROUP * HEAD_DIM), jnp.bfloat16)

    def apart(slab):
        return jnp.concatenate([jnp.where(head_of == head, slab, zero) for head in range(GROUP)], axis=0)

    def together(tall):
        merged = tall[:WINDOW]
        for head in range(1, GROUP):
            merged = jnp.where(head_of == head, tall[head * WINDOW : (head + 1) * WINDOW], merged)
        return merged.astype(jnp.bfloat16)

    for window in range(2):
        rows = slice(window * WINDOW, (window + 1) * WINDOW)
        shape = (WINDOW, GROUP * WINDOW)
        key_label = token_labels(lax.broadcasted_iota(jnp.int32, shape, 0), window, place[1], place[2])
        query_label = token_labels(lax.broadcasted_iota(jnp.int32, shape, 1) % WINDOW, window, place[1], place[2])
        bias = jnp.where(key_label == query_label, 0.0, -1000000000.0)
        for group in range(HEADS // GROUP):
            cols = [slice(part * D + group * GROUP * HEAD_DIM, part * D + (group + 1) * GROUP * HEAD_DIM) for part in range(3)]
            query, keys, values = (qkv[rows, at] for at in cols)
            query, grad = apart(query), apart(upstream[rows, cols[0]])
            scores = dot(keys, query, 1, 1) + bias
            expo = jnp.exp(scores - jnp.max(scores, axis=0, keepdims=True))
            probs = expo * (1.0 / jnp.sum(expo, axis=0, keepdims=True))
            low = probs.astype(jnp.bfloat16)
            prob_grad = dot(values, grad, 1, 1)
            inner = jnp.sum(probs * prob_grad, axis=0, keepdims=True)
            score_grad = (probs * (prob_grad - inner)).astype(jnp.bfloat16)
            attended[rows, cols[0]] = together(dot(low, values, 0, 0))
            qkv_grad[rows, cols[0]] = together(dot(score_grad, keys, 0, 0) * HEAD_DIM ** (-0.5))
            qkv_grad[rows, cols[1]] = dot(score_grad, query, 1, 0).astype(jnp.bfloat16)
            qkv_grad[rows, cols[2]] = dot(low, grad, 1, 0).astype(jnp.bfloat16)

    normed_grad = dot(qkv_grad[...], qkv_weight[...], 1, 1)
    x = x_held[...].astype(jnp.float32)
    centered = x - jnp.mean(x, axis=-1, keepdims=True)
    inverse = lax.rsqrt(jnp.mean(centered * centered, axis=-1, keepdims=True) + 1e-05)
    xhat = centered * inverse
    average = jnp.mean(normed_grad, axis=-1, keepdims=True)
    product = jnp.mean(normed_grad * xhat, axis=-1, keepdims=True)
    dx = inverse * (normed_grad - average - xhat * product)
    for quarter in range(4):
        chunks = [dx[(4 * window + quarter) * QUARTER : (4 * window + quarter + 1) * QUARTER] for window in range(2)]
        branch[quarter][...] = jnp.concatenate(chunks, axis=0).astype(jnp.bfloat16)

    def put(step, block):
        block = block.astype(jnp.bfloat16)
        for half in range(2):
            grads_ref[:, 2 * step + half] = block[:, 128 * half : 128 * half + 128].reshape(D // 16, 16, 128)

    @pl.loop(0, 3 * D // 256)
    def _(step):
        cols = pl.ds(pl.multiple_of(step * 256, 256), 256)
        put(step, dot(normed[...], qkv_grad[:, cols], 0, 0))

    @pl.loop(0, D // 256)
    def _(step):
        cols = pl.ds(pl.multiple_of(step * 256, 256), 256)
        put(step + 3 * D // 256, dot(attended[...], cot_held[:, cols], 0, 0))


def block(place, quarters, qkv_weight, proj_weight):
    whole = pl.BlockSpec(memory_space=pltpu.VMEM)
    return pl.pallas_call(
        block_kernel,
        out_shape=(jax.ShapeDtypeStruct((2 * QUARTER, D), jnp.bfloat16),) * 4
        + (jax.ShapeDtypeStruct((D // 16, 4 * D // 128, 16, 128), jnp.bfloat16),),
        in_specs=[pl.BlockSpec(memory_space=pltpu.SMEM)] + [whole] * 6,
        out_specs=(whole,) * 5,
        scratch_shapes=[
            pltpu.VMEM((TOKENS, D), jnp.bfloat16),
            pltpu.VMEM((TOKENS, D), jnp.bfloat16),
            pltpu.VMEM((TOKENS, D), jnp.bfloat16),
            pltpu.VMEM((TOKENS, 3 * D), jnp.bfloat16),
            pltpu.VMEM((TOKENS, D), jnp.bfloat16),
            pltpu.VMEM((TOKENS, D), jnp.bfloat16),
            pltpu.VMEM((TOKENS, 3 * D), jnp.bfloat16),
        ],
        compiler_params=pltpu.CompilerParams(vmem_limit_bytes=48 * 2**20),
        cost_estimate=pl.CostEstimate(flops=2 * 10**9, bytes_accessed=6 * 10**6, transcendentals=6 * 10**5),
        name="block",
    )(place, *quarters, qkv_weight, proj_weight)


def added(arrived):
    total = arrived[0].astype(jnp.float32)
    for part in range(1, arrived.shape[0]):
        total = total + arrived[part].astype(jnp.float32)
    return total


def device_groups(members):
    tall, wide = lax.axis_size("y_hi"), lax.axis_size("x")
    cores, y_los = lax.axis_size("core"), lax.axis_size("y_lo")

    def index(z, y, x, core):
        return (((z * tall + y // y_los) * cores + core) * wide + x) * y_los + y % y_los

    return [[index(*at, core) for at in group] for core in range(cores) for group in members(core)]


def chips():
    return lax.axis_size("z"), lax.axis_size("y_hi") * lax.axis_size("y_lo"), lax.axis_size("x")


def near_groups():
    def along(size, core):
        if size == 1:
            return [[0]]
        return [[(2 * at + 2 * core) % size, 2 * at + 1] for at in range(size // 2)]

    def members(core):
        zs, ys, xs = (along(size, core) for size in chips())
        return [[(z, y, x) for z in za for y in ya for x in xa] for za in zs for ya in ys for xa in xs]

    return device_groups(members)


def strided(size):
    step = min(size, 2)
    return [list(range(parity, size, step)) for parity in range(step)]


def middle_groups():
    def members(core):
        z_size, y_size, x_size = chips()
        xs = strided(x_size)
        if core == 0:
            return [[(z, y, x) for x in xa for z in za] for xa in xs for za in strided(z_size) for y in range(y_size)]
        return [[(z, y, x) for x in xa for y in ya] for xa in xs for ya in strided(y_size) for z in range(z_size)]

    return device_groups(members)


def far_groups():
    def members(core):
        z_size, y_size, x_size = chips()
        if core == 0:
            return [[(z, y, x) for y in ya] for ya in strided(y_size) for z in range(z_size) for x in range(x_size)]
        return [[(z, y, x) for z in za] for za in strided(z_size) for y in range(y_size) for x in range(x_size)]

    return device_groups(members)


def core_groups():
    z_size, y_size, x_size = chips()
    at = [(z, y, x) for z in range(z_size) for y in range(y_size) for x in range(x_size)]
    singles = device_groups(lambda core: [at])
    return [list(pair) for pair in zip(*singles)]


def all_to_all(split, groups):
    return lax.all_to_all(split, ALL, 0, 0, axis_index_groups=groups)


def scattered_sum(tiles, groups):
    count = len(groups[0])
    split = tiles.reshape((count, tiles.shape[0] // count) + tiles.shape[1:])
    return added(all_to_all(split, groups)).astype(jnp.bfloat16)


def exchanged(tiles, groups):
    return all_to_all(jnp.broadcast_to(tiles[None], (len(groups[0]),) + tiles.shape), groups)


def gathered(tiles, groups):
    return exchanged(tiles, groups).reshape((-1,) + tiles.shape[1:])


def summed_over_mesh(tiles, factor, branch):
    core, near, middle, far = core_groups(), near_groups(), middle_groups(), far_groups()
    lon = moved(branch[1], 1, True)
    tiles, lat, both = lax.optimization_barrier((scattered_sum(tiles, core), *branch[2:]))
    tiles, lon, lat = lax.optimization_barrier((scattered_sum(tiles, near), lon, moved(lat, 2, True)))
    tiles = scattered_sum(tiles, middle)
    tiles = (added(exchanged(tiles, far)) * factor).astype(jnp.bfloat16)
    tiles, both = lax.optimization_barrier((gathered(tiles, middle), both))
    tiles, both = lax.optimization_barrier((gathered(tiles, near), moved(both, 3, True)))
    return gathered(tiles, core), (branch[0], lon, lat, both)


def untile_kernel(tiles, qkv_out, proj_out):
    for col in range(4 * D // 128):
        strip = tiles[:, col].reshape(-1, 128)
        if col < 3 * D // 128:
            qkv_out[:, 128 * col : 128 * col + 128] = strip
        else:
            proj_out[:, 128 * col - 3 * D : 128 * col - 3 * D + 128] = strip


def untile(tiles):
    steps = 4
    return pl.pallas_call(
        untile_kernel,
        grid=(steps,),
        out_shape=(jax.ShapeDtypeStruct((D, 3 * D), jnp.bfloat16), jax.ShapeDtypeStruct((D, D), jnp.bfloat16)),
        in_specs=[pl.BlockSpec((D // 16 // steps, 4 * D // 128, 16, 128), lambda i: (i, 0, 0, 0))],
        out_specs=(
            pl.BlockSpec((D // steps, 3 * D), lambda i: (i, 0)),
            pl.BlockSpec((D // steps, D), lambda i: (i, 0)),
        ),
        compiler_params=pltpu.CompilerParams(vmem_limit_bytes=32 * 2**20),
        cost_estimate=pl.CostEstimate(flops=0, bytes_accessed=4 * 2**20, transcendentals=0),
        name="untile",
    )(tiles)


def per_device(activations, cotangent, qkv_weight, proj_weight):
    lat, lon = lax.axis_index(LAT), lax.axis_index(LON)
    odd = lat % 2 == 1
    lon_edge = jnp.where(odd, lon == lax.axis_size(LON) - 1, lon == 0)
    place = jnp.stack([odd, lat == 0, lon_edge]).astype(jnp.int32)
    quarters = pack(place, activations, cotangent)
    quarters = [quarters[0]] + [moved(quarters[kind], kind, False) for kind in range(1, 4)]
    *branch, grads = block(place, quarters, qkv_weight, proj_weight)
    factor = (LEVELS * ROWS * COLS * lax.axis_size(ALL)) ** (-0.5)
    tiles, quarters = summed_over_mesh(grads.reshape(-1, 16, 128), factor, branch)
    qkv_weight_grad, proj_weight_grad = untile(tiles.reshape(D // 16, 4 * D // 128, 16, 128))
    return (unpack(place, cotangent, quarters), qkv_weight_grad, proj_weight_grad)


def over(physical):
    spec = P(None, LAT, LON, None)
    return jax.shard_map(
        per_device,
        mesh=physical,
        in_specs=(spec, spec, P(), P()),
        out_specs=(spec, P(), P()),
        check_vma=False,
    )


def solution(mesh):
    return over(Mesh(mesh.devices.reshape(8, 4, 2, 4, 2), ALL))
```

```python
import itertools

import jax
import jax.numpy as jnp
from jax import lax
from jax.experimental import pallas as pl
from jax.experimental.pallas import tpu as pltpu
from jax.sharding import Mesh, PartitionSpec as P

D = 512
HEADS = 8
HEAD_DIM = 64
GROUP = 4
LEVELS = 4
HALF_LAT = 3
HALF_LON = 6
ROWS = 6
COLS = 12
PAIRS = ((1, 2), (3, 0))
QUARTER = 2 * HALF_LAT * HALF_LON
WINDOW = 4 * QUARTER
TOKENS = 2 * WINDOW

LON = ("z", "y_hi", "core")
LAT = ("x", "y_lo")
ALL = LON + LAT


def dot(a, b, a_dim, b_dim):
    return lax.dot_general(a, b, (((a_dim,), (b_dim,)), ((), ())), preferred_element_type=jnp.float32)


def owner_of(kind, lat, lon):
    lat = lat + kind // 2
    return lat, lon + kind % 2 * (-1 if lat % 2 == 1 else 1)


def moved(value, kind, back):
    lons, lats = lax.axis_size(LON), lax.axis_size(LAT)
    pairs = []
    for lon in range(lons):
        for lat in range(lats):
            to_lat, to_lon = owner_of(kind, lat, lon)
            pair = (lon * lats + lat, to_lon % lons * lats + to_lat % lats)
            pairs.append(pair[::-1] if back else pair)
    return lax.ppermute(value, ALL, pairs)


def token_labels(token, window, lat_edge, lon_edge):
    quarter = token // QUARTER
    level = token % QUARTER // (QUARTER // 2)
    return level * window + 2 * lat_edge * (quarter // 2) + 4 * lon_edge * (quarter % 2)


def pack_kernel(place, act_ref, cot_ref, own, lon, lat, both, lines):
    whole = {}
    for row_half in range(2):
        for col_half in range(2):
            cuts = []
            for kind, ref in enumerate((act_ref, cot_ref)):
                held = [lines.at[4 * (4 * kind + 2 * row_half + col_half) + part] for part in range(4)]
                for row in range(HALF_LAT):
                    for col in range(HALF_LON):
                        token = ref[row_half * HALF_LAT + row, col_half * HALF_LON + col]
                        token = token.astype(jnp.float32)
                        for part in range(4):
                            at = pl.ds(LEVELS * (row * HALF_LON + col), LEVELS)
                            held[part][at] = token[:, 128 * part : 128 * part + 128]
                for pair in PAIRS:
                    for level in pair:
                        at = pl.ds(level, HALF_LAT * HALF_LON, stride=LEVELS)
                        cuts.append(jnp.concatenate([part[at] for part in held], axis=1))
            whole[row_half, col_half] = jnp.concatenate(cuts, axis=0).astype(jnp.bfloat16)

    def put(parity):
        own[...] = whole[0, parity]
        lon[...] = whole[0, 1 - parity]
        lat[...] = whole[1, 1 - parity]
        both[...] = whole[1, parity]

    for parity in range(2):
        pl.when(place[0] == parity)(lambda parity=parity: put(parity))


def pack(place, activations, cotangent):
    whole = pl.BlockSpec(memory_space=pltpu.VMEM)
    return pl.pallas_call(
        pack_kernel,
        out_shape=(jax.ShapeDtypeStruct((4 * QUARTER, D), jnp.bfloat16),) * 4,
        in_specs=[pl.BlockSpec(memory_space=pltpu.SMEM)] + [whole] * 2,
        out_specs=(whole,) * 4,
        scratch_shapes=[pltpu.VMEM((32, LEVELS * HALF_LAT * HALF_LON, 128), jnp.float32)],
        compiler_params=pltpu.CompilerParams(vmem_limit_bytes=32 * 2**20),
        cost_estimate=pl.CostEstimate(flops=0, bytes_accessed=1200000, transcendentals=0),
        name="pack",
    )(place, activations.transpose(1, 2, 0, 3), cotangent.transpose(1, 2, 0, 3))


def unpack_kernel(place, cot_ref, *refs):
    own, lon_ref, lat_both, out = refs
    own, lon = (ref[: 2 * QUARTER].astype(jnp.float32) for ref in (own, lon_ref))
    lat, both = (lat_both[part * 2 * QUARTER : (part + 1) * 2 * QUARTER].astype(jnp.float32) for part in range(2))
    even = place[0] == 0
    whole = {
        (0, 0): jnp.where(even, own, lon),
        (0, 1): jnp.where(even, lon, own),
        (1, 0): jnp.where(even, both, lat),
        (1, 1): jnp.where(even, lat, both),
    }
    at = [0, 0]
    for pair in PAIRS:
        for level in pair:
            for row in range(ROWS):
                half = row // HALF_LAT
                cuts = [whole[half, col_half][at[half] : at[half] + HALF_LON] for col_half in range(2)]
                at[half] += HALF_LON
                line = cot_ref[level, row].astype(jnp.float32) + jnp.concatenate(cuts, axis=0)
                out[level, row] = line.astype(jnp.bfloat16)


def unpack(place, cotangent, *quarters):
    whole = pl.BlockSpec(memory_space=pltpu.VMEM)
    return pl.pallas_call(
        unpack_kernel,
        out_shape=jax.ShapeDtypeStruct(cotangent.shape, jnp.bfloat16),
        in_specs=[pl.BlockSpec(memory_space=pltpu.SMEM)] + [whole] * 4,
        out_specs=whole,
        compiler_params=pltpu.CompilerParams(vmem_limit_bytes=32 * 2**20),
        cost_estimate=pl.CostEstimate(flops=0, bytes_accessed=900000, transcendentals=0),
        name="unpack",
    )(place, cotangent, *quarters)


def half_grads(half, normed, attended, qkv_grad, cot_held, tiles):
    rows = pl.ds(pl.multiple_of(half * (D // 2), D // 2), D // 2)

    def put(step, block):
        block = block.astype(jnp.bfloat16)
        for part in range(2):
            tiles[:, 2 * step + part] = block[:, 128 * part : 128 * part + 128].reshape(D // 32, 16, 128)

    @pl.loop(0, 3 * D // 256)
    def _(step):
        cols = pl.ds(pl.multiple_of(step * 256, 256), 256)
        put(step, dot(normed[:, rows], qkv_grad[:, cols], 0, 0))

    @pl.loop(0, D // 256)
    def _(step):
        cols = pl.ds(pl.multiple_of(step * 256, 256), 256)
        put(step + 3 * D // 256, dot(attended[:, rows], cot_held[:, cols], 0, 0))


def block_kernel(place, *refs):
    quarters, weights = refs[:4], refs[4:6]
    x_held, cot_held, normed, attended, qkv_grad, tiles, qkv, upstream, qkv_weight, proj_weight, arrivals = refs[6:]
    copies = [
        pltpu.make_async_copy(source, target, arrivals.at[at])
        for at, (source, target) in enumerate(zip(weights, (qkv_weight, proj_weight)))
    ]
    for copy in copies:
        copy.start()
    held = [ref[...].astype(jnp.float32) for ref in quarters]
    for kind, target in enumerate((x_held, cot_held)):
        chunks = [
            held[quarter][(2 * kind + window) * QUARTER : (2 * kind + window + 1) * QUARTER]
            for window in range(2)
            for quarter in range(4)
        ]
        target[...] = jnp.concatenate(chunks, axis=0).astype(jnp.bfloat16)
    x = x_held[...].astype(jnp.float32)
    centered = x - jnp.mean(x, axis=-1, keepdims=True)
    inverse = lax.rsqrt(jnp.mean(centered * centered, axis=-1, keepdims=True) + 1e-05)
    normed[...] = (centered * inverse).astype(jnp.bfloat16)

    for copy in copies:
        copy.wait()

    @pl.loop(0, 3 * D // 256)
    def _(step):
        cols = pl.ds(pl.multiple_of(step * 256, 256), 256)
        gain = jnp.where(step < D // 256, HEAD_DIM ** (-0.5), 1.0)
        qkv[:, cols] = (dot(normed[...], qkv_weight[:, cols], 1, 0) * gain).astype(jnp.bfloat16)

    @pl.loop(0, D // 256)
    def _(step):
        cols = pl.ds(pl.multiple_of(step * 256, 256), 256)
        upstream[:, cols] = dot(cot_held[...], proj_weight[cols, :], 1, 1).astype(jnp.bfloat16)

    head_of = lax.broadcasted_iota(jnp.int32, (WINDOW, GROUP * HEAD_DIM), 1) // HEAD_DIM
    zero = jnp.zeros((WINDOW, GROUP * HEAD_DIM), jnp.bfloat16)

    def apart(slab):
        return jnp.concatenate([jnp.where(head_of == head, slab, zero) for head in range(GROUP)], axis=0)

    def together(tall):
        merged = tall[:WINDOW]
        for head in range(1, GROUP):
            merged = jnp.where(head_of == head, tall[head * WINDOW : (head + 1) * WINDOW], merged)
        return merged.astype(jnp.bfloat16)

    for window in range(2):
        rows = slice(window * WINDOW, (window + 1) * WINDOW)
        shape = (WINDOW, GROUP * WINDOW)
        key_label = token_labels(lax.broadcasted_iota(jnp.int32, shape, 0), window, place[1], place[2])
        query_label = token_labels(lax.broadcasted_iota(jnp.int32, shape, 1) % WINDOW, window, place[1], place[2])
        bias = jnp.where(key_label == query_label, 0.0, -1000000000.0)
        for group in range(HEADS // GROUP):
            cols = [slice(part * D + group * GROUP * HEAD_DIM, part * D + (group + 1) * GROUP * HEAD_DIM) for part in range(3)]
            query, keys, values = (qkv[rows, at] for at in cols)
            query, grad = apart(query), apart(upstream[rows, cols[0]])
            scores = dot(keys, query, 1, 1) + bias
            expo = jnp.exp(scores - jnp.max(scores, axis=0, keepdims=True))
            probs = expo * (1.0 / jnp.sum(expo, axis=0, keepdims=True))
            low = probs.astype(jnp.bfloat16)
            prob_grad = dot(values, grad, 1, 1)
            inner = jnp.sum(probs * prob_grad, axis=0, keepdims=True)
            score_grad = (probs * (prob_grad - inner)).astype(jnp.bfloat16)
            attended[rows, cols[0]] = together(dot(low, values, 0, 0))
            qkv_grad[rows, cols[0]] = together(dot(score_grad, keys, 0, 0) * HEAD_DIM ** (-0.5))
            qkv_grad[rows, cols[1]] = dot(score_grad, query, 1, 0).astype(jnp.bfloat16)
            qkv_grad[rows, cols[2]] = dot(low, grad, 1, 0).astype(jnp.bfloat16)

    half_grads(1 - place[3], normed, attended, qkv_grad, cot_held, tiles)


def rest_kernel(place, x_held, cot_held, normed, attended, qkv_grad, qkv_weight, tiles, own, lat, lon_both):
    half_grads(place[3], normed, attended, qkv_grad, cot_held, tiles)
    normed_grad = dot(qkv_grad[...], qkv_weight[...], 1, 1)
    x = x_held[...].astype(jnp.float32)
    centered = x - jnp.mean(x, axis=-1, keepdims=True)
    inverse = lax.rsqrt(jnp.mean(centered * centered, axis=-1, keepdims=True) + 1e-05)
    xhat = centered * inverse
    average = jnp.mean(normed_grad, axis=-1, keepdims=True)
    product = jnp.mean(normed_grad * xhat, axis=-1, keepdims=True)
    dx = inverse * (normed_grad - average - xhat * product)
    for target, kinds in ((own, (0,)), (lat, (2,)), (lon_both, (1, 3))):
        chunks = [
            dx[(4 * window + kind) * QUARTER : (4 * window + kind + 1) * QUARTER] for kind in kinds for window in range(2)
        ]
        target[...] = jnp.concatenate(chunks, axis=0).astype(jnp.bfloat16)


HALF_TILES = jax.ShapeDtypeStruct((D // 32, 4 * D // 128, 16, 128), jnp.bfloat16)


def rows_of(count, width=D):
    return jax.ShapeDtypeStruct((count, width), jnp.bfloat16)


def block(place, quarters, qkv_weight, proj_weight):
    whole = pl.BlockSpec(memory_space=pltpu.VMEM)
    return pl.pallas_call(
        block_kernel,
        out_shape=(rows_of(TOKENS),) * 4 + (rows_of(TOKENS, 3 * D), HALF_TILES),
        in_specs=[pl.BlockSpec(memory_space=pltpu.SMEM)] + [whole] * 4 + [pl.BlockSpec(memory_space=pl.ANY)] * 2,
        out_specs=(whole,) * 6,
        scratch_shapes=[
            pltpu.VMEM((TOKENS, 3 * D), jnp.bfloat16),
            pltpu.VMEM((TOKENS, D), jnp.bfloat16),
            pltpu.VMEM((D, 3 * D), jnp.bfloat16),
            pltpu.VMEM((D, D), jnp.bfloat16),
            pltpu.SemaphoreType.DMA((2,)),
        ],
        compiler_params=pltpu.CompilerParams(vmem_limit_bytes=48 * 2**20),
        cost_estimate=pl.CostEstimate(flops=2 * 10**9, bytes_accessed=6 * 10**6, transcendentals=6 * 10**5),
        name="block",
    )(place, *quarters, qkv_weight, proj_weight)


def rest(place, kept, qkv_weight):
    whole = pl.BlockSpec(memory_space=pltpu.VMEM)
    return pl.pallas_call(
        rest_kernel,
        out_shape=(HALF_TILES, rows_of(2 * QUARTER), rows_of(2 * QUARTER), rows_of(4 * QUARTER)),
        in_specs=[pl.BlockSpec(memory_space=pltpu.SMEM)] + [whole] * 6,
        out_specs=(whole,) * 4,
        compiler_params=pltpu.CompilerParams(vmem_limit_bytes=48 * 2**20),
        cost_estimate=pl.CostEstimate(flops=10**9, bytes_accessed=5 * 10**6, transcendentals=300),
        name="rest",
    )(place, *kept, qkv_weight)


def added(arrived):
    total = arrived[0].astype(jnp.float32)
    for part in range(1, arrived.shape[0]):
        total = total + arrived[part].astype(jnp.float32)
    return total


def device_groups(members):
    tall, wide = lax.axis_size("y_hi"), lax.axis_size("x")
    cores, y_los = lax.axis_size("core"), lax.axis_size("y_lo")

    def index(z, y, x, core):
        return (((z * tall + y // y_los) * cores + core) * wide + x) * y_los + y % y_los

    return [[index(*at, core) for at in group] for core in range(cores) for group in members(core)]


def chips():
    return lax.axis_size("z"), lax.axis_size("y_hi") * lax.axis_size("y_lo"), lax.axis_size("x")


def near_groups():
    def along(size, core):
        if size == 1:
            return [[0]]
        return [[(2 * at + 2 * core) % size, 2 * at + 1] for at in range(size // 2)]

    def members(core):
        zs, ys, xs = (along(size, core) for size in chips())
        return [[(z, y, x) for z in za for y in ya for x in xa] for za in zs for ya in ys for xa in xs]

    return device_groups(members)


def strided(size):
    step = min(size, 2)
    return [list(range(parity, size, step)) for parity in range(step)]


def middle_groups():
    def members(core):
        z_size, y_size, x_size = chips()
        xs = strided(x_size)
        if core == 0:
            return [[(z, y, x) for x in xa for z in za] for xa in xs for za in strided(z_size) for y in range(y_size)]
        return [[(z, y, x) for x in xa for y in ya] for xa in xs for ya in strided(y_size) for z in range(z_size)]

    return device_groups(members)


def far_groups():
    def members(core):
        z_size, y_size, x_size = chips()
        if core == 0:
            return [[(z, y, x) for y in ya] for ya in strided(y_size) for z in range(z_size) for x in range(x_size)]
        return [[(z, y, x) for z in za] for za in strided(z_size) for y in range(y_size) for x in range(x_size)]

    return device_groups(members)


def swapped(value):
    at = [(z, y, x) for z, y, x in itertools.product(*(range(size) for size in chips()))]
    first, second = device_groups(lambda core: [at])
    return lax.ppermute(value, ALL, [*zip(first, second), *zip(second, first)])


def all_to_all(split, groups):
    return lax.all_to_all(split, ALL, 0, 0, axis_index_groups=groups)


def scattered_sum(tiles, groups):
    count = len(groups[0])
    split = tiles.reshape((count, tiles.shape[0] // count) + tiles.shape[1:])
    return added(all_to_all(split, groups)).astype(jnp.bfloat16)


def exchanged(tiles, groups):
    return all_to_all(jnp.broadcast_to(tiles[None], (len(groups[0]),) + tiles.shape), groups)


def gathered(tiles, groups):
    return exchanged(tiles, groups).reshape((-1,) + tiles.shape[1:])


def untile_kernel(place, tiles, *refs):
    qkv_out, proj_out = refs[-2:]
    for col in range(4 * D // 128):
        strip = tiles[:, col].reshape(-1, 128)
        if col < 3 * D // 128:
            qkv_out[:, 128 * col : 128 * col + 128] = strip
        else:
            proj_out[:, 128 * col - 3 * D : 128 * col - 3 * D + 128] = strip


def untile(place, tiles, other, so_far=()):
    steps = 2
    half = D // 2

    def at(step, place):
        core = 1 - place[3] if other else place[3]
        return (core * steps + step, 0)

    return pl.pallas_call(
        untile_kernel,
        grid_spec=pltpu.PrefetchScalarGridSpec(
            num_scalar_prefetch=1,
            grid=(steps,),
            in_specs=[pl.BlockSpec((half // 16 // steps, 4 * D // 128, 16, 128), lambda step, place: (step, 0, 0, 0))]
            + [pl.BlockSpec(memory_space=pl.ANY)] * len(so_far),
            out_specs=(pl.BlockSpec((half // steps, 3 * D), at), pl.BlockSpec((half // steps, D), at)),
        ),
        out_shape=(rows_of(D, 3 * D), rows_of(D)),
        input_output_aliases={2: 0, 3: 1} if so_far else {},
        compiler_params=pltpu.CompilerParams(vmem_limit_bytes=32 * 2**20),
        cost_estimate=pl.CostEstimate(flops=0, bytes_accessed=2 * 2**20, transcendentals=0),
        name="untile_other" if other else "untile_own",
    )(place, tiles, *so_far)


def per_device(activations, cotangent, qkv_weight, proj_weight):
    lat, lon = lax.axis_index(LAT), lax.axis_index(LON)
    odd = lat % 2 == 1
    lon_edge = jnp.where(odd, lon == lax.axis_size(LON) - 1, lon == 0)
    place = jnp.stack([odd, lat == 0, lon_edge, lax.axis_index("core") == 1]).astype(jnp.int32)
    quarters = pack(place, activations, cotangent)
    quarters = [quarters[0]] + [moved(quarters[kind], kind, False) for kind in range(1, 4)]
    *kept, theirs = block(place, quarters, qkv_weight, proj_weight)
    arrived = swapped(theirs)
    mine, own, lat, lon_both = rest(place, kept, qkv_weight)

    near, middle, far = near_groups(), middle_groups(), far_groups()
    tiles = (mine.astype(jnp.float32) + arrived.astype(jnp.float32)).astype(jnp.bfloat16)
    tiles, lon_both = lax.optimization_barrier((tiles.reshape(-1, 16, 128), lon_both))
    tiles, lon_both = lax.optimization_barrier((scattered_sum(tiles, near), moved(lon_both, 1, True)))
    tiles = scattered_sum(tiles, middle)
    factor = (LEVELS * ROWS * COLS * lax.axis_size(ALL)) ** (-0.5)
    tiles = (added(exchanged(tiles, far)) * factor).astype(jnp.bfloat16)
    lat_both = jnp.concatenate([lat, lon_both[2 * QUARTER :]], axis=0)
    tiles, lat_both = lax.optimization_barrier((gathered(tiles, middle), lat_both))
    tiles, lat_both = lax.optimization_barrier((gathered(tiles, near), moved(lat_both, 2, True)))
    tiles = tiles.reshape(HALF_TILES.shape)
    arrived = swapped(tiles)
    grads = untile(place, tiles, False)
    input_grad = unpack(place, cotangent, own, lon_both, lat_both)
    arrived, grads, input_grad = lax.optimization_barrier((arrived, grads, input_grad))
    qkv_weight_grad, proj_weight_grad = untile(place, arrived, True, grads)
    return (input_grad, qkv_weight_grad, proj_weight_grad)


def over(physical):
    spec = P(None, LAT, LON, None)
    return jax.shard_map(
        per_device,
        mesh=physical,
        in_specs=(spec, spec, P(), P()),
        out_specs=(spec, P(), P()),
        check_vma=False,
    )


def solution(mesh):
    return over(Mesh(mesh.devices.reshape(8, 4, 2, 4, 2), ALL))
```

```python
import functools
import itertools

import jax
import jax.numpy as jnp
from jax import lax
from jax.experimental import pallas as pl
from jax.experimental.pallas import tpu as pltpu
from jax.sharding import Mesh, PartitionSpec as P

D = 512
HEADS = 8
HEAD_DIM = 64
GROUP = 4
LEVELS = 4
HALF_LAT = 3
HALF_LON = 6
ROWS = 6
COLS = 12
PAIRS = ((1, 2), (3, 0))
QUARTER = 2 * HALF_LAT * HALF_LON
WINDOW = 4 * QUARTER
TOKENS = 2 * WINDOW

LON = ("z", "y_hi", "core")
LAT = ("x", "y_lo")
ALL = LON + LAT


def dot(a, b, a_dim, b_dim):
    return lax.dot_general(a, b, (((a_dim,), (b_dim,)), ((), ())), preferred_element_type=jnp.float32)


def owner_of(kind, lat, lon):
    lat = lat + kind // 2
    return lat, lon + kind % 2 * (-1 if lat % 2 == 1 else 1)


def moved(value, kind, back):
    lons, lats = lax.axis_size(LON), lax.axis_size(LAT)
    pairs = []
    for lon in range(lons):
        for lat in range(lats):
            to_lat, to_lon = owner_of(kind, lat, lon)
            pair = (lon * lats + lat, to_lon % lons * lats + to_lat % lats)
            pairs.append(pair[::-1] if back else pair)
    return lax.ppermute(value, ALL, pairs)


def token_labels(token, window, lat_edge, lon_edge):
    quarter = token // QUARTER
    level = token % QUARTER // (QUARTER // 2)
    return level * window + 2 * lat_edge * (quarter // 2) + 4 * lon_edge * (quarter % 2)


def fetched(sources, targets, semaphores):
    copies = [
        pltpu.make_async_copy(source, target, semaphores.at[at])
        for at, (source, target) in enumerate(zip(sources, targets))
    ]
    for copy in copies:
        copy.start()
    return copies


def pack_kernel(place, act_ref, cot_ref, own, lon, lat, both, lines):
    cuts = {(row_half, col_half): [] for row_half in range(2) for col_half in range(2)}
    for kind, ref in enumerate((act_ref, cot_ref)):
        for row_half, col_half in cuts:
            held = [lines.at[4 * (4 * kind + 2 * row_half + col_half) + part] for part in range(4)]
            for row in range(HALF_LAT):
                for col in range(HALF_LON):
                    token = ref[row_half * HALF_LAT + row, col_half * HALF_LON + col].astype(jnp.float32)
                    at = pl.ds(LEVELS * (row * HALF_LON + col), LEVELS)
                    for part in range(4):
                        held[part][at] = token[:, 128 * part : 128 * part + 128]
            for pair in PAIRS:
                for level in pair:
                    at = pl.ds(level, HALF_LAT * HALF_LON, stride=LEVELS)
                    cuts[row_half, col_half].append(jnp.concatenate([part[at] for part in held], axis=1))
    whole = {at: jnp.concatenate(pieces, axis=0).astype(jnp.bfloat16) for at, pieces in cuts.items()}

    def put(parity):
        own[...] = whole[0, parity]
        lon[...] = whole[0, 1 - parity]
        lat[...] = whole[1, 1 - parity]
        both[...] = whole[1, parity]

    for parity in range(2):
        pl.when(place[0] == parity)(lambda parity=parity: put(parity))


SMEM = pl.BlockSpec(memory_space=pltpu.SMEM)
VMEM = pl.BlockSpec(memory_space=pltpu.VMEM)
HBM = pl.BlockSpec(memory_space=pltpu.HBM)
LOCAL = (ROWS, COLS, LEVELS, D)


def pack(place, activations, cotangent):
    return pl.pallas_call(
        pack_kernel,
        out_shape=(jax.ShapeDtypeStruct((4 * QUARTER, D), jnp.bfloat16),) * 4,
        in_specs=[SMEM, VMEM, VMEM],
        out_specs=(VMEM,) * 4,
        scratch_shapes=[
            pltpu.VMEM((32, LEVELS * HALF_LAT * HALF_LON, 128), jnp.float32),
        ],
        compiler_params=pltpu.CompilerParams(vmem_limit_bytes=32 * 2**20),
        cost_estimate=pl.CostEstimate(flops=0, bytes_accessed=1200000, transcendentals=0),
        name="pack",
    )(place, activations.transpose(1, 2, 0, 3), cotangent.transpose(1, 2, 0, 3))


def unpack_kernel(place, cot_ref, *refs):
    own, lon_ref, lat_both, out = refs
    own, lon = (ref[: 2 * QUARTER].astype(jnp.float32) for ref in (own, lon_ref))
    lat, both = (lat_both[part * 2 * QUARTER : (part + 1) * 2 * QUARTER].astype(jnp.float32) for part in range(2))
    even = place[0] == 0
    whole = {
        (0, 0): jnp.where(even, own, lon),
        (0, 1): jnp.where(even, lon, own),
        (1, 0): jnp.where(even, both, lat),
        (1, 1): jnp.where(even, lat, both),
    }
    at = [0, 0]
    for pair in PAIRS:
        for level in pair:
            for row in range(ROWS):
                half = row // HALF_LAT
                cuts = [whole[half, col_half][at[half] : at[half] + HALF_LON] for col_half in range(2)]
                at[half] += HALF_LON
                line = cot_ref[level, row].astype(jnp.float32) + jnp.concatenate(cuts, axis=0)
                out[level, row] = line.astype(jnp.bfloat16)


def unpack(place, cotangent, *quarters):
    whole = pl.BlockSpec(memory_space=pltpu.VMEM)
    return pl.pallas_call(
        unpack_kernel,
        out_shape=jax.ShapeDtypeStruct(cotangent.shape, jnp.bfloat16),
        in_specs=[pl.BlockSpec(memory_space=pltpu.SMEM)] + [whole] * 4,
        out_specs=whole,
        compiler_params=pltpu.CompilerParams(vmem_limit_bytes=32 * 2**20),
        cost_estimate=pl.CostEstimate(flops=0, bytes_accessed=900000, transcendentals=0),
        name="unpack",
    )(place, cotangent, *quarters)


def weights_kernel(qkv_weight, proj_weight, qkv_held, proj_held, semaphores):
    for copy in fetched((qkv_weight, proj_weight), (qkv_held, proj_held), semaphores):
        copy.wait()


def near_weights(qkv_weight, proj_weight):
    return pl.pallas_call(
        weights_kernel,
        out_shape=(rows_of(D, 3 * D), rows_of(D)),
        in_specs=[HBM, HBM],
        out_specs=(VMEM, VMEM),
        scratch_shapes=[pltpu.SemaphoreType.DMA((2,))],
        compiler_params=pltpu.CompilerParams(vmem_limit_bytes=32 * 2**20),
        cost_estimate=pl.CostEstimate(flops=0, bytes_accessed=4 * 2**20, transcendentals=0),
        name="near_weights",
    )(qkv_weight, proj_weight)


def block_kernel(place, *refs):
    quarters, (qkv_weight, proj_weight), (theirs, mine, own, lat, lon_both) = refs[:4], refs[4:6], refs[6:11]
    x_held, cot_held, normed, attended, qkv_grad, qkv, upstream, tiles = refs[11:]
    held = [ref[...].astype(jnp.float32) for ref in quarters]
    for kind, target in enumerate((x_held, cot_held)):
        chunks = [
            held[quarter][(2 * kind + window) * QUARTER : (2 * kind + window + 1) * QUARTER]
            for window in range(2)
            for quarter in range(4)
        ]
        target[...] = jnp.concatenate(chunks, axis=0).astype(jnp.bfloat16)
    x = x_held[...].astype(jnp.float32)
    centered = x - jnp.mean(x, axis=-1, keepdims=True)
    inverse = lax.rsqrt(jnp.mean(centered * centered, axis=-1, keepdims=True) + 1e-05)
    normed[...] = (centered * inverse).astype(jnp.bfloat16)

    for step in range(3 * D // 256):
        cols = slice(step * 256, (step + 1) * 256)
        gain = HEAD_DIM ** (-0.5) if step < D // 256 else 1.0
        qkv[:, cols] = (dot(normed[...], qkv_weight[:, cols], 1, 0) * gain).astype(jnp.bfloat16)
    for step in range(D // 256):
        cols = slice(step * 256, (step + 1) * 256)
        upstream[:, cols] = dot(cot_held[...], proj_weight[cols, :], 1, 1).astype(jnp.bfloat16)

    head_of = lax.broadcasted_iota(jnp.int32, (WINDOW, GROUP * HEAD_DIM), 1) // HEAD_DIM
    zero = jnp.zeros((WINDOW, GROUP * HEAD_DIM), jnp.bfloat16)

    def apart(slab):
        return jnp.concatenate([jnp.where(head_of == head, slab, zero) for head in range(GROUP)], axis=0)

    def together(tall):
        merged = tall[:WINDOW]
        for head in range(1, GROUP):
            merged = jnp.where(head_of == head, tall[head * WINDOW : (head + 1) * WINDOW], merged)
        return merged.astype(jnp.bfloat16)

    for window in range(2):
        rows = slice(window * WINDOW, (window + 1) * WINDOW)
        shape = (WINDOW, GROUP * WINDOW)
        key_label = token_labels(lax.broadcasted_iota(jnp.int32, shape, 0), window, place[1], place[2])
        query_label = token_labels(lax.broadcasted_iota(jnp.int32, shape, 1) % WINDOW, window, place[1], place[2])
        bias = jnp.where(key_label == query_label, 0.0, -1000000000.0)
        for group in range(HEADS // GROUP):
            cols = [slice(part * D + group * GROUP * HEAD_DIM, part * D + (group + 1) * GROUP * HEAD_DIM) for part in range(3)]
            query, keys, values = (qkv[rows, at] for at in cols)
            query, grad = apart(query), apart(upstream[rows, cols[0]])
            scores = dot(keys, query, 1, 1) + bias
            expo = jnp.exp(scores - jnp.max(scores, axis=0, keepdims=True))
            probs = expo * (1.0 / jnp.sum(expo, axis=0, keepdims=True))
            low = probs.astype(jnp.bfloat16)
            prob_grad = dot(values, grad, 1, 1)
            inner = jnp.sum(probs * prob_grad, axis=0, keepdims=True)
            score_grad = (probs * (prob_grad - inner)).astype(jnp.bfloat16)
            attended[rows, cols[0]] = together(dot(low, values, 0, 0))
            qkv_grad[rows, cols[0]] = together(dot(score_grad, keys, 0, 0) * HEAD_DIM ** (-0.5))
            qkv_grad[rows, cols[1]] = dot(score_grad, query, 1, 0).astype(jnp.bfloat16)
            qkv_grad[rows, cols[2]] = dot(low, grad, 1, 0).astype(jnp.bfloat16)

    def put(step, grads):
        grads = grads.astype(jnp.bfloat16)
        for half in range(2):
            rows = grads[half * (D // 2) : (half + 1) * (D // 2)]
            for part in range(2):
                tiles[half, :, 2 * step + part] = rows[:, 128 * part : 128 * part + 128].reshape(D // 32, 16, 128)

    tall = normed[...].T
    for step in range(3 * D // 256):
        put(step, dot(tall, qkv_grad[:, step * 256 : (step + 1) * 256], 1, 0))
    tall = attended[...].T
    for step in range(D // 256):
        put(step + 3 * D // 256, dot(tall, cot_held[:, step * 256 : (step + 1) * 256], 1, 0))
    theirs[...] = tiles[1 - place[3]]
    mine[...] = tiles[place[3]]
    normed_grad = dot(qkv_grad[...], qkv_weight[...], 1, 1)
    x = x_held[...].astype(jnp.float32)
    centered = x - jnp.mean(x, axis=-1, keepdims=True)
    inverse = lax.rsqrt(jnp.mean(centered * centered, axis=-1, keepdims=True) + 1e-05)
    xhat = centered * inverse
    average = jnp.mean(normed_grad, axis=-1, keepdims=True)
    product = jnp.mean(normed_grad * xhat, axis=-1, keepdims=True)
    dx = inverse * (normed_grad - average - xhat * product)
    for target, kinds in ((own, (0,)), (lat, (2,)), (lon_both, (1, 3))):
        chunks = [
            dx[(4 * window + kind) * QUARTER : (4 * window + kind + 1) * QUARTER] for kind in kinds for window in range(2)
        ]
        target[...] = jnp.concatenate(chunks, axis=0).astype(jnp.bfloat16)


HALF_TILES = jax.ShapeDtypeStruct((D // 32, 4 * D // 128, 16, 128), jnp.bfloat16)


def rows_of(count, width=D):
    return jax.ShapeDtypeStruct((count, width), jnp.bfloat16)


def block(place, quarters, qkv_weight, proj_weight):
    return pl.pallas_call(
        block_kernel,
        out_shape=(HALF_TILES, HALF_TILES, rows_of(2 * QUARTER), rows_of(2 * QUARTER), rows_of(4 * QUARTER)),
        in_specs=[SMEM] + [VMEM] * 6,
        out_specs=(VMEM,) * 5,
        scratch_shapes=[
            pltpu.VMEM((TOKENS, D), jnp.bfloat16),
            pltpu.VMEM((TOKENS, D), jnp.bfloat16),
            pltpu.VMEM((TOKENS, D), jnp.bfloat16),
            pltpu.VMEM((TOKENS, D), jnp.bfloat16),
            pltpu.VMEM((TOKENS, 3 * D), jnp.bfloat16),
            pltpu.VMEM((TOKENS, 3 * D), jnp.bfloat16),
            pltpu.VMEM((TOKENS, D), jnp.bfloat16),
            pltpu.VMEM((2,) + HALF_TILES.shape, jnp.bfloat16),
        ],
        compiler_params=pltpu.CompilerParams(vmem_limit_bytes=48 * 2**20),
        cost_estimate=pl.CostEstimate(flops=2 * 10**9, bytes_accessed=6 * 10**6, transcendentals=6 * 10**5),
        name="block",
    )(place, *quarters, qkv_weight, proj_weight)


def added(arrived):
    total = arrived[0].astype(jnp.float32)
    for part in range(1, arrived.shape[0]):
        total = total + arrived[part].astype(jnp.float32)
    return total


def device_groups(members):
    tall, wide = lax.axis_size("y_hi"), lax.axis_size("x")
    cores, y_los = lax.axis_size("core"), lax.axis_size("y_lo")

    def index(z, y, x, core):
        return (((z * tall + y // y_los) * cores + core) * wide + x) * y_los + y % y_los

    return [[index(*at, core) for at in group] for core in range(cores) for group in members(core)]


def chips():
    return lax.axis_size("z"), lax.axis_size("y_hi") * lax.axis_size("y_lo"), lax.axis_size("x")


def cube_groups(stride):
    def along(size):
        firsts = [at for at in range(size) if at // stride % 2 == 0]
        return [[at, at + stride] if at + stride < size else [at] for at in firsts]

    def members(core):
        return [list(itertools.product(*lines)) for lines in itertools.product(*(along(size) for size in chips()))]

    return device_groups(members)


def swapped(value):
    at = [(z, y, x) for z, y, x in itertools.product(*(range(size) for size in chips()))]
    first, second = device_groups(lambda core: [at])
    return lax.ppermute(value, ALL, [*zip(first, second), *zip(second, first)])


def all_to_all(split, groups):
    return lax.all_to_all(split, ALL, 0, 0, axis_index_groups=groups)


def scattered_sum(tiles, groups):
    count = len(groups[0])
    split = tiles.reshape((count, tiles.shape[0] // count) + tiles.shape[1:])
    return added(all_to_all(split, groups)).astype(jnp.bfloat16)


def exchanged(tiles, groups):
    return all_to_all(jnp.broadcast_to(tiles[None], (len(groups[0]),) + tiles.shape), groups)


def gathered(tiles, groups):
    return exchanged(tiles, groups).reshape((-1,) + tiles.shape[1:])


def untile_kernel(other, place, tiles, *refs):
    qkv_out, proj_out, qkv_held, proj_held, semaphores = refs[-5:]
    first = (1 - place[3] if other else place[3]) * (D // 2)
    chunk = D // 2 // CHUNKS
    copies = []
    for at in range(CHUNKS):
        rows = slice(at * chunk, (at + 1) * chunk)
        for col in range(4 * D // 128):
            strip = tiles[at * chunk // 16 : (at + 1) * chunk // 16, col].reshape(chunk, 128)
            if col < 3 * D // 128:
                qkv_held[rows, 128 * col : 128 * col + 128] = strip
            else:
                proj_held[rows, 128 * col - 3 * D : 128 * col - 3 * D + 128] = strip
        target = pl.ds(pl.multiple_of(first + at * chunk, chunk), chunk)
        for kind, (held, out) in enumerate(((qkv_held, qkv_out), (proj_held, proj_out))):
            copies.append(pltpu.make_async_copy(held.at[rows], out.at[target], semaphores.at[2 * at + kind]))
            copies[-1].start()
    for copy in copies:
        copy.wait()


CHUNKS = 4


def untile(place, tiles, other, so_far=()):
    return pl.pallas_call(
        functools.partial(untile_kernel, other),
        in_specs=[SMEM, VMEM] + [HBM] * len(so_far),
        out_specs=(HBM, HBM),
        out_shape=(rows_of(D, 3 * D), rows_of(D)),
        scratch_shapes=[
            pltpu.VMEM((D // 2, 3 * D), jnp.bfloat16),
            pltpu.VMEM((D // 2, D), jnp.bfloat16),
            pltpu.SemaphoreType.DMA((2 * CHUNKS,)),
        ],
        input_output_aliases={2: 0, 3: 1} if so_far else {},
        compiler_params=pltpu.CompilerParams(vmem_limit_bytes=32 * 2**20),
        cost_estimate=pl.CostEstimate(flops=0, bytes_accessed=2 * 2**20, transcendentals=0),
        name="untile_other" if other else "untile_own",
    )(place, tiles, *so_far)


def per_device(activations, cotangent, qkv_weight, proj_weight):
    lat, lon = lax.axis_index(LAT), lax.axis_index(LON)
    odd = lat % 2 == 1
    lon_edge = jnp.where(odd, lon == lax.axis_size(LON) - 1, lon == 0)
    place = jnp.stack([odd, lat == 0, lon_edge, lax.axis_index("core") == 1]).astype(jnp.int32)
    own, lon, lat, both = pack(place, activations, cotangent)
    own, qkv_weight, proj_weight = lax.optimization_barrier((own, qkv_weight, proj_weight))
    lat, lon, both = moved(lat, 2, False), moved(lon, 1, False), moved(both, 3, False)
    qkv_weight, proj_weight = near_weights(qkv_weight, proj_weight)
    theirs, mine, own, lat, lon_both = block(place, (own, lon, lat, both), qkv_weight, proj_weight)

    near, middle, far = cube_groups(1), cube_groups(2), cube_groups(4)
    tiles = (mine.astype(jnp.float32) + swapped(theirs).astype(jnp.float32)).astype(jnp.bfloat16)
    tiles, lon_both = lax.optimization_barrier((tiles.reshape(-1, 16, 128), lon_both))
    tiles, lon_both = lax.optimization_barrier((scattered_sum(tiles, near), moved(lon_both, 1, True)))
    tiles = scattered_sum(tiles, middle)
    factor = (LEVELS * ROWS * COLS * lax.axis_size(ALL)) ** (-0.5)
    tiles = (added(exchanged(tiles, far)) * factor).astype(jnp.bfloat16)
    lat_both = jnp.concatenate([lat, lon_both[2 * QUARTER :]], axis=0)
    tiles, lat_both = lax.optimization_barrier((gathered(tiles, middle), lat_both))
    tiles, lat_both = lax.optimization_barrier((gathered(tiles, near), moved(lat_both, 2, True)))
    tiles = tiles.reshape(HALF_TILES.shape)
    arrived = swapped(tiles)
    grads = untile(place, tiles, False)
    input_grad = unpack(place, cotangent, own, lon_both, lat_both)
    arrived, grads, input_grad = lax.optimization_barrier((arrived, grads, input_grad))
    qkv_weight_grad, proj_weight_grad = untile(place, arrived, True, grads)
    return (input_grad, qkv_weight_grad, proj_weight_grad)


def over(physical):
    spec = P(None, LAT, LON, None)
    return jax.shard_map(
        per_device,
        mesh=physical,
        in_specs=(spec, spec, P(), P()),
        out_specs=(spec, P(), P()),
        check_vma=False,
    )


def solution(mesh):
    return over(Mesh(mesh.devices.reshape(8, 4, 2, 4, 2), ALL))
```

```python
import functools
import itertools

import jax
import jax.numpy as jnp
from jax import lax
from jax.experimental import pallas as pl
from jax.experimental.pallas import tpu as pltpu
from jax.sharding import Mesh, PartitionSpec as P

D = 512
HEADS = 8
HEAD_DIM = 64
GROUP = 4
LEVELS = 4
HALF_LAT = 3
HALF_LON = 6
ROWS = 6
COLS = 12
PAIRS = ((1, 2), (3, 0))
QUARTER = 2 * HALF_LAT * HALF_LON
WINDOW = 4 * QUARTER
TOKENS = 2 * WINDOW

LON = ("z", "y_hi", "core")
LAT = ("x", "y_lo")
ALL = LON + LAT


def dot(a, b, a_dim, b_dim):
    return lax.dot_general(a, b, (((a_dim,), (b_dim,)), ((), ())), preferred_element_type=jnp.float32)


def owner_of(kind, lat, lon):
    lat = lat + kind // 2
    return lat, lon + kind % 2 * (-1 if lat % 2 == 1 else 1)


def moved(value, kind, back):
    lons, lats = lax.axis_size(LON), lax.axis_size(LAT)
    pairs = []
    for lon in range(lons):
        for lat in range(lats):
            to_lat, to_lon = owner_of(kind, lat, lon)
            pair = (lon * lats + lat, to_lon % lons * lats + to_lat % lats)
            pairs.append(pair[::-1] if back else pair)
    return lax.ppermute(value, ALL, pairs)


def token_labels(token, window, lat_edge, lon_edge):
    quarter = token // QUARTER
    level = token % QUARTER // (QUARTER // 2)
    return level * window + 2 * lat_edge * (quarter // 2) + 4 * lon_edge * (quarter % 2)


def fetched(sources, targets, semaphores):
    copies = [
        pltpu.make_async_copy(source, target, semaphores.at[at])
        for at, (source, target) in enumerate(zip(sources, targets))
    ]
    for copy in copies:
        copy.start()
    return copies


def pack_kernel(place, act_ref, cot_ref, own, lon, lat, both, lines):
    cuts = {(row_half, col_half): [] for row_half in range(2) for col_half in range(2)}
    for kind, ref in enumerate((act_ref, cot_ref)):
        for row_half, col_half in cuts:
            held = [lines.at[4 * (4 * kind + 2 * row_half + col_half) + part] for part in range(4)]
            for row in range(HALF_LAT):
                for col in range(HALF_LON):
                    token = ref[row_half * HALF_LAT + row, col_half * HALF_LON + col].astype(jnp.float32)
                    at = pl.ds(LEVELS * (row * HALF_LON + col), LEVELS)
                    for part in range(4):
                        held[part][at] = token[:, 128 * part : 128 * part + 128]
            for pair in PAIRS:
                for level in pair:
                    at = pl.ds(level, HALF_LAT * HALF_LON, stride=LEVELS)
                    cuts[row_half, col_half].append(jnp.concatenate([part[at] for part in held], axis=1))
    whole = {at: jnp.concatenate(pieces, axis=0).astype(jnp.bfloat16) for at, pieces in cuts.items()}

    def put(parity):
        own[...] = whole[0, parity]
        lon[...] = whole[0, 1 - parity]
        lat[...] = whole[1, 1 - parity]
        both[...] = whole[1, parity]

    for parity in range(2):
        pl.when(place[0] == parity)(lambda parity=parity: put(parity))


SMEM = pl.BlockSpec(memory_space=pltpu.SMEM)
VMEM = pl.BlockSpec(memory_space=pltpu.VMEM)
HBM = pl.BlockSpec(memory_space=pltpu.HBM)
LOCAL = (ROWS, COLS, LEVELS, D)


def pack(place, activations, cotangent):
    return pl.pallas_call(
        pack_kernel,
        out_shape=(jax.ShapeDtypeStruct((4 * QUARTER, D), jnp.bfloat16),) * 4,
        in_specs=[SMEM, VMEM, VMEM],
        out_specs=(VMEM,) * 4,
        scratch_shapes=[
            pltpu.VMEM((32, LEVELS * HALF_LAT * HALF_LON, 128), jnp.float32),
        ],
        compiler_params=pltpu.CompilerParams(vmem_limit_bytes=32 * 2**20),
        cost_estimate=pl.CostEstimate(flops=0, bytes_accessed=1200000, transcendentals=0),
        name="pack",
    )(place, activations.transpose(1, 2, 0, 3), cotangent.transpose(1, 2, 0, 3))


def unpack_kernel(place, own, lon_ref, lat_both, cot, out, cot_ref, lines, semaphores):
    (copy,) = fetched((cot,), (cot_ref,), semaphores)
    own, lon = (ref[: 2 * QUARTER].astype(jnp.float32) for ref in (own, lon_ref))
    lat, both = (lat_both[part * 2 * QUARTER : (part + 1) * 2 * QUARTER].astype(jnp.float32) for part in range(2))
    even = place[0] == 0
    whole = {
        (0, 0): jnp.where(even, own, lon),
        (0, 1): jnp.where(even, lon, own),
        (1, 0): jnp.where(even, both, lat),
        (1, 1): jnp.where(even, lat, both),
    }
    copy.wait()
    count = HALF_LAT * HALF_LON
    for (row_half, col_half), quarter in whole.items():
        held = [lines.at[4 * (2 * row_half + col_half) + part] for part in range(4)]
        for at, level in enumerate(PAIRS[0] + PAIRS[1]):
            for part in range(4):
                cut = quarter[at * count : (at + 1) * count, 128 * part : 128 * part + 128]
                held[part][pl.ds(level, count, stride=LEVELS)] = cut
        for row in range(HALF_LAT):
            for col in range(HALF_LON):
                at = pl.ds(LEVELS * (row * HALF_LON + col), LEVELS)
                token = jnp.concatenate([part[at] for part in held], axis=1)
                place_of = (row_half * HALF_LAT + row, col_half * HALF_LON + col)
                out[place_of] = (cot_ref[place_of].astype(jnp.float32) + token).astype(jnp.bfloat16)


def unpack(place, cotangent, *quarters):
    local = pl.pallas_call(
        unpack_kernel,
        out_shape=jax.ShapeDtypeStruct(LOCAL, jnp.bfloat16),
        in_specs=[SMEM] + [VMEM] * 3 + [HBM],
        out_specs=VMEM,
        scratch_shapes=[
            pltpu.VMEM(LOCAL, jnp.bfloat16),
            pltpu.VMEM((16, LEVELS * HALF_LAT * HALF_LON, 128), jnp.float32),
            pltpu.SemaphoreType.DMA((1,)),
        ],
        compiler_params=pltpu.CompilerParams(vmem_limit_bytes=32 * 2**20),
        cost_estimate=pl.CostEstimate(flops=0, bytes_accessed=900000, transcendentals=0),
        name="unpack",
    )(place, *quarters, cotangent.transpose(1, 2, 0, 3))
    return local.transpose(2, 0, 1, 3)


def weights_kernel(qkv_weight, proj_weight, qkv_held, proj_held, semaphores):
    for copy in fetched((qkv_weight, proj_weight), (qkv_held, proj_held), semaphores):
        copy.wait()


def near_weights(qkv_weight, proj_weight):
    return pl.pallas_call(
        weights_kernel,
        out_shape=(rows_of(D, 3 * D), rows_of(D)),
        in_specs=[HBM, HBM],
        out_specs=(VMEM, VMEM),
        scratch_shapes=[pltpu.SemaphoreType.DMA((2,))],
        compiler_params=pltpu.CompilerParams(vmem_limit_bytes=32 * 2**20),
        cost_estimate=pl.CostEstimate(flops=0, bytes_accessed=4 * 2**20, transcendentals=0),
        name="near_weights",
    )(qkv_weight, proj_weight)


def block_kernel(place, *refs):
    quarters, (qkv_weight, proj_weight), (theirs, mine, own, lat, lon_both) = refs[:4], refs[4:6], refs[6:11]
    x_held, cot_held, normed, attended, qkv_grad, qkv, upstream, tiles = refs[11:]
    held = [ref[...].astype(jnp.float32) for ref in quarters]
    for kind, target in enumerate((x_held, cot_held)):
        chunks = [
            held[quarter][(2 * kind + window) * QUARTER : (2 * kind + window + 1) * QUARTER]
            for window in range(2)
            for quarter in range(4)
        ]
        target[...] = jnp.concatenate(chunks, axis=0).astype(jnp.bfloat16)
    x = x_held[...].astype(jnp.float32)
    centered = x - jnp.mean(x, axis=-1, keepdims=True)
    inverse = lax.rsqrt(jnp.mean(centered * centered, axis=-1, keepdims=True) + 1e-05)
    normed[...] = (centered * inverse).astype(jnp.bfloat16)

    for step in range(3 * D // 256):
        cols = slice(step * 256, (step + 1) * 256)
        gain = HEAD_DIM ** (-0.5) if step < D // 256 else 1.0
        qkv[:, cols] = (dot(normed[...], qkv_weight[:, cols], 1, 0) * gain).astype(jnp.bfloat16)
    for step in range(D // 256):
        cols = slice(step * 256, (step + 1) * 256)
        upstream[:, cols] = dot(cot_held[...], proj_weight[cols, :], 1, 1).astype(jnp.bfloat16)

    head_of = lax.broadcasted_iota(jnp.int32, (WINDOW, GROUP * HEAD_DIM), 1) // HEAD_DIM
    zero = jnp.zeros((WINDOW, GROUP * HEAD_DIM), jnp.bfloat16)

    def apart(slab):
        return jnp.concatenate([jnp.where(head_of == head, slab, zero) for head in range(GROUP)], axis=0)

    def together(tall):
        merged = tall[:WINDOW]
        for head in range(1, GROUP):
            merged = jnp.where(head_of == head, tall[head * WINDOW : (head + 1) * WINDOW], merged)
        return merged.astype(jnp.bfloat16)

    for window in range(2):
        rows = slice(window * WINDOW, (window + 1) * WINDOW)
        shape = (WINDOW, GROUP * WINDOW)
        key_label = token_labels(lax.broadcasted_iota(jnp.int32, shape, 0), window, place[1], place[2])
        query_label = token_labels(lax.broadcasted_iota(jnp.int32, shape, 1) % WINDOW, window, place[1], place[2])
        bias = jnp.where(key_label == query_label, 0.0, -1000000000.0)
        for group in range(HEADS // GROUP):
            cols = [slice(part * D + group * GROUP * HEAD_DIM, part * D + (group + 1) * GROUP * HEAD_DIM) for part in range(3)]
            query, keys, values = (qkv[rows, at] for at in cols)
            query, grad = apart(query), apart(upstream[rows, cols[0]])
            scores = dot(keys, query, 1, 1) + bias
            expo = jnp.exp(scores - jnp.max(scores, axis=0, keepdims=True))
            probs = expo * (1.0 / jnp.sum(expo, axis=0, keepdims=True))
            low = probs.astype(jnp.bfloat16)
            prob_grad = dot(values, grad, 1, 1)
            inner = jnp.sum(probs * prob_grad, axis=0, keepdims=True)
            score_grad = (probs * (prob_grad - inner)).astype(jnp.bfloat16)
            attended[rows, cols[0]] = together(dot(low, values, 0, 0))
            qkv_grad[rows, cols[0]] = together(dot(score_grad, keys, 0, 0) * HEAD_DIM ** (-0.5))
            qkv_grad[rows, cols[1]] = dot(score_grad, query, 1, 0).astype(jnp.bfloat16)
            qkv_grad[rows, cols[2]] = dot(low, grad, 1, 0).astype(jnp.bfloat16)

    def put(step, grads):
        grads = grads.astype(jnp.bfloat16)
        for half in range(2):
            rows = grads[half * (D // 2) : (half + 1) * (D // 2)]
            for part in range(2):
                tiles[half, :, 2 * step + part] = rows[:, 128 * part : 128 * part + 128].reshape(D // 32, 16, 128)

    tall = normed[...].T
    for step in range(3 * D // 256):
        put(step, dot(tall, qkv_grad[:, step * 256 : (step + 1) * 256], 1, 0))
    tall = attended[...].T
    for step in range(D // 256):
        put(step + 3 * D // 256, dot(tall, cot_held[:, step * 256 : (step + 1) * 256], 1, 0))
    theirs[...] = tiles[1 - place[3]]
    mine[...] = tiles[place[3]]
    normed_grad = dot(qkv_grad[...], qkv_weight[...], 1, 1)
    x = x_held[...].astype(jnp.float32)
    centered = x - jnp.mean(x, axis=-1, keepdims=True)
    inverse = lax.rsqrt(jnp.mean(centered * centered, axis=-1, keepdims=True) + 1e-05)
    xhat = centered * inverse
    average = jnp.mean(normed_grad, axis=-1, keepdims=True)
    product = jnp.mean(normed_grad * xhat, axis=-1, keepdims=True)
    dx = inverse * (normed_grad - average - xhat * product)
    for target, kinds in ((own, (0,)), (lat, (2,)), (lon_both, (1, 3))):
        chunks = [
            dx[(4 * window + kind) * QUARTER : (4 * window + kind + 1) * QUARTER] for kind in kinds for window in range(2)
        ]
        target[...] = jnp.concatenate(chunks, axis=0).astype(jnp.bfloat16)


HALF_TILES = jax.ShapeDtypeStruct((D // 32, 4 * D // 128, 16, 128), jnp.bfloat16)


def rows_of(count, width=D):
    return jax.ShapeDtypeStruct((count, width), jnp.bfloat16)


def block(place, quarters, qkv_weight, proj_weight):
    return pl.pallas_call(
        block_kernel,
        out_shape=(HALF_TILES, HALF_TILES, rows_of(2 * QUARTER), rows_of(2 * QUARTER), rows_of(4 * QUARTER)),
        in_specs=[SMEM] + [VMEM] * 6,
        out_specs=(VMEM,) * 5,
        scratch_shapes=[
            pltpu.VMEM((TOKENS, D), jnp.bfloat16),
            pltpu.VMEM((TOKENS, D), jnp.bfloat16),
            pltpu.VMEM((TOKENS, D), jnp.bfloat16),
            pltpu.VMEM((TOKENS, D), jnp.bfloat16),
            pltpu.VMEM((TOKENS, 3 * D), jnp.bfloat16),
            pltpu.VMEM((TOKENS, 3 * D), jnp.bfloat16),
            pltpu.VMEM((TOKENS, D), jnp.bfloat16),
            pltpu.VMEM((2,) + HALF_TILES.shape, jnp.bfloat16),
        ],
        compiler_params=pltpu.CompilerParams(vmem_limit_bytes=48 * 2**20),
        cost_estimate=pl.CostEstimate(flops=2 * 10**9, bytes_accessed=6 * 10**6, transcendentals=6 * 10**5),
        name="block",
    )(place, *quarters, qkv_weight, proj_weight)


def added(arrived):
    total = arrived[0].astype(jnp.float32)
    for part in range(1, arrived.shape[0]):
        total = total + arrived[part].astype(jnp.float32)
    return total


def device_groups(members):
    tall, wide = lax.axis_size("y_hi"), lax.axis_size("x")
    cores, y_los = lax.axis_size("core"), lax.axis_size("y_lo")

    def index(z, y, x, core):
        return (((z * tall + y // y_los) * cores + core) * wide + x) * y_los + y % y_los

    return [[index(*at, core) for at in group] for core in range(cores) for group in members(core)]


def chips():
    return lax.axis_size("z"), lax.axis_size("y_hi") * lax.axis_size("y_lo"), lax.axis_size("x")


def cube_groups(stride):
    def along(size):
        firsts = [at for at in range(size) if at // stride % 2 == 0]
        return [[at, at + stride] if at + stride < size else [at] for at in firsts]

    def members(core):
        return [list(itertools.product(*lines)) for lines in itertools.product(*(along(size) for size in chips()))]

    return device_groups(members)


def strided(size):
    step = min(size, 2)
    return [list(range(parity, size, step)) for parity in range(step)]


def middle_groups():
    def members(core):
        z_size, y_size, x_size = chips()
        xs = strided(x_size)
        if core == 0:
            return [[(z, y, x) for x in xa for z in za] for xa in xs for za in strided(z_size) for y in range(y_size)]
        return [[(z, y, x) for x in xa for y in ya] for xa in xs for ya in strided(y_size) for z in range(z_size)]

    return device_groups(members)


def far_groups():
    def members(core):
        z_size, y_size, x_size = chips()
        if core == 0:
            return [[(z, y, x) for y in ya] for ya in strided(y_size) for z in range(z_size) for x in range(x_size)]
        return [[(z, y, x) for z in za] for za in strided(z_size) for y in range(y_size) for x in range(x_size)]

    return device_groups(members)


def swapped(value):
    at = [(z, y, x) for z, y, x in itertools.product(*(range(size) for size in chips()))]
    first, second = device_groups(lambda core: [at])
    return lax.ppermute(value, ALL, [*zip(first, second), *zip(second, first)])


def all_to_all(split, groups):
    return lax.all_to_all(split, ALL, 0, 0, axis_index_groups=groups)


def scattered_sum(tiles, groups):
    count = len(groups[0])
    split = tiles.reshape((count, tiles.shape[0] // count) + tiles.shape[1:])
    return added(all_to_all(split, groups)).astype(jnp.bfloat16)


def exchanged(tiles, groups):
    return all_to_all(jnp.broadcast_to(tiles[None], (len(groups[0]),) + tiles.shape), groups)


def gathered(tiles, groups):
    return exchanged(tiles, groups).reshape((-1,) + tiles.shape[1:])


def untile_kernel(other, place, tiles, *refs):
    qkv_out, proj_out, qkv_held, proj_held, semaphores = refs[-5:]
    first = (1 - place[3] if other else place[3]) * (D // 2)
    chunk = D // 2 // CHUNKS
    copies = []
    for at in range(CHUNKS):
        rows = slice(at * chunk, (at + 1) * chunk)
        for col in range(4 * D // 128):
            strip = tiles[at * chunk // 16 : (at + 1) * chunk // 16, col].reshape(chunk, 128)
            if col < 3 * D // 128:
                qkv_held[rows, 128 * col : 128 * col + 128] = strip
            else:
                proj_held[rows, 128 * col - 3 * D : 128 * col - 3 * D + 128] = strip
        target = pl.ds(pl.multiple_of(first + at * chunk, chunk), chunk)
        for kind, (held, out) in enumerate(((qkv_held, qkv_out), (proj_held, proj_out))):
            copies.append(pltpu.make_async_copy(held.at[rows], out.at[target], semaphores.at[2 * at + kind]))
            copies[-1].start()
    for copy in copies:
        copy.wait()


CHUNKS = 4


def untile(place, tiles, other, so_far=()):
    return pl.pallas_call(
        functools.partial(untile_kernel, other),
        in_specs=[SMEM, VMEM] + [HBM] * len(so_far),
        out_specs=(HBM, HBM),
        out_shape=(rows_of(D, 3 * D), rows_of(D)),
        scratch_shapes=[
            pltpu.VMEM((D // 2, 3 * D), jnp.bfloat16),
            pltpu.VMEM((D // 2, D), jnp.bfloat16),
            pltpu.SemaphoreType.DMA((2 * CHUNKS,)),
        ],
        input_output_aliases={2: 0, 3: 1} if so_far else {},
        compiler_params=pltpu.CompilerParams(vmem_limit_bytes=32 * 2**20),
        cost_estimate=pl.CostEstimate(flops=0, bytes_accessed=2 * 2**20, transcendentals=0),
        name="untile_other" if other else "untile_own",
    )(place, tiles, *so_far)


def per_device(activations, cotangent, qkv_weight, proj_weight):
    lat, lon = lax.axis_index(LAT), lax.axis_index(LON)
    odd = lat % 2 == 1
    lon_edge = jnp.where(odd, lon == lax.axis_size(LON) - 1, lon == 0)
    place = jnp.stack([odd, lat == 0, lon_edge, lax.axis_index("core") == 1]).astype(jnp.int32)
    own, lon, lat, both = pack(place, activations, cotangent)
    own, qkv_weight, proj_weight = lax.optimization_barrier((own, qkv_weight, proj_weight))
    both, lon, lat = moved(both, 3, False), moved(lon, 1, False), moved(lat, 2, False)
    qkv_weight, proj_weight = near_weights(qkv_weight, proj_weight)
    theirs, mine, own, lat, lon_both = block(place, (own, lon, lat, both), qkv_weight, proj_weight)

    near, middle, far = cube_groups(1), middle_groups(), far_groups()
    tiles = (mine.astype(jnp.float32) + swapped(theirs).astype(jnp.float32)).astype(jnp.bfloat16)
    tiles = scattered_sum(tiles.reshape(-1, 16, 128), near)
    tiles, lon_both = lax.optimization_barrier((tiles, lon_both))
    tiles = scattered_sum(tiles, middle)
    factor = (LEVELS * ROWS * COLS * lax.axis_size(ALL)) ** (-0.5)
    tiles, lon_both = lax.optimization_barrier((exchanged(tiles, far), moved(lon_both, 1, True)))
    tiles = (added(tiles) * factor).astype(jnp.bfloat16)
    lat_both = jnp.concatenate([lat, lon_both[2 * QUARTER :]], axis=0)
    tiles, lat_both = lax.optimization_barrier((tiles, lat_both))
    tiles, lat_both = lax.optimization_barrier((gathered(tiles, middle), moved(lat_both, 2, True)))
    input_grad = unpack(place, cotangent, own, lon_both, lat_both)
    tiles, input_grad = lax.optimization_barrier((gathered(tiles, near), input_grad))
    tiles = tiles.reshape(HALF_TILES.shape)
    arrived = swapped(tiles)
    grads = untile(place, tiles, False)
    arrived, grads = lax.optimization_barrier((arrived, grads))
    qkv_weight_grad, proj_weight_grad = untile(place, arrived, True, grads)
    return (input_grad, qkv_weight_grad, proj_weight_grad)


def over(physical):
    spec = P(None, LAT, LON, None)
    return jax.shard_map(
        per_device,
        mesh=physical,
        in_specs=(spec, spec, P(), P()),
        out_specs=(spec, P(), P()),
        check_vma=False,
    )


def solution(mesh):
    return over(Mesh(mesh.devices.reshape(8, 4, 2, 4, 2), ALL))
```

```python
import functools
import itertools

import jax
import jax.numpy as jnp
from jax import lax
from jax.experimental import pallas as pl
from jax.experimental.pallas import tpu as pltpu
from jax.sharding import Mesh, PartitionSpec as P

D = 512
HEADS = 8
HEAD_DIM = 64
GROUP = 4
LEVELS = 4
HALF_LAT = 3
HALF_LON = 6
ROWS = 6
COLS = 12
PAIRS = ((1, 2), (3, 0))
QUARTER = 2 * HALF_LAT * HALF_LON
WINDOW = 4 * QUARTER
TOKENS = 2 * WINDOW

LON = ("z", "y_hi", "core")
LAT = ("x", "y_lo")
ALL = LON + LAT


def dot(a, b, a_dim, b_dim):
    return lax.dot_general(a, b, (((a_dim,), (b_dim,)), ((), ())), preferred_element_type=jnp.float32)


def owner_of(kind, lat, lon):
    lat = lat + kind // 2
    return lat, lon + kind % 2 * (-1 if lat % 2 == 1 else 1)


def moved(value, kind, back):
    lons, lats = lax.axis_size(LON), lax.axis_size(LAT)
    pairs = []
    for lon in range(lons):
        for lat in range(lats):
            to_lat, to_lon = owner_of(kind, lat, lon)
            pair = (lon * lats + lat, to_lon % lons * lats + to_lat % lats)
            pairs.append(pair[::-1] if back else pair)
    return lax.ppermute(value, ALL, pairs)


def token_labels(token, window, lat_edge, lon_edge):
    quarter = token // QUARTER
    level = token % QUARTER // (QUARTER // 2)
    return level * window + 2 * lat_edge * (quarter // 2) + 4 * lon_edge * (quarter % 2)


def fetched(sources, targets, semaphores):
    copies = [
        pltpu.make_async_copy(source, target, semaphores.at[at])
        for at, (source, target) in enumerate(zip(sources, targets))
    ]
    for copy in copies:
        copy.start()
    return copies


def pack_kernel(place, act_ref, cot_ref, own, lon, lat, both, lines):
    cuts = {(row_half, col_half): [] for row_half in range(2) for col_half in range(2)}
    for kind, ref in enumerate((act_ref, cot_ref)):
        for row_half, col_half in cuts:
            held = [lines.at[4 * (4 * kind + 2 * row_half + col_half) + part] for part in range(4)]
            for row in range(HALF_LAT):
                for col in range(HALF_LON):
                    token = ref[row_half * HALF_LAT + row, col_half * HALF_LON + col].astype(jnp.float32)
                    at = pl.ds(LEVELS * (row * HALF_LON + col), LEVELS)
                    for part in range(4):
                        held[part][at] = token[:, 128 * part : 128 * part + 128]
            for pair in PAIRS:
                for level in pair:
                    at = pl.ds(level, HALF_LAT * HALF_LON, stride=LEVELS)
                    cuts[row_half, col_half].append(jnp.concatenate([part[at] for part in held], axis=1))
    whole = {at: jnp.concatenate(pieces, axis=0).astype(jnp.bfloat16) for at, pieces in cuts.items()}

    def put(parity):
        own[...] = whole[0, parity]
        lon[...] = whole[0, 1 - parity]
        lat[...] = whole[1, 1 - parity]
        both[...] = whole[1, parity]

    for parity in range(2):
        pl.when(place[0] == parity)(lambda parity=parity: put(parity))


SMEM = pl.BlockSpec(memory_space=pltpu.SMEM)
VMEM = pl.BlockSpec(memory_space=pltpu.VMEM)
HBM = pl.BlockSpec(memory_space=pltpu.HBM)
LOCAL = (ROWS, COLS, LEVELS, D)


def pack(place, activations, cotangent):
    return pl.pallas_call(
        pack_kernel,
        out_shape=(jax.ShapeDtypeStruct((4 * QUARTER, D), jnp.bfloat16),) * 4,
        in_specs=[SMEM, VMEM, VMEM],
        out_specs=(VMEM,) * 4,
        scratch_shapes=[
            pltpu.VMEM((32, LEVELS * HALF_LAT * HALF_LON, 128), jnp.float32),
        ],
        compiler_params=pltpu.CompilerParams(vmem_limit_bytes=32 * 2**20),
        cost_estimate=pl.CostEstimate(flops=0, bytes_accessed=1200000, transcendentals=0),
        name="pack",
    )(place, activations.transpose(1, 2, 0, 3), cotangent.transpose(1, 2, 0, 3))


def unpack_kernel(place, own, lon_ref, lat_both, cot, out, cot_ref, lines, semaphores):
    (copy,) = fetched((cot,), (cot_ref,), semaphores)
    own, lon = (ref[: 2 * QUARTER].astype(jnp.float32) for ref in (own, lon_ref))
    lat, both = (lat_both[part * 2 * QUARTER : (part + 1) * 2 * QUARTER].astype(jnp.float32) for part in range(2))
    even = place[0] == 0
    whole = {
        (0, 0): jnp.where(even, own, lon),
        (0, 1): jnp.where(even, lon, own),
        (1, 0): jnp.where(even, both, lat),
        (1, 1): jnp.where(even, lat, both),
    }
    copy.wait()
    count = HALF_LAT * HALF_LON
    for (row_half, col_half), quarter in whole.items():
        held = [lines.at[4 * (2 * row_half + col_half) + part] for part in range(4)]
        for at, level in enumerate(PAIRS[0] + PAIRS[1]):
            for part in range(4):
                cut = quarter[at * count : (at + 1) * count, 128 * part : 128 * part + 128]
                held[part][pl.ds(level, count, stride=LEVELS)] = cut
        for row in range(HALF_LAT):
            for col in range(HALF_LON):
                at = pl.ds(LEVELS * (row * HALF_LON + col), LEVELS)
                token = jnp.concatenate([part[at] for part in held], axis=1)
                place_of = (row_half * HALF_LAT + row, col_half * HALF_LON + col)
                out[place_of] = (cot_ref[place_of].astype(jnp.float32) + token).astype(jnp.bfloat16)


def unpack(place, cotangent, *quarters):
    local = pl.pallas_call(
        unpack_kernel,
        out_shape=jax.ShapeDtypeStruct(LOCAL, jnp.bfloat16),
        in_specs=[SMEM] + [VMEM] * 3 + [HBM],
        out_specs=VMEM,
        scratch_shapes=[
            pltpu.VMEM(LOCAL, jnp.bfloat16),
            pltpu.VMEM((16, LEVELS * HALF_LAT * HALF_LON, 128), jnp.float32),
            pltpu.SemaphoreType.DMA((1,)),
        ],
        compiler_params=pltpu.CompilerParams(vmem_limit_bytes=32 * 2**20),
        cost_estimate=pl.CostEstimate(flops=0, bytes_accessed=900000, transcendentals=0),
        name="unpack",
    )(place, *quarters, cotangent.transpose(1, 2, 0, 3))
    return local.transpose(2, 0, 1, 3)


def weights_kernel(qkv_weight, proj_weight, qkv_held, proj_held, semaphores):
    for copy in fetched((qkv_weight, proj_weight), (qkv_held, proj_held), semaphores):
        copy.wait()


def near_weights(qkv_weight, proj_weight):
    return pl.pallas_call(
        weights_kernel,
        out_shape=(rows_of(D, 3 * D), rows_of(D)),
        in_specs=[HBM, HBM],
        out_specs=(VMEM, VMEM),
        scratch_shapes=[pltpu.SemaphoreType.DMA((2,))],
        compiler_params=pltpu.CompilerParams(vmem_limit_bytes=32 * 2**20),
        cost_estimate=pl.CostEstimate(flops=0, bytes_accessed=4 * 2**20, transcendentals=0),
        name="near_weights",
    )(qkv_weight, proj_weight)


def block_kernel(place, *refs):
    quarters, (qkv_weight, proj_weight), theirs, mine, (own, lat, lon_both) = refs[:4], refs[4:6], refs[6:8], refs[8:10], refs[10:13]
    x_held, cot_held, normed, attended, qkv_grad, qkv, upstream, tiles = refs[13:]
    own_ref, both_ref, lon_ref, lat_ref = quarters
    held = [ref[...].astype(jnp.float32) for ref in (own_ref, lon_ref, lat_ref, both_ref)]
    for kind, target in enumerate((x_held, cot_held)):
        chunks = [
            held[quarter][(2 * kind + window) * QUARTER : (2 * kind + window + 1) * QUARTER]
            for window in range(2)
            for quarter in range(4)
        ]
        target[...] = jnp.concatenate(chunks, axis=0).astype(jnp.bfloat16)
    x = x_held[...].astype(jnp.float32)
    centered = x - jnp.mean(x, axis=-1, keepdims=True)
    inverse = lax.rsqrt(jnp.mean(centered * centered, axis=-1, keepdims=True) + 1e-05)
    normed[...] = (centered * inverse).astype(jnp.bfloat16)

    for step in range(3 * D // 256):
        cols = slice(step * 256, (step + 1) * 256)
        gain = HEAD_DIM ** (-0.5) if step < D // 256 else 1.0
        qkv[:, cols] = (dot(normed[...], qkv_weight[:, cols], 1, 0) * gain).astype(jnp.bfloat16)
    for step in range(D // 256):
        cols = slice(step * 256, (step + 1) * 256)
        upstream[:, cols] = dot(cot_held[...], proj_weight[cols, :], 1, 1).astype(jnp.bfloat16)

    head_of = lax.broadcasted_iota(jnp.int32, (WINDOW, GROUP * HEAD_DIM), 1) // HEAD_DIM
    zero = jnp.zeros((WINDOW, GROUP * HEAD_DIM), jnp.bfloat16)

    def apart(slab):
        return jnp.concatenate([jnp.where(head_of == head, slab, zero) for head in range(GROUP)], axis=0)

    def together(tall):
        merged = tall[:WINDOW]
        for head in range(1, GROUP):
            merged = jnp.where(head_of == head, tall[head * WINDOW : (head + 1) * WINDOW], merged)
        return merged.astype(jnp.bfloat16)

    for window in range(2):
        rows = slice(window * WINDOW, (window + 1) * WINDOW)
        shape = (WINDOW, GROUP * WINDOW)
        key_label = token_labels(lax.broadcasted_iota(jnp.int32, shape, 0), window, place[1], place[2])
        query_label = token_labels(lax.broadcasted_iota(jnp.int32, shape, 1) % WINDOW, window, place[1], place[2])
        bias = jnp.where(key_label == query_label, 0.0, -1000000000.0)
        for group in range(HEADS // GROUP):
            cols = [slice(part * D + group * GROUP * HEAD_DIM, part * D + (group + 1) * GROUP * HEAD_DIM) for part in range(3)]
            query, keys, values = (qkv[rows, at] for at in cols)
            query, grad = apart(query), apart(upstream[rows, cols[0]])
            scores = dot(keys, query, 1, 1) + bias
            expo = jnp.exp(scores - jnp.max(scores, axis=0, keepdims=True))
            probs = expo * (1.0 / jnp.sum(expo, axis=0, keepdims=True))
            low = probs.astype(jnp.bfloat16)
            prob_grad = dot(values, grad, 1, 1)
            inner = jnp.sum(probs * prob_grad, axis=0, keepdims=True)
            score_grad = (probs * (prob_grad - inner)).astype(jnp.bfloat16)
            attended[rows, cols[0]] = together(dot(low, values, 0, 0))
            qkv_grad[rows, cols[0]] = together(dot(score_grad, keys, 0, 0) * HEAD_DIM ** (-0.5))
            qkv_grad[rows, cols[1]] = dot(score_grad, query, 1, 0).astype(jnp.bfloat16)
            qkv_grad[rows, cols[2]] = dot(low, grad, 1, 0).astype(jnp.bfloat16)

    def put(step, grads):
        grads = grads.astype(jnp.bfloat16)
        for half in range(2):
            rows = grads[half * (D // 2) : (half + 1) * (D // 2)]
            for part in range(2):
                tiles[half, :, 2 * step + part] = rows[:, 128 * part : 128 * part + 128].reshape(D // 32, 16, 128)

    tall = normed[...].T
    for step in range(3 * D // 256):
        put(step, dot(tall, qkv_grad[:, step * 256 : (step + 1) * 256], 1, 0))
    tall = attended[...].T
    for step in range(D // 256):
        put(step + 3 * D // 256, dot(tall, cot_held[:, step * 256 : (step + 1) * 256], 1, 0))
    for chunk in range(2):
        rows = slice(chunk * D // 64, (chunk + 1) * D // 64)
        theirs[chunk][...] = tiles[1 - place[3], rows]
        mine[chunk][...] = tiles[place[3], rows]
    normed_grad = dot(qkv_grad[...], qkv_weight[...], 1, 1)
    x = x_held[...].astype(jnp.float32)
    centered = x - jnp.mean(x, axis=-1, keepdims=True)
    inverse = lax.rsqrt(jnp.mean(centered * centered, axis=-1, keepdims=True) + 1e-05)
    xhat = centered * inverse
    average = jnp.mean(normed_grad, axis=-1, keepdims=True)
    product = jnp.mean(normed_grad * xhat, axis=-1, keepdims=True)
    dx = inverse * (normed_grad - average - xhat * product)
    for target, kinds in ((own, (0,)), (lat, (2,)), (lon_both, (1, 3))):
        chunks = [
            dx[(4 * window + kind) * QUARTER : (4 * window + kind + 1) * QUARTER] for kind in kinds for window in range(2)
        ]
        target[...] = jnp.concatenate(chunks, axis=0).astype(jnp.bfloat16)


CHUNK_TILES = jax.ShapeDtypeStruct((D // 64, 4 * D // 128, 16, 128), jnp.bfloat16)


def rows_of(count, width=D):
    return jax.ShapeDtypeStruct((count, width), jnp.bfloat16)


def block(place, quarters, qkv_weight, proj_weight):
    return pl.pallas_call(
        block_kernel,
        out_shape=(CHUNK_TILES,) * 4 + (rows_of(2 * QUARTER), rows_of(2 * QUARTER), rows_of(4 * QUARTER)),
        in_specs=[SMEM] + [VMEM] * 6,
        out_specs=(VMEM,) * 7,
        scratch_shapes=[
            pltpu.VMEM((TOKENS, D), jnp.bfloat16),
            pltpu.VMEM((TOKENS, D), jnp.bfloat16),
            pltpu.VMEM((TOKENS, D), jnp.bfloat16),
            pltpu.VMEM((TOKENS, D), jnp.bfloat16),
            pltpu.VMEM((TOKENS, 3 * D), jnp.bfloat16),
            pltpu.VMEM((TOKENS, 3 * D), jnp.bfloat16),
            pltpu.VMEM((TOKENS, D), jnp.bfloat16),
            pltpu.VMEM((2, D // 32, 4 * D // 128, 16, 128), jnp.bfloat16),
        ],
        compiler_params=pltpu.CompilerParams(vmem_limit_bytes=48 * 2**20),
        cost_estimate=pl.CostEstimate(flops=2 * 10**9, bytes_accessed=6 * 10**6, transcendentals=6 * 10**5),
        name="block",
    )(place, *quarters, qkv_weight, proj_weight)


def added(arrived):
    total = arrived[0].astype(jnp.float32)
    for part in range(1, arrived.shape[0]):
        total = total + arrived[part].astype(jnp.float32)
    return total


def device_groups(members):
    tall, wide = lax.axis_size("y_hi"), lax.axis_size("x")
    cores, y_los = lax.axis_size("core"), lax.axis_size("y_lo")

    def index(z, y, x, core):
        return (((z * tall + y // y_los) * cores + core) * wide + x) * y_los + y % y_los

    return [[index(*at, core) for at in group] for core in range(cores) for group in members(core)]


def chips():
    return lax.axis_size("z"), lax.axis_size("y_hi") * lax.axis_size("y_lo"), lax.axis_size("x")


def cube_groups(stride):
    def along(size):
        firsts = [at for at in range(size) if at // stride % 2 == 0]
        return [[at, at + stride] if at + stride < size else [at] for at in firsts]

    def members(core):
        return [list(itertools.product(*lines)) for lines in itertools.product(*(along(size) for size in chips()))]

    return device_groups(members)


def strided(size):
    step = min(size, 2)
    return [list(range(parity, size, step)) for parity in range(step)]


def middle_groups():
    def members(core):
        z_size, y_size, x_size = chips()
        xs = strided(x_size)
        if core == 0:
            return [[(z, y, x) for x in xa for z in za] for xa in xs for za in strided(z_size) for y in range(y_size)]
        return [[(z, y, x) for x in xa for y in ya] for xa in xs for ya in strided(y_size) for z in range(z_size)]

    return device_groups(members)


def far_groups():
    def members(core):
        z_size, y_size, x_size = chips()
        if core == 0:
            return [[(z, y, x) for y in ya] for ya in strided(y_size) for z in range(z_size) for x in range(x_size)]
        return [[(z, y, x) for z in za] for za in strided(z_size) for y in range(y_size) for x in range(x_size)]

    return device_groups(members)


def swapped(value):
    at = [(z, y, x) for z, y, x in itertools.product(*(range(size) for size in chips()))]
    first, second = device_groups(lambda core: [at])
    return lax.ppermute(value, ALL, [*zip(first, second), *zip(second, first)])


def all_to_all(split, groups):
    return lax.all_to_all(split, ALL, 0, 0, axis_index_groups=groups)


def scattered_sum(tiles, groups):
    count = len(groups[0])
    split = tiles.reshape((count, tiles.shape[0] // count) + tiles.shape[1:])
    return added(all_to_all(split, groups)).astype(jnp.bfloat16)


def exchanged(tiles, groups):
    return all_to_all(jnp.broadcast_to(tiles[None], (len(groups[0]),) + tiles.shape), groups)


def gathered(tiles, groups):
    return exchanged(tiles, groups).reshape((-1,) + tiles.shape[1:])


def untile_kernel(other, place, *refs):
    qkv_out, proj_out, qkv_held, proj_held, semaphores = refs[-5:]
    first = (1 - place[3] if other else place[3]) * (D // 2)
    height = D // 8
    copies = []
    for at in range(4):
        tiles = refs[at // 2].at[at % 2 * height // 16 : (at % 2 + 1) * height // 16]
        rows = slice(at * height, (at + 1) * height)
        for col in range(4 * D // 128):
            strip = tiles[:, col].reshape(height, 128)
            if col < 3 * D // 128:
                qkv_held[rows, 128 * col : 128 * col + 128] = strip
            else:
                proj_held[rows, 128 * col - 3 * D : 128 * col - 3 * D + 128] = strip
        target = pl.ds(pl.multiple_of(first + at * height, height), height)
        for kind, (held, out) in enumerate(((qkv_held, qkv_out), (proj_held, proj_out))):
            copies.append(pltpu.make_async_copy(held.at[rows], out.at[target], semaphores.at[2 * at + kind]))
            copies[-1].start()
    for copy in copies:
        copy.wait()


def untile(place, chunks, other, so_far=()):
    return pl.pallas_call(
        functools.partial(untile_kernel, other),
        in_specs=[SMEM, VMEM, VMEM] + [HBM] * len(so_far),
        out_specs=(HBM, HBM),
        out_shape=(rows_of(D, 3 * D), rows_of(D)),
        scratch_shapes=[
            pltpu.VMEM((D // 2, 3 * D), jnp.bfloat16),
            pltpu.VMEM((D // 2, D), jnp.bfloat16),
            pltpu.SemaphoreType.DMA((8,)),
        ],
        input_output_aliases={3: 0, 4: 1} if so_far else {},
        compiler_params=pltpu.CompilerParams(vmem_limit_bytes=32 * 2**20),
        cost_estimate=pl.CostEstimate(flops=0, bytes_accessed=2 * 2**20, transcendentals=0),
        name="untile_other" if other else "untile_own",
    )(place, *chunks, *so_far)


def per_device(activations, cotangent, qkv_weight, proj_weight):
    lat, lon = lax.axis_index(LAT), lax.axis_index(LON)
    odd = lat % 2 == 1
    lon_edge = jnp.where(odd, lon == lax.axis_size(LON) - 1, lon == 0)
    place = jnp.stack([odd, lat == 0, lon_edge, lax.axis_index("core") == 1]).astype(jnp.int32)
    own, lon, lat, both = pack(place, activations, cotangent)
    own, qkv_weight, proj_weight = lax.optimization_barrier((own, qkv_weight, proj_weight))
    both, lon, lat = moved(both, 3, False), moved(lon, 1, False), moved(lat, 2, False)
    qkv_weight, proj_weight = near_weights(qkv_weight, proj_weight)
    *grads, own, lat, lon_both = block(place, (own, both, lon, lat), qkv_weight, proj_weight)

    near, middle, far = cube_groups(1), middle_groups(), far_groups()
    chunks = []
    for theirs, mine in zip(grads[:2], grads[2:]):
        chunk = (mine.astype(jnp.float32) + swapped(theirs).astype(jnp.float32)).astype(jnp.bfloat16)
        chunks.append(scattered_sum(chunk.reshape(-1, 16, 128), near))
    tiles = jnp.concatenate(chunks, axis=0)
    tiles, lon_both = lax.optimization_barrier((tiles, lon_both))
    tiles = scattered_sum(tiles, middle)
    factor = (LEVELS * ROWS * COLS * lax.axis_size(ALL)) ** (-0.5)
    tiles, lon_both = lax.optimization_barrier((exchanged(tiles, far), moved(lon_both, 1, True)))
    tiles = (added(tiles) * factor).astype(jnp.bfloat16)
    lat_both = jnp.concatenate([lat, lon_both[2 * QUARTER :]], axis=0)
    tiles, lat_both = lax.optimization_barrier((tiles, lat_both))
    tiles, lat_both = lax.optimization_barrier((gathered(tiles, middle), moved(lat_both, 2, True)))
    input_grad = unpack(place, cotangent, own, lon_both, lat_both)
    chunks = [gathered(chunk, near).reshape(CHUNK_TILES.shape) for chunk in jnp.split(tiles, 2)]
    arrived = [swapped(chunk) for chunk in chunks]
    chunks, input_grad = lax.optimization_barrier((chunks, input_grad))
    grads = untile(place, chunks, False)
    arrived, grads = lax.optimization_barrier((arrived, grads))
    qkv_weight_grad, proj_weight_grad = untile(place, arrived, True, grads)
    return (input_grad, qkv_weight_grad, proj_weight_grad)


def over(physical):
    spec = P(None, LAT, LON, None)
    return jax.shard_map(
        per_device,
        mesh=physical,
        in_specs=(spec, spec, P(), P()),
        out_specs=(spec, P(), P()),
        check_vma=False,
    )


def solution(mesh):
    return over(Mesh(mesh.devices.reshape(8, 4, 2, 4, 2), ALL))
```

```python
import functools
import itertools

import jax
import jax.numpy as jnp
from jax import lax
from jax.experimental import pallas as pl
from jax.experimental.pallas import tpu as pltpu
from jax.sharding import Mesh, PartitionSpec as P

D = 512
HEADS = 8
HEAD_DIM = 64
GROUP = 4
LEVELS = 4
HALF_LAT = 3
HALF_LON = 6
ROWS = 6
COLS = 12
PAIRS = ((1, 2), (3, 0))
QUARTER = 2 * HALF_LAT * HALF_LON
WINDOW = 4 * QUARTER
TOKENS = 2 * WINDOW

LON = ("z", "y_hi", "core")
LAT = ("x", "y_lo")
ALL = LON + LAT


def dot(a, b, a_dim, b_dim):
    return lax.dot_general(a, b, (((a_dim,), (b_dim,)), ((), ())), preferred_element_type=jnp.float32)


def owner_of(kind, lat, lon):
    lat = lat + kind // 2
    return lat, lon + kind % 2 * (-1 if lat % 2 == 1 else 1)


def moved(value, kind, back):
    lons, lats = lax.axis_size(LON), lax.axis_size(LAT)
    pairs = []
    for lon in range(lons):
        for lat in range(lats):
            to_lat, to_lon = owner_of(kind, lat, lon)
            pair = (lon * lats + lat, to_lon % lons * lats + to_lat % lats)
            pairs.append(pair[::-1] if back else pair)
    return lax.ppermute(value, ALL, pairs)


def token_labels(token, window, lat_edge, lon_edge):
    quarter = token // QUARTER
    level = token % QUARTER // (QUARTER // 2)
    return level * window + 2 * lat_edge * (quarter // 2) + 4 * lon_edge * (quarter % 2)


def fetched(sources, targets, semaphores):
    copies = [
        pltpu.make_async_copy(source, target, semaphores.at[at])
        for at, (source, target) in enumerate(zip(sources, targets))
    ]
    for copy in copies:
        copy.start()
    return copies


def pack_kernel(place, act_ref, cot_ref, own, lon, lat, both, lines):
    cuts = {(row_half, col_half): [] for row_half in range(2) for col_half in range(2)}
    for kind, ref in enumerate((act_ref, cot_ref)):
        for row_half, col_half in cuts:
            held = [lines.at[4 * (4 * kind + 2 * row_half + col_half) + part] for part in range(4)]
            for row in range(HALF_LAT):
                for col in range(HALF_LON):
                    token = ref[row_half * HALF_LAT + row, col_half * HALF_LON + col].astype(jnp.float32)
                    at = pl.ds(LEVELS * (row * HALF_LON + col), LEVELS)
                    for part in range(4):
                        held[part][at] = token[:, 128 * part : 128 * part + 128]
            for pair in PAIRS:
                for level in pair:
                    at = pl.ds(level, HALF_LAT * HALF_LON, stride=LEVELS)
                    cuts[row_half, col_half].append(jnp.concatenate([part[at] for part in held], axis=1))
    whole = {at: jnp.concatenate(pieces, axis=0).astype(jnp.bfloat16) for at, pieces in cuts.items()}

    def put(parity):
        own[...] = whole[0, parity]
        lon[...] = whole[0, 1 - parity]
        lat[...] = whole[1, 1 - parity]
        both[...] = whole[1, parity]

    for parity in range(2):
        pl.when(place[0] == parity)(lambda parity=parity: put(parity))


SMEM = pl.BlockSpec(memory_space=pltpu.SMEM)
VMEM = pl.BlockSpec(memory_space=pltpu.VMEM)
HBM = pl.BlockSpec(memory_space=pltpu.HBM)
LOCAL = (ROWS, COLS, LEVELS, D)


def pack(place, activations, cotangent):
    return pl.pallas_call(
        pack_kernel,
        out_shape=(jax.ShapeDtypeStruct((4 * QUARTER, D), jnp.bfloat16),) * 4,
        in_specs=[SMEM, VMEM, VMEM],
        out_specs=(VMEM,) * 4,
        scratch_shapes=[
            pltpu.VMEM((32, LEVELS * HALF_LAT * HALF_LON, 128), jnp.float32),
        ],
        compiler_params=pltpu.CompilerParams(vmem_limit_bytes=32 * 2**20),
        cost_estimate=pl.CostEstimate(flops=0, bytes_accessed=1200000, transcendentals=0),
        name="pack",
    )(place, activations.transpose(1, 2, 0, 3), cotangent.transpose(1, 2, 0, 3))


def unpack_kernel(place, own, lon_ref, lat_both, cot, out, cot_ref, lines, semaphores):
    (copy,) = fetched((cot,), (cot_ref,), semaphores)
    own, lon = (ref[: 2 * QUARTER].astype(jnp.float32) for ref in (own, lon_ref))
    lat, both = (lat_both[part * 2 * QUARTER : (part + 1) * 2 * QUARTER].astype(jnp.float32) for part in range(2))
    even = place[0] == 0
    whole = {
        (0, 0): jnp.where(even, own, lon),
        (0, 1): jnp.where(even, lon, own),
        (1, 0): jnp.where(even, both, lat),
        (1, 1): jnp.where(even, lat, both),
    }
    copy.wait()
    count = HALF_LAT * HALF_LON
    for (row_half, col_half), quarter in whole.items():
        held = [lines.at[4 * (2 * row_half + col_half) + part] for part in range(4)]
        for at, level in enumerate(PAIRS[0] + PAIRS[1]):
            for part in range(4):
                cut = quarter[at * count : (at + 1) * count, 128 * part : 128 * part + 128]
                held[part][pl.ds(level, count, stride=LEVELS)] = cut
        for row in range(HALF_LAT):
            for col in range(HALF_LON):
                at = pl.ds(LEVELS * (row * HALF_LON + col), LEVELS)
                token = jnp.concatenate([part[at] for part in held], axis=1)
                place_of = (row_half * HALF_LAT + row, col_half * HALF_LON + col)
                out[place_of] = (cot_ref[place_of].astype(jnp.float32) + token).astype(jnp.bfloat16)


def unpack(place, cotangent, *quarters):
    local = pl.pallas_call(
        unpack_kernel,
        out_shape=jax.ShapeDtypeStruct(LOCAL, jnp.bfloat16),
        in_specs=[SMEM] + [VMEM] * 3 + [HBM],
        out_specs=VMEM,
        scratch_shapes=[
            pltpu.VMEM(LOCAL, jnp.bfloat16),
            pltpu.VMEM((16, LEVELS * HALF_LAT * HALF_LON, 128), jnp.float32),
            pltpu.SemaphoreType.DMA((1,)),
        ],
        compiler_params=pltpu.CompilerParams(vmem_limit_bytes=32 * 2**20),
        cost_estimate=pl.CostEstimate(flops=0, bytes_accessed=900000, transcendentals=0),
        name="unpack",
    )(place, *quarters, cotangent.transpose(1, 2, 0, 3))
    return local.transpose(2, 0, 1, 3)


def weights_kernel(qkv_weight, proj_weight, qkv_held, proj_held, semaphores):
    for copy in fetched((qkv_weight, proj_weight), (qkv_held, proj_held), semaphores):
        copy.wait()


def near_weights(qkv_weight, proj_weight):
    return pl.pallas_call(
        weights_kernel,
        out_shape=(rows_of(D, 3 * D), rows_of(D)),
        in_specs=[HBM, HBM],
        out_specs=(VMEM, VMEM),
        scratch_shapes=[pltpu.SemaphoreType.DMA((2,))],
        compiler_params=pltpu.CompilerParams(vmem_limit_bytes=32 * 2**20),
        cost_estimate=pl.CostEstimate(flops=0, bytes_accessed=4 * 2**20, transcendentals=0),
        name="near_weights",
    )(qkv_weight, proj_weight)


def block_kernel(place, *refs):
    quarters, (qkv_weight, proj_weight), (theirs, mine, own, lat, lon_both) = refs[:4], refs[4:6], refs[6:11]
    x_held, cot_held, normed, attended, qkv_grad, qkv, upstream, tiles = refs[11:]
    own_ref, both_ref, lon_ref, lat_ref = quarters
    held = [ref[...].astype(jnp.float32) for ref in (own_ref, lon_ref, lat_ref, both_ref)]
    for kind, target in enumerate((x_held, cot_held)):
        chunks = [
            held[quarter][(2 * kind + window) * QUARTER : (2 * kind + window + 1) * QUARTER]
            for window in range(2)
            for quarter in range(4)
        ]
        target[...] = jnp.concatenate(chunks, axis=0).astype(jnp.bfloat16)
    x = x_held[...].astype(jnp.float32)
    centered = x - jnp.mean(x, axis=-1, keepdims=True)
    inverse = lax.rsqrt(jnp.mean(centered * centered, axis=-1, keepdims=True) + 1e-05)
    normed[...] = (centered * inverse).astype(jnp.bfloat16)

    for step in range(3 * D // 256):
        cols = slice(step * 256, (step + 1) * 256)
        gain = HEAD_DIM ** (-0.5) if step < D // 256 else 1.0
        qkv[:, cols] = (dot(normed[...], qkv_weight[:, cols], 1, 0) * gain).astype(jnp.bfloat16)
    for step in range(D // 256):
        cols = slice(step * 256, (step + 1) * 256)
        upstream[:, cols] = dot(cot_held[...], proj_weight[cols, :], 1, 1).astype(jnp.bfloat16)

    head_of = lax.broadcasted_iota(jnp.int32, (WINDOW, GROUP * HEAD_DIM), 1) // HEAD_DIM
    zero = jnp.zeros((WINDOW, GROUP * HEAD_DIM), jnp.bfloat16)

    def apart(slab):
        return jnp.concatenate([jnp.where(head_of == head, slab, zero) for head in range(GROUP)], axis=0)

    def together(tall):
        merged = tall[:WINDOW]
        for head in range(1, GROUP):
            merged = jnp.where(head_of == head, tall[head * WINDOW : (head + 1) * WINDOW], merged)
        return merged.astype(jnp.bfloat16)

    for window in range(2):
        rows = slice(window * WINDOW, (window + 1) * WINDOW)
        shape = (WINDOW, GROUP * WINDOW)
        key_label = token_labels(lax.broadcasted_iota(jnp.int32, shape, 0), window, place[1], place[2])
        query_label = token_labels(lax.broadcasted_iota(jnp.int32, shape, 1) % WINDOW, window, place[1], place[2])
        bias = jnp.where(key_label == query_label, 0.0, -1000000000.0)
        for group in range(HEADS // GROUP):
            cols = [slice(part * D + group * GROUP * HEAD_DIM, part * D + (group + 1) * GROUP * HEAD_DIM) for part in range(3)]
            query, keys, values = (qkv[rows, at] for at in cols)
            query, grad = apart(query), apart(upstream[rows, cols[0]])
            scores = dot(keys, query, 1, 1) + bias
            expo = jnp.exp(scores - jnp.max(scores, axis=0, keepdims=True))
            probs = expo * (1.0 / jnp.sum(expo, axis=0, keepdims=True))
            low = probs.astype(jnp.bfloat16)
            prob_grad = dot(values, grad, 1, 1)
            inner = jnp.sum(probs * prob_grad, axis=0, keepdims=True)
            score_grad = (probs * (prob_grad - inner)).astype(jnp.bfloat16)
            attended[rows, cols[0]] = together(dot(low, values, 0, 0))
            qkv_grad[rows, cols[0]] = together(dot(score_grad, keys, 0, 0) * HEAD_DIM ** (-0.5))
            qkv_grad[rows, cols[1]] = dot(score_grad, query, 1, 0).astype(jnp.bfloat16)
            qkv_grad[rows, cols[2]] = dot(low, grad, 1, 0).astype(jnp.bfloat16)

    def put(step, grads):
        grads = grads.astype(jnp.bfloat16)
        for half in range(2):
            rows = grads[half * (D // 2) : (half + 1) * (D // 2)]
            for part in range(2):
                tiles[half, :, 2 * step + part] = rows[:, 128 * part : 128 * part + 128].reshape(D // 32, 16, 128)

    tall = normed[...].T
    for step in range(3 * D // 256):
        put(step, dot(tall, qkv_grad[:, step * 256 : (step + 1) * 256], 1, 0))
    tall = attended[...].T
    for step in range(D // 256):
        put(step + 3 * D // 256, dot(tall, cot_held[:, step * 256 : (step + 1) * 256], 1, 0))
    theirs[...] = tiles[1 - place[3]]
    mine[...] = tiles[place[3]]
    normed_grad = dot(qkv_grad[...], qkv_weight[...], 1, 1)
    x = x_held[...].astype(jnp.float32)
    centered = x - jnp.mean(x, axis=-1, keepdims=True)
    inverse = lax.rsqrt(jnp.mean(centered * centered, axis=-1, keepdims=True) + 1e-05)
    xhat = centered * inverse
    average = jnp.mean(normed_grad, axis=-1, keepdims=True)
    product = jnp.mean(normed_grad * xhat, axis=-1, keepdims=True)
    dx = inverse * (normed_grad - average - xhat * product)
    for target, kinds in ((own, (0,)), (lat, (2,)), (lon_both, (1, 3))):
        chunks = [
            dx[(4 * window + kind) * QUARTER : (4 * window + kind + 1) * QUARTER] for kind in kinds for window in range(2)
        ]
        target[...] = jnp.concatenate(chunks, axis=0).astype(jnp.bfloat16)


HALF_TILES = jax.ShapeDtypeStruct((D // 32, 4 * D // 128, 16, 128), jnp.bfloat16)


def rows_of(count, width=D):
    return jax.ShapeDtypeStruct((count, width), jnp.bfloat16)


def block(place, quarters, qkv_weight, proj_weight):
    return pl.pallas_call(
        block_kernel,
        out_shape=(HALF_TILES, HALF_TILES, rows_of(2 * QUARTER), rows_of(2 * QUARTER), rows_of(4 * QUARTER)),
        in_specs=[SMEM] + [VMEM] * 6,
        out_specs=(VMEM,) * 5,
        scratch_shapes=[
            pltpu.VMEM((TOKENS, D), jnp.bfloat16),
            pltpu.VMEM((TOKENS, D), jnp.bfloat16),
            pltpu.VMEM((TOKENS, D), jnp.bfloat16),
            pltpu.VMEM((TOKENS, D), jnp.bfloat16),
            pltpu.VMEM((TOKENS, 3 * D), jnp.bfloat16),
            pltpu.VMEM((TOKENS, 3 * D), jnp.bfloat16),
            pltpu.VMEM((TOKENS, D), jnp.bfloat16),
            pltpu.VMEM((2,) + HALF_TILES.shape, jnp.bfloat16),
        ],
        compiler_params=pltpu.CompilerParams(vmem_limit_bytes=48 * 2**20),
        cost_estimate=pl.CostEstimate(flops=2 * 10**9, bytes_accessed=6 * 10**6, transcendentals=6 * 10**5),
        name="block",
    )(place, *quarters, qkv_weight, proj_weight)


def added(arrived):
    total = arrived[0].astype(jnp.float32)
    for part in range(1, arrived.shape[0]):
        total = total + arrived[part].astype(jnp.float32)
    return total


def device_groups(members):
    tall, wide = lax.axis_size("y_hi"), lax.axis_size("x")
    cores, y_los = lax.axis_size("core"), lax.axis_size("y_lo")

    def index(z, y, x, core):
        return (((z * tall + y // y_los) * cores + core) * wide + x) * y_los + y % y_los

    return [[index(*at, core) for at in group] for core in range(cores) for group in members(core)]


def chips():
    return lax.axis_size("z"), lax.axis_size("y_hi") * lax.axis_size("y_lo"), lax.axis_size("x")


def cube_groups(stride):
    def along(size):
        firsts = [at for at in range(size) if at // stride % 2 == 0]
        return [[at, at + stride] if at + stride < size else [at] for at in firsts]

    def members(core):
        return [list(itertools.product(*lines)) for lines in itertools.product(*(along(size) for size in chips()))]

    return device_groups(members)


def strided(size):
    step = min(size, 2)
    return [list(range(parity, size, step)) for parity in range(step)]


def middle_groups():
    def members(core):
        z_size, y_size, x_size = chips()
        xs = strided(x_size)
        if core == 0:
            return [[(z, y, x) for x in xa for z in za] for xa in xs for za in strided(z_size) for y in range(y_size)]
        return [[(z, y, x) for x in xa for y in ya] for xa in xs for ya in strided(y_size) for z in range(z_size)]

    return device_groups(members)


def far_groups():
    def members(core):
        z_size, y_size, x_size = chips()
        if core == 0:
            return [[(z, y, x) for y in ya] for ya in strided(y_size) for z in range(z_size) for x in range(x_size)]
        return [[(z, y, x) for z in za] for za in strided(z_size) for y in range(y_size) for x in range(x_size)]

    return device_groups(members)


def swapped(value):
    at = [(z, y, x) for z, y, x in itertools.product(*(range(size) for size in chips()))]
    first, second = device_groups(lambda core: [at])
    return lax.ppermute(value, ALL, [*zip(first, second), *zip(second, first)])


def all_to_all(split, groups):
    return lax.all_to_all(split, ALL, 0, 0, axis_index_groups=groups)


def scattered_sum(tiles, groups):
    count = len(groups[0])
    split = tiles.reshape((count, tiles.shape[0] // count) + tiles.shape[1:])
    return added(all_to_all(split, groups)).astype(jnp.bfloat16)


def exchanged(tiles, groups):
    return all_to_all(jnp.broadcast_to(tiles[None], (len(groups[0]),) + tiles.shape), groups)


def gathered(tiles, groups):
    return exchanged(tiles, groups).reshape((-1,) + tiles.shape[1:])


def untile_kernel(other, place, tiles, *refs):
    qkv_out, proj_out, qkv_held, proj_held, semaphores = refs[-5:]
    first = (1 - place[3] if other else place[3]) * (D // 2)
    chunk = D // 2 // CHUNKS
    copies = []
    for at in range(CHUNKS):
        rows = slice(at * chunk, (at + 1) * chunk)
        for col in range(4 * D // 128):
            strip = tiles[at * chunk // 16 : (at + 1) * chunk // 16, col].reshape(chunk, 128)
            if col < 3 * D // 128:
                qkv_held[rows, 128 * col : 128 * col + 128] = strip
            else:
                proj_held[rows, 128 * col - 3 * D : 128 * col - 3 * D + 128] = strip
        target = pl.ds(pl.multiple_of(first + at * chunk, chunk), chunk)
        for kind, (held, out) in enumerate(((qkv_held, qkv_out), (proj_held, proj_out))):
            copies.append(pltpu.make_async_copy(held.at[rows], out.at[target], semaphores.at[2 * at + kind]))
            copies[-1].start()
    for copy in copies:
        copy.wait()


CHUNKS = 4


def untile(place, tiles, other, so_far=()):
    return pl.pallas_call(
        functools.partial(untile_kernel, other),
        in_specs=[SMEM, VMEM] + [HBM] * len(so_far),
        out_specs=(HBM, HBM),
        out_shape=(rows_of(D, 3 * D), rows_of(D)),
        scratch_shapes=[
            pltpu.VMEM((D // 2, 3 * D), jnp.bfloat16),
            pltpu.VMEM((D // 2, D), jnp.bfloat16),
            pltpu.SemaphoreType.DMA((2 * CHUNKS,)),
        ],
        input_output_aliases={2: 0, 3: 1} if so_far else {},
        compiler_params=pltpu.CompilerParams(vmem_limit_bytes=32 * 2**20),
        cost_estimate=pl.CostEstimate(flops=0, bytes_accessed=2 * 2**20, transcendentals=0),
        name="untile_other" if other else "untile_own",
    )(place, tiles, *so_far)


def per_device(activations, cotangent, qkv_weight, proj_weight):
    lat, lon = lax.axis_index(LAT), lax.axis_index(LON)
    odd = lat % 2 == 1
    lon_edge = jnp.where(odd, lon == lax.axis_size(LON) - 1, lon == 0)
    place = jnp.stack([odd, lat == 0, lon_edge, lax.axis_index("core") == 1]).astype(jnp.int32)
    own, lon, lat, both = pack(place, activations, cotangent)
    own, qkv_weight, proj_weight = lax.optimization_barrier((own, qkv_weight, proj_weight))
    both, lon, lat = moved(both, 3, False), moved(lon, 1, False), moved(lat, 2, False)
    qkv_weight, proj_weight = near_weights(qkv_weight, proj_weight)
    theirs, mine, own, lat, lon_both = block(place, (own, both, lon, lat), qkv_weight, proj_weight)

    near, middle, far = cube_groups(1), middle_groups(), far_groups()
    tiles = (mine.astype(jnp.float32) + swapped(theirs).astype(jnp.float32)).astype(jnp.bfloat16)
    tiles = scattered_sum(tiles.reshape(-1, 16, 128), near)
    tiles, lon_both = lax.optimization_barrier((tiles, lon_both))
    tiles, lon_both = lax.optimization_barrier((scattered_sum(tiles, middle), moved(lon_both, 1, True)))
    lat_both = jnp.concatenate([lat, lon_both[2 * QUARTER :]], axis=0)
    tiles, lat_both = lax.optimization_barrier((tiles, lat_both))
    factor = (LEVELS * ROWS * COLS * lax.axis_size(ALL)) ** (-0.5)
    tiles = (added(exchanged(tiles, far)) * factor).astype(jnp.bfloat16)
    tiles, lat_both = lax.optimization_barrier((tiles, lat_both))
    tiles, lat_both = lax.optimization_barrier((gathered(tiles, middle), moved(lat_both, 2, True)))
    input_grad = unpack(place, cotangent, own, lon_both, lat_both)
    tiles, input_grad = lax.optimization_barrier((gathered(tiles, near), input_grad))
    tiles = tiles.reshape(HALF_TILES.shape)
    arrived = swapped(tiles)
    grads = untile(place, tiles, False)
    arrived, grads = lax.optimization_barrier((arrived, grads))
    qkv_weight_grad, proj_weight_grad = untile(place, arrived, True, grads)
    return (input_grad, qkv_weight_grad, proj_weight_grad)


def over(physical):
    spec = P(None, LAT, LON, None)
    return jax.shard_map(
        per_device,
        mesh=physical,
        in_specs=(spec, spec, P(), P()),
        out_specs=(spec, P(), P()),
        check_vma=False,
    )


def solution(mesh):
    return over(Mesh(mesh.devices.reshape(8, 4, 2, 4, 2), ALL))
```

```python
import functools
import itertools

import jax
import jax.numpy as jnp
from jax import lax
from jax.experimental import pallas as pl
from jax.experimental.pallas import tpu as pltpu
from jax.sharding import Mesh, PartitionSpec as P

D = 512
HEADS = 8
HEAD_DIM = 64
GROUP = 4
LEVELS = 4
HALF_LAT = 3
HALF_LON = 6
ROWS = 6
COLS = 12
PAIRS = ((1, 2), (3, 0))
QUARTER = 2 * HALF_LAT * HALF_LON
WINDOW = 4 * QUARTER
TOKENS = 2 * WINDOW

LON = ("z", "y_hi", "core")
LAT = ("x", "y_lo")
ALL = LON + LAT


def dot(a, b, a_dim, b_dim):
    return lax.dot_general(a, b, (((a_dim,), (b_dim,)), ((), ())), preferred_element_type=jnp.float32)


def owner_of(kind, lat, lon):
    lat = lat + kind // 2
    return lat, lon + kind % 2 * (-1 if lat % 2 == 1 else 1)


def moved(value, kind, back):
    lons, lats = lax.axis_size(LON), lax.axis_size(LAT)
    pairs = []
    for lon in range(lons):
        for lat in range(lats):
            to_lat, to_lon = owner_of(kind, lat, lon)
            pair = (lon * lats + lat, to_lon % lons * lats + to_lat % lats)
            pairs.append(pair[::-1] if back else pair)
    return lax.ppermute(value, ALL, pairs)


def token_labels(token, window, lat_edge, lon_edge):
    quarter = token // QUARTER
    level = token % QUARTER // (QUARTER // 2)
    return level * window + 2 * lat_edge * (quarter // 2) + 4 * lon_edge * (quarter % 2)


def fetched(sources, targets, semaphores):
    copies = [
        pltpu.make_async_copy(source, target, semaphores.at[at])
        for at, (source, target) in enumerate(zip(sources, targets))
    ]
    for copy in copies:
        copy.start()
    return copies


def pack_kernel(place, act_ref, cot_ref, own, lon, lat, both, lines):
    cuts = {(row_half, col_half): [] for row_half in range(2) for col_half in range(2)}
    for kind, ref in enumerate((act_ref, cot_ref)):
        for row_half, col_half in cuts:
            held = [lines.at[4 * (4 * kind + 2 * row_half + col_half) + part] for part in range(4)]
            for row in range(HALF_LAT):
                for col in range(HALF_LON):
                    token = ref[row_half * HALF_LAT + row, col_half * HALF_LON + col].astype(jnp.float32)
                    at = pl.ds(LEVELS * (row * HALF_LON + col), LEVELS)
                    for part in range(4):
                        held[part][at] = token[:, 128 * part : 128 * part + 128]
            for pair in PAIRS:
                for level in pair:
                    at = pl.ds(level, HALF_LAT * HALF_LON, stride=LEVELS)
                    cuts[row_half, col_half].append(jnp.concatenate([part[at] for part in held], axis=1))
    whole = {at: jnp.concatenate(pieces, axis=0).astype(jnp.bfloat16) for at, pieces in cuts.items()}

    def put(parity):
        own[...] = whole[0, parity]
        lon[...] = whole[0, 1 - parity]
        lat[...] = whole[1, 1 - parity]
        both[...] = whole[1, parity]

    for parity in range(2):
        pl.when(place[0] == parity)(lambda parity=parity: put(parity))


SMEM = pl.BlockSpec(memory_space=pltpu.SMEM)
VMEM = pl.BlockSpec(memory_space=pltpu.VMEM)
HBM = pl.BlockSpec(memory_space=pltpu.HBM)
LOCAL = (ROWS, COLS, LEVELS, D)


def pack(place, activations, cotangent):
    return pl.pallas_call(
        pack_kernel,
        out_shape=(jax.ShapeDtypeStruct((4 * QUARTER, D), jnp.bfloat16),) * 4,
        in_specs=[SMEM, VMEM, VMEM],
        out_specs=(VMEM,) * 4,
        scratch_shapes=[
            pltpu.VMEM((32, LEVELS * HALF_LAT * HALF_LON, 128), jnp.float32),
        ],
        compiler_params=pltpu.CompilerParams(vmem_limit_bytes=32 * 2**20),
        cost_estimate=pl.CostEstimate(flops=0, bytes_accessed=1200000, transcendentals=0),
        name="pack",
    )(place, activations.transpose(1, 2, 0, 3), cotangent.transpose(1, 2, 0, 3))


def unpack_kernel(place, own, lon, lat, both, cot, out, cot_ref, lines, semaphores):
    (copy,) = fetched((cot,), (cot_ref,), semaphores)
    own, lon, lat, both = (ref[...].astype(jnp.float32) for ref in (own, lon, lat, both))
    even = place[0] == 0
    whole = {
        (0, 0): jnp.where(even, own, lon),
        (0, 1): jnp.where(even, lon, own),
        (1, 0): jnp.where(even, both, lat),
        (1, 1): jnp.where(even, lat, both),
    }
    copy.wait()
    count = HALF_LAT * HALF_LON
    for (row_half, col_half), quarter in whole.items():
        held = [lines.at[4 * (2 * row_half + col_half) + part] for part in range(4)]
        for at, level in enumerate(PAIRS[0] + PAIRS[1]):
            for part in range(4):
                cut = quarter[at * count : (at + 1) * count, 128 * part : 128 * part + 128]
                held[part][pl.ds(level, count, stride=LEVELS)] = cut
        for row in range(HALF_LAT):
            for col in range(HALF_LON):
                at = pl.ds(LEVELS * (row * HALF_LON + col), LEVELS)
                token = jnp.concatenate([part[at] for part in held], axis=1)
                place_of = (row_half * HALF_LAT + row, col_half * HALF_LON + col)
                out[place_of] = (cot_ref[place_of].astype(jnp.float32) + token).astype(jnp.bfloat16)


def unpack(place, cotangent, *quarters):
    local = pl.pallas_call(
        unpack_kernel,
        out_shape=jax.ShapeDtypeStruct(LOCAL, jnp.bfloat16),
        in_specs=[SMEM] + [VMEM] * 4 + [HBM],
        out_specs=VMEM,
        scratch_shapes=[
            pltpu.VMEM(LOCAL, jnp.bfloat16),
            pltpu.VMEM((16, LEVELS * HALF_LAT * HALF_LON, 128), jnp.float32),
            pltpu.SemaphoreType.DMA((1,)),
        ],
        compiler_params=pltpu.CompilerParams(vmem_limit_bytes=32 * 2**20),
        cost_estimate=pl.CostEstimate(flops=0, bytes_accessed=900000, transcendentals=0),
        name="unpack",
    )(place, *quarters, cotangent.transpose(1, 2, 0, 3))
    return local.transpose(2, 0, 1, 3)


def weights_kernel(qkv_weight, proj_weight, qkv_held, proj_held, semaphores):
    for copy in fetched((qkv_weight, proj_weight), (qkv_held, proj_held), semaphores):
        copy.wait()


def near_weights(qkv_weight, proj_weight):
    return pl.pallas_call(
        weights_kernel,
        out_shape=(rows_of(D, 3 * D), rows_of(D)),
        in_specs=[HBM, HBM],
        out_specs=(VMEM, VMEM),
        scratch_shapes=[pltpu.SemaphoreType.DMA((2,))],
        compiler_params=pltpu.CompilerParams(vmem_limit_bytes=32 * 2**20),
        cost_estimate=pl.CostEstimate(flops=0, bytes_accessed=4 * 2**20, transcendentals=0),
        name="near_weights",
    )(qkv_weight, proj_weight)


def block_kernel(place, *refs):
    quarters, (qkv_weight, proj_weight), (theirs, mine), branch = refs[:4], refs[4:6], refs[6:8], refs[8:12]
    x_held, cot_held, normed, attended, qkv_grad, qkv, upstream, tiles = refs[12:]
    own_ref, both_ref, lon_ref, lat_ref = quarters
    held = [ref[...].astype(jnp.float32) for ref in (own_ref, lon_ref, lat_ref, both_ref)]
    for kind, target in enumerate((x_held, cot_held)):
        chunks = [
            held[quarter][(2 * kind + window) * QUARTER : (2 * kind + window + 1) * QUARTER]
            for window in range(2)
            for quarter in range(4)
        ]
        target[...] = jnp.concatenate(chunks, axis=0).astype(jnp.bfloat16)
    x = x_held[...].astype(jnp.float32)
    centered = x - jnp.mean(x, axis=-1, keepdims=True)
    inverse = lax.rsqrt(jnp.mean(centered * centered, axis=-1, keepdims=True) + 1e-05)
    normed[...] = (centered * inverse).astype(jnp.bfloat16)

    for step in range(3 * D // 256):
        cols = slice(step * 256, (step + 1) * 256)
        gain = HEAD_DIM ** (-0.5) if step < D // 256 else 1.0
        qkv[:, cols] = (dot(normed[...], qkv_weight[:, cols], 1, 0) * gain).astype(jnp.bfloat16)
    for step in range(D // 256):
        cols = slice(step * 256, (step + 1) * 256)
        upstream[:, cols] = dot(cot_held[...], proj_weight[cols, :], 1, 1).astype(jnp.bfloat16)

    head_of = lax.broadcasted_iota(jnp.int32, (WINDOW, GROUP * HEAD_DIM), 1) // HEAD_DIM
    zero = jnp.zeros((WINDOW, GROUP * HEAD_DIM), jnp.bfloat16)

    def apart(slab):
        return jnp.concatenate([jnp.where(head_of == head, slab, zero) for head in range(GROUP)], axis=0)

    def together(tall):
        merged = tall[:WINDOW]
        for head in range(1, GROUP):
            merged = jnp.where(head_of == head, tall[head * WINDOW : (head + 1) * WINDOW], merged)
        return merged.astype(jnp.bfloat16)

    for window in range(2):
        rows = slice(window * WINDOW, (window + 1) * WINDOW)
        shape = (WINDOW, GROUP * WINDOW)
        key_label = token_labels(lax.broadcasted_iota(jnp.int32, shape, 0), window, place[1], place[2])
        query_label = token_labels(lax.broadcasted_iota(jnp.int32, shape, 1) % WINDOW, window, place[1], place[2])
        bias = jnp.where(key_label == query_label, 0.0, -1000000000.0)
        for group in range(HEADS // GROUP):
            cols = [slice(part * D + group * GROUP * HEAD_DIM, part * D + (group + 1) * GROUP * HEAD_DIM) for part in range(3)]
            query, keys, values = (qkv[rows, at] for at in cols)
            query, grad = apart(query), apart(upstream[rows, cols[0]])
            scores = dot(keys, query, 1, 1) + bias
            expo = jnp.exp(scores - jnp.max(scores, axis=0, keepdims=True))
            probs = expo * (1.0 / jnp.sum(expo, axis=0, keepdims=True))
            low = probs.astype(jnp.bfloat16)
            prob_grad = dot(values, grad, 1, 1)
            inner = jnp.sum(probs * prob_grad, axis=0, keepdims=True)
            score_grad = (probs * (prob_grad - inner)).astype(jnp.bfloat16)
            attended[rows, cols[0]] = together(dot(low, values, 0, 0))
            qkv_grad[rows, cols[0]] = together(dot(score_grad, keys, 0, 0) * HEAD_DIM ** (-0.5))
            qkv_grad[rows, cols[1]] = dot(score_grad, query, 1, 0).astype(jnp.bfloat16)
            qkv_grad[rows, cols[2]] = dot(low, grad, 1, 0).astype(jnp.bfloat16)

    def put(step, grads):
        grads = grads.astype(jnp.bfloat16)
        for half in range(2):
            rows = grads[half * (D // 2) : (half + 1) * (D // 2)]
            for part in range(2):
                tiles[half, :, 2 * step + part] = rows[:, 128 * part : 128 * part + 128].reshape(D // 32, 16, 128)

    tall = normed[...].T
    for step in range(3 * D // 256):
        put(step, dot(tall, qkv_grad[:, step * 256 : (step + 1) * 256], 1, 0))
    tall = attended[...].T
    for step in range(D // 256):
        put(step + 3 * D // 256, dot(tall, cot_held[:, step * 256 : (step + 1) * 256], 1, 0))
    theirs[...] = tiles[1 - place[3]]
    mine[...] = tiles[place[3]]
    normed_grad = dot(qkv_grad[...], qkv_weight[...], 1, 1)
    x = x_held[...].astype(jnp.float32)
    centered = x - jnp.mean(x, axis=-1, keepdims=True)
    inverse = lax.rsqrt(jnp.mean(centered * centered, axis=-1, keepdims=True) + 1e-05)
    xhat = centered * inverse
    average = jnp.mean(normed_grad, axis=-1, keepdims=True)
    product = jnp.mean(normed_grad * xhat, axis=-1, keepdims=True)
    dx = inverse * (normed_grad - average - xhat * product)
    for kind, target in enumerate(branch):
        chunks = [dx[(4 * window + kind) * QUARTER : (4 * window + kind + 1) * QUARTER] for window in range(2)]
        target[...] = jnp.concatenate(chunks, axis=0).astype(jnp.bfloat16)


HALF_TILES = jax.ShapeDtypeStruct((D // 32, 4 * D // 128, 16, 128), jnp.bfloat16)


def rows_of(count, width=D):
    return jax.ShapeDtypeStruct((count, width), jnp.bfloat16)


def block(place, quarters, qkv_weight, proj_weight):
    return pl.pallas_call(
        block_kernel,
        out_shape=(HALF_TILES, HALF_TILES) + (rows_of(2 * QUARTER),) * 4,
        in_specs=[SMEM] + [VMEM] * 6,
        out_specs=(VMEM,) * 6,
        scratch_shapes=[
            pltpu.VMEM((TOKENS, D), jnp.bfloat16),
            pltpu.VMEM((TOKENS, D), jnp.bfloat16),
            pltpu.VMEM((TOKENS, D), jnp.bfloat16),
            pltpu.VMEM((TOKENS, D), jnp.bfloat16),
            pltpu.VMEM((TOKENS, 3 * D), jnp.bfloat16),
            pltpu.VMEM((TOKENS, 3 * D), jnp.bfloat16),
            pltpu.VMEM((TOKENS, D), jnp.bfloat16),
            pltpu.VMEM((2,) + HALF_TILES.shape, jnp.bfloat16),
        ],
        compiler_params=pltpu.CompilerParams(vmem_limit_bytes=48 * 2**20),
        cost_estimate=pl.CostEstimate(flops=2 * 10**9, bytes_accessed=6 * 10**6, transcendentals=6 * 10**5),
        name="block",
    )(place, *quarters, qkv_weight, proj_weight)


def added(arrived):
    total = arrived[0].astype(jnp.float32)
    for part in range(1, arrived.shape[0]):
        total = total + arrived[part].astype(jnp.float32)
    return total


def device_groups(members):
    tall, wide = lax.axis_size("y_hi"), lax.axis_size("x")
    cores, y_los = lax.axis_size("core"), lax.axis_size("y_lo")

    def index(z, y, x, core):
        return (((z * tall + y // y_los) * cores + core) * wide + x) * y_los + y % y_los

    return [[index(*at, core) for at in group] for core in range(cores) for group in members(core)]


def chips():
    return lax.axis_size("z"), lax.axis_size("y_hi") * lax.axis_size("y_lo"), lax.axis_size("x")


def near_groups():
    def along(size, core):
        if size == 1:
            return [[0]]
        return [[(2 * at + 2 * core) % size, 2 * at + 1] for at in range(size // 2)]

    def members(core):
        zs, ys, xs = (along(size, core) for size in chips())
        return [[(z, y, x) for z in za for y in ya for x in xa] for za in zs for ya in ys for xa in xs]

    return device_groups(members)


def strided(size):
    step = min(size, 2)
    return [list(range(parity, size, step)) for parity in range(step)]


def middle_groups():
    def members(core):
        z_size, y_size, x_size = chips()
        xs = strided(x_size)
        if core == 0:
            return [[(z, y, x) for x in xa for z in za] for xa in xs for za in strided(z_size) for y in range(y_size)]
        return [[(z, y, x) for x in xa for y in ya] for xa in xs for ya in strided(y_size) for z in range(z_size)]

    return device_groups(members)


def far_groups():
    def members(core):
        z_size, y_size, x_size = chips()
        if core == 0:
            return [[(z, y, x) for y in ya] for ya in strided(y_size) for z in range(z_size) for x in range(x_size)]
        return [[(z, y, x) for z in za] for za in strided(z_size) for y in range(y_size) for x in range(x_size)]

    return device_groups(members)


def swapped(value):
    at = [(z, y, x) for z, y, x in itertools.product(*(range(size) for size in chips()))]
    first, second = device_groups(lambda core: [at])
    return lax.ppermute(value, ALL, [*zip(first, second), *zip(second, first)])


def all_to_all(split, groups):
    return lax.all_to_all(split, ALL, 0, 0, axis_index_groups=groups)


def scattered_sum(tiles, groups):
    count = len(groups[0])
    split = tiles.reshape((count, tiles.shape[0] // count) + tiles.shape[1:])
    return added(all_to_all(split, groups)).astype(jnp.bfloat16)


def exchanged(tiles, groups):
    return all_to_all(jnp.broadcast_to(tiles[None], (len(groups[0]),) + tiles.shape), groups)


def gathered(tiles, groups):
    return exchanged(tiles, groups).reshape((-1,) + tiles.shape[1:])


def untile_kernel(other, place, tiles, *refs):
    qkv_out, proj_out, qkv_held, proj_held, semaphores = refs[-5:]
    first = (1 - place[3] if other else place[3]) * (D // 2)
    chunk = D // 2 // CHUNKS
    copies = []
    for at in range(CHUNKS):
        rows = slice(at * chunk, (at + 1) * chunk)
        for col in range(4 * D // 128):
            strip = tiles[at * chunk // 16 : (at + 1) * chunk // 16, col].reshape(chunk, 128)
            if col < 3 * D // 128:
                qkv_held[rows, 128 * col : 128 * col + 128] = strip
            else:
                proj_held[rows, 128 * col - 3 * D : 128 * col - 3 * D + 128] = strip
        target = pl.ds(pl.multiple_of(first + at * chunk, chunk), chunk)
        for kind, (held, out) in enumerate(((qkv_held, qkv_out), (proj_held, proj_out))):
            copies.append(pltpu.make_async_copy(held.at[rows], out.at[target], semaphores.at[2 * at + kind]))
            copies[-1].start()
    for copy in copies:
        copy.wait()


CHUNKS = 4


def untile(place, tiles, other, so_far=()):
    return pl.pallas_call(
        functools.partial(untile_kernel, other),
        in_specs=[SMEM, VMEM] + [HBM] * len(so_far),
        out_specs=(HBM, HBM),
        out_shape=(rows_of(D, 3 * D), rows_of(D)),
        scratch_shapes=[
            pltpu.VMEM((D // 2, 3 * D), jnp.bfloat16),
            pltpu.VMEM((D // 2, D), jnp.bfloat16),
            pltpu.SemaphoreType.DMA((2 * CHUNKS,)),
        ],
        input_output_aliases={2: 0, 3: 1} if so_far else {},
        compiler_params=pltpu.CompilerParams(vmem_limit_bytes=32 * 2**20),
        cost_estimate=pl.CostEstimate(flops=0, bytes_accessed=2 * 2**20, transcendentals=0),
        name="untile_other" if other else "untile_own",
    )(place, tiles, *so_far)


def per_device(activations, cotangent, qkv_weight, proj_weight):
    lat, lon = lax.axis_index(LAT), lax.axis_index(LON)
    odd = lat % 2 == 1
    lon_edge = jnp.where(odd, lon == lax.axis_size(LON) - 1, lon == 0)
    place = jnp.stack([odd, lat == 0, lon_edge, lax.axis_index("core") == 1]).astype(jnp.int32)
    own, lon, lat, both = pack(place, activations, cotangent)
    own, qkv_weight, proj_weight = lax.optimization_barrier((own, qkv_weight, proj_weight))
    both, lon, lat = moved(both, 3, False), moved(lon, 1, False), moved(lat, 2, False)
    qkv_weight, proj_weight = near_weights(qkv_weight, proj_weight)
    theirs, mine, own, lon, lat, both = block(place, (own, both, lon, lat), qkv_weight, proj_weight)

    near, middle, far = near_groups(), middle_groups(), far_groups()
    lon = moved(lon, 1, True)
    tiles = (mine.astype(jnp.float32) + swapped(theirs).astype(jnp.float32)).astype(jnp.bfloat16)
    tiles, lat, both = lax.optimization_barrier((tiles.reshape(-1, 16, 128), lat, both))
    tiles, lon, lat = lax.optimization_barrier((scattered_sum(tiles, near), lon, moved(lat, 2, True)))
    tiles = scattered_sum(tiles, middle)
    factor = (LEVELS * ROWS * COLS * lax.axis_size(ALL)) ** (-0.5)
    tiles = (added(exchanged(tiles, far)) * factor).astype(jnp.bfloat16)
    tiles, both = lax.optimization_barrier((gathered(tiles, middle), both))
    tiles, both = lax.optimization_barrier((gathered(tiles, near), moved(both, 3, True)))
    tiles = tiles.reshape(HALF_TILES.shape)
    arrived = swapped(tiles)
    grads = untile(place, tiles, False)
    input_grad = unpack(place, cotangent, own, lon, lat, both)
    arrived, grads, input_grad = lax.optimization_barrier((arrived, grads, input_grad))
    qkv_weight_grad, proj_weight_grad = untile(place, arrived, True, grads)
    return (input_grad, qkv_weight_grad, proj_weight_grad)


def over(physical):
    spec = P(None, LAT, LON, None)
    return jax.shard_map(
        per_device,
        mesh=physical,
        in_specs=(spec, spec, P(), P()),
        out_specs=(spec, P(), P()),
        check_vma=False,
    )


def solution(mesh):
    return over(Mesh(mesh.devices.reshape(8, 4, 2, 4, 2), ALL))
```

```python
import functools
import itertools

import jax
import jax.numpy as jnp
from jax import lax
from jax.experimental import pallas as pl
from jax.experimental.pallas import tpu as pltpu
from jax.sharding import Mesh, PartitionSpec as P

D = 512
HEADS = 8
HEAD_DIM = 64
GROUP = 4
LEVELS = 4
HALF_LAT = 3
HALF_LON = 6
ROWS = 6
COLS = 12
PAIRS = ((1, 2), (3, 0))
QUARTER = 2 * HALF_LAT * HALF_LON
WINDOW = 4 * QUARTER
TOKENS = 2 * WINDOW

LON = ("z", "y_hi", "core")
LAT = ("x", "y_lo")
ALL = LON + LAT


def dot(a, b, a_dim, b_dim):
    return lax.dot_general(a, b, (((a_dim,), (b_dim,)), ((), ())), preferred_element_type=jnp.float32)


def owner_of(kind, lat, lon):
    lat = lat + kind // 2
    return lat, lon + kind % 2 * (-1 if lat % 2 == 1 else 1)


def moved(value, kind, back):
    lons, lats = lax.axis_size(LON), lax.axis_size(LAT)
    pairs = []
    for lon in range(lons):
        for lat in range(lats):
            to_lat, to_lon = owner_of(kind, lat, lon)
            pair = (lon * lats + lat, to_lon % lons * lats + to_lat % lats)
            pairs.append(pair[::-1] if back else pair)
    return lax.ppermute(value, ALL, pairs)


def token_labels(token, window, lat_edge, lon_edge):
    quarter = token // QUARTER
    level = token % QUARTER // (QUARTER // 2)
    return level * window + 2 * lat_edge * (quarter // 2) + 4 * lon_edge * (quarter % 2)


def fetched(sources, targets, semaphores):
    copies = [
        pltpu.make_async_copy(source, target, semaphores.at[at])
        for at, (source, target) in enumerate(zip(sources, targets))
    ]
    for copy in copies:
        copy.start()
    return copies


def pack_kernel(place, act_ref, cot_ref, own, lon, lat, both, lines):
    cuts = {(row_half, col_half): [] for row_half in range(2) for col_half in range(2)}
    for kind, ref in enumerate((act_ref, cot_ref)):
        for row_half, col_half in cuts:
            held = [lines.at[4 * (4 * kind + 2 * row_half + col_half) + part] for part in range(4)]
            for row in range(HALF_LAT):
                for col in range(HALF_LON):
                    token = ref[row_half * HALF_LAT + row, col_half * HALF_LON + col].astype(jnp.float32)
                    at = pl.ds(LEVELS * (row * HALF_LON + col), LEVELS)
                    for part in range(4):
                        held[part][at] = token[:, 128 * part : 128 * part + 128]
            for pair in PAIRS:
                for level in pair:
                    at = pl.ds(level, HALF_LAT * HALF_LON, stride=LEVELS)
                    cuts[row_half, col_half].append(jnp.concatenate([part[at] for part in held], axis=1))
    whole = {at: jnp.concatenate(pieces, axis=0).astype(jnp.bfloat16) for at, pieces in cuts.items()}

    def put(parity):
        own[...] = whole[0, parity]
        lon[...] = whole[0, 1 - parity]
        lat[...] = whole[1, 1 - parity]
        both[...] = whole[1, parity]

    for parity in range(2):
        pl.when(place[0] == parity)(lambda parity=parity: put(parity))


SMEM = pl.BlockSpec(memory_space=pltpu.SMEM)
VMEM = pl.BlockSpec(memory_space=pltpu.VMEM)
HBM = pl.BlockSpec(memory_space=pltpu.HBM)
LOCAL = (ROWS, COLS, LEVELS, D)


def pack(place, activations, cotangent):
    return pl.pallas_call(
        pack_kernel,
        out_shape=(jax.ShapeDtypeStruct((4 * QUARTER, D), jnp.bfloat16),) * 4,
        in_specs=[SMEM, VMEM, VMEM],
        out_specs=(VMEM,) * 4,
        scratch_shapes=[
            pltpu.VMEM((32, LEVELS * HALF_LAT * HALF_LON, 128), jnp.float32),
        ],
        compiler_params=pltpu.CompilerParams(vmem_limit_bytes=32 * 2**20),
        cost_estimate=pl.CostEstimate(flops=0, bytes_accessed=1200000, transcendentals=0),
        name="pack",
    )(place, activations.transpose(1, 2, 0, 3), cotangent.transpose(1, 2, 0, 3))


def unpack_kernel(place, own, lon, lat, both, cot, out, cot_ref, lines, semaphores):
    (copy,) = fetched((cot,), (cot_ref,), semaphores)
    own, lon, lat, both = (ref[...].astype(jnp.float32) for ref in (own, lon, lat, both))
    even = place[0] == 0
    whole = {
        (0, 0): jnp.where(even, own, lon),
        (0, 1): jnp.where(even, lon, own),
        (1, 0): jnp.where(even, both, lat),
        (1, 1): jnp.where(even, lat, both),
    }
    copy.wait()
    count = HALF_LAT * HALF_LON
    for (row_half, col_half), quarter in whole.items():
        held = [lines.at[4 * (2 * row_half + col_half) + part] for part in range(4)]
        for at, level in enumerate(PAIRS[0] + PAIRS[1]):
            for part in range(4):
                cut = quarter[at * count : (at + 1) * count, 128 * part : 128 * part + 128]
                held[part][pl.ds(level, count, stride=LEVELS)] = cut
        for row in range(HALF_LAT):
            for col in range(HALF_LON):
                at = pl.ds(LEVELS * (row * HALF_LON + col), LEVELS)
                token = jnp.concatenate([part[at] for part in held], axis=1)
                place_of = (row_half * HALF_LAT + row, col_half * HALF_LON + col)
                out[place_of] = (cot_ref[place_of].astype(jnp.float32) + token).astype(jnp.bfloat16)


def unpack(place, cotangent, *quarters):
    local = pl.pallas_call(
        unpack_kernel,
        out_shape=jax.ShapeDtypeStruct(LOCAL, jnp.bfloat16),
        in_specs=[SMEM] + [VMEM] * 4 + [HBM],
        out_specs=VMEM,
        scratch_shapes=[
            pltpu.VMEM(LOCAL, jnp.bfloat16),
            pltpu.VMEM((16, LEVELS * HALF_LAT * HALF_LON, 128), jnp.float32),
            pltpu.SemaphoreType.DMA((1,)),
        ],
        compiler_params=pltpu.CompilerParams(vmem_limit_bytes=32 * 2**20),
        cost_estimate=pl.CostEstimate(flops=0, bytes_accessed=900000, transcendentals=0),
        name="unpack",
    )(place, *quarters, cotangent.transpose(1, 2, 0, 3))
    return local.transpose(2, 0, 1, 3)


def weights_kernel(qkv_weight, proj_weight, qkv_held, proj_held, semaphores):
    for copy in fetched((qkv_weight, proj_weight), (qkv_held, proj_held), semaphores):
        copy.wait()


def near_weights(qkv_weight, proj_weight):
    return pl.pallas_call(
        weights_kernel,
        out_shape=(rows_of(D, 3 * D), rows_of(D)),
        in_specs=[HBM, HBM],
        out_specs=(VMEM, VMEM),
        scratch_shapes=[pltpu.SemaphoreType.DMA((2,))],
        compiler_params=pltpu.CompilerParams(vmem_limit_bytes=32 * 2**20),
        cost_estimate=pl.CostEstimate(flops=0, bytes_accessed=4 * 2**20, transcendentals=0),
        name="near_weights",
    )(qkv_weight, proj_weight)


def block_kernel(place, *refs):
    quarters, (qkv_weight, proj_weight), (theirs, mine, x_held, qkv_grad) = refs[:4], refs[4:6], refs[6:10]
    cot_held, normed, attended, qkv, upstream, tiles = refs[10:]
    own_ref, both_ref, lon_ref, lat_ref = quarters
    held = [ref[...].astype(jnp.float32) for ref in (own_ref, lon_ref, lat_ref, both_ref)]
    for kind, target in enumerate((x_held, cot_held)):
        chunks = [
            held[quarter][(2 * kind + window) * QUARTER : (2 * kind + window + 1) * QUARTER]
            for window in range(2)
            for quarter in range(4)
        ]
        target[...] = jnp.concatenate(chunks, axis=0).astype(jnp.bfloat16)
    x = x_held[...].astype(jnp.float32)
    centered = x - jnp.mean(x, axis=-1, keepdims=True)
    inverse = lax.rsqrt(jnp.mean(centered * centered, axis=-1, keepdims=True) + 1e-05)
    normed[...] = (centered * inverse).astype(jnp.bfloat16)

    for step in range(3 * D // 256):
        cols = slice(step * 256, (step + 1) * 256)
        gain = HEAD_DIM ** (-0.5) if step < D // 256 else 1.0
        qkv[:, cols] = (dot(normed[...], qkv_weight[:, cols], 1, 0) * gain).astype(jnp.bfloat16)
    for step in range(D // 256):
        cols = slice(step * 256, (step + 1) * 256)
        upstream[:, cols] = dot(cot_held[...], proj_weight[cols, :], 1, 1).astype(jnp.bfloat16)

    head_of = lax.broadcasted_iota(jnp.int32, (WINDOW, GROUP * HEAD_DIM), 1) // HEAD_DIM
    zero = jnp.zeros((WINDOW, GROUP * HEAD_DIM), jnp.bfloat16)

    def apart(slab):
        return jnp.concatenate([jnp.where(head_of == head, slab, zero) for head in range(GROUP)], axis=0)

    def together(tall):
        merged = tall[:WINDOW]
        for head in range(1, GROUP):
            merged = jnp.where(head_of == head, tall[head * WINDOW : (head + 1) * WINDOW], merged)
        return merged.astype(jnp.bfloat16)

    for window in range(2):
        rows = slice(window * WINDOW, (window + 1) * WINDOW)
        shape = (WINDOW, GROUP * WINDOW)
        key_label = token_labels(lax.broadcasted_iota(jnp.int32, shape, 0), window, place[1], place[2])
        query_label = token_labels(lax.broadcasted_iota(jnp.int32, shape, 1) % WINDOW, window, place[1], place[2])
        bias = jnp.where(key_label == query_label, 0.0, -1000000000.0)
        for group in range(HEADS // GROUP):
            cols = [slice(part * D + group * GROUP * HEAD_DIM, part * D + (group + 1) * GROUP * HEAD_DIM) for part in range(3)]
            query, keys, values = (qkv[rows, at] for at in cols)
            query, grad = apart(query), apart(upstream[rows, cols[0]])
            scores = dot(keys, query, 1, 1) + bias
            expo = jnp.exp(scores - jnp.max(scores, axis=0, keepdims=True))
            probs = expo * (1.0 / jnp.sum(expo, axis=0, keepdims=True))
            low = probs.astype(jnp.bfloat16)
            prob_grad = dot(values, grad, 1, 1)
            inner = jnp.sum(probs * prob_grad, axis=0, keepdims=True)
            score_grad = (probs * (prob_grad - inner)).astype(jnp.bfloat16)
            attended[rows, cols[0]] = together(dot(low, values, 0, 0))
            qkv_grad[rows, cols[0]] = together(dot(score_grad, keys, 0, 0) * HEAD_DIM ** (-0.5))
            qkv_grad[rows, cols[1]] = dot(score_grad, query, 1, 0).astype(jnp.bfloat16)
            qkv_grad[rows, cols[2]] = dot(low, grad, 1, 0).astype(jnp.bfloat16)

    def put(step, grads):
        grads = grads.astype(jnp.bfloat16)
        for half in range(2):
            rows = grads[half * (D // 2) : (half + 1) * (D // 2)]
            for part in range(2):
                tiles[half, :, 2 * step + part] = rows[:, 128 * part : 128 * part + 128].reshape(D // 32, 16, 128)

    tall = normed[...].T
    for step in range(3 * D // 256):
        put(step, dot(tall, qkv_grad[:, step * 256 : (step + 1) * 256], 1, 0))
    tall = attended[...].T
    for step in range(D // 256):
        put(step + 3 * D // 256, dot(tall, cot_held[:, step * 256 : (step + 1) * 256], 1, 0))
    theirs[...] = tiles[1 - place[3]]
    mine[...] = tiles[place[3]]


def rest_kernel(x_held, qkv_grad, qkv_weight, *branch):
    normed_grad = dot(qkv_grad[...], qkv_weight[...], 1, 1)
    x = x_held[...].astype(jnp.float32)
    centered = x - jnp.mean(x, axis=-1, keepdims=True)
    inverse = lax.rsqrt(jnp.mean(centered * centered, axis=-1, keepdims=True) + 1e-05)
    xhat = centered * inverse
    average = jnp.mean(normed_grad, axis=-1, keepdims=True)
    product = jnp.mean(normed_grad * xhat, axis=-1, keepdims=True)
    dx = inverse * (normed_grad - average - xhat * product)
    for kind, target in enumerate(branch):
        chunks = [dx[(4 * window + kind) * QUARTER : (4 * window + kind + 1) * QUARTER] for window in range(2)]
        target[...] = jnp.concatenate(chunks, axis=0).astype(jnp.bfloat16)


HALF_TILES = jax.ShapeDtypeStruct((D // 32, 4 * D // 128, 16, 128), jnp.bfloat16)


def rows_of(count, width=D):
    return jax.ShapeDtypeStruct((count, width), jnp.bfloat16)


def block(place, quarters, qkv_weight, proj_weight):
    return pl.pallas_call(
        block_kernel,
        out_shape=(HALF_TILES, HALF_TILES, rows_of(TOKENS), rows_of(TOKENS, 3 * D)),
        in_specs=[SMEM] + [VMEM] * 6,
        out_specs=(VMEM,) * 4,
        scratch_shapes=[
            pltpu.VMEM((TOKENS, D), jnp.bfloat16),
            pltpu.VMEM((TOKENS, D), jnp.bfloat16),
            pltpu.VMEM((TOKENS, D), jnp.bfloat16),
            pltpu.VMEM((TOKENS, 3 * D), jnp.bfloat16),
            pltpu.VMEM((TOKENS, D), jnp.bfloat16),
            pltpu.VMEM((2,) + HALF_TILES.shape, jnp.bfloat16),
        ],
        compiler_params=pltpu.CompilerParams(vmem_limit_bytes=48 * 2**20),
        cost_estimate=pl.CostEstimate(flops=2 * 10**9, bytes_accessed=6 * 10**6, transcendentals=6 * 10**5),
        name="block",
    )(place, *quarters, qkv_weight, proj_weight)


def rest(x_held, qkv_grad, qkv_weight):
    return pl.pallas_call(
        rest_kernel,
        out_shape=(rows_of(2 * QUARTER),) * 4,
        in_specs=[VMEM] * 3,
        out_specs=(VMEM,) * 4,
        compiler_params=pltpu.CompilerParams(vmem_limit_bytes=48 * 2**20),
        cost_estimate=pl.CostEstimate(flops=5 * 10**8, bytes_accessed=3 * 10**6, transcendentals=300),
        name="rest",
    )(x_held, qkv_grad, qkv_weight)


def added(arrived):
    total = arrived[0].astype(jnp.float32)
    for part in range(1, arrived.shape[0]):
        total = total + arrived[part].astype(jnp.float32)
    return total


def device_groups(members):
    tall, wide = lax.axis_size("y_hi"), lax.axis_size("x")
    cores, y_los = lax.axis_size("core"), lax.axis_size("y_lo")

    def index(z, y, x, core):
        return (((z * tall + y // y_los) * cores + core) * wide + x) * y_los + y % y_los

    return [[index(*at, core) for at in group] for core in range(cores) for group in members(core)]


def chips():
    return lax.axis_size("z"), lax.axis_size("y_hi") * lax.axis_size("y_lo"), lax.axis_size("x")


def near_groups():
    def along(size, core):
        if size == 1:
            return [[0]]
        return [[(2 * at + 2 * core) % size, 2 * at + 1] for at in range(size // 2)]

    def members(core):
        zs, ys, xs = (along(size, core) for size in chips())
        return [[(z, y, x) for z in za for y in ya for x in xa] for za in zs for ya in ys for xa in xs]

    return device_groups(members)


def strided(size):
    step = min(size, 2)
    return [list(range(parity, size, step)) for parity in range(step)]


def middle_groups():
    def members(core):
        z_size, y_size, x_size = chips()
        xs = strided(x_size)
        if core == 0:
            return [[(z, y, x) for x in xa for z in za] for xa in xs for za in strided(z_size) for y in range(y_size)]
        return [[(z, y, x) for x in xa for y in ya] for xa in xs for ya in strided(y_size) for z in range(z_size)]

    return device_groups(members)


def far_groups():
    def members(core):
        z_size, y_size, x_size = chips()
        if core == 0:
            return [[(z, y, x) for y in ya] for ya in strided(y_size) for z in range(z_size) for x in range(x_size)]
        return [[(z, y, x) for z in za] for za in strided(z_size) for y in range(y_size) for x in range(x_size)]

    return device_groups(members)


def swapped(value):
    at = [(z, y, x) for z, y, x in itertools.product(*(range(size) for size in chips()))]
    first, second = device_groups(lambda core: [at])
    return lax.ppermute(value, ALL, [*zip(first, second), *zip(second, first)])


def all_to_all(split, groups):
    return lax.all_to_all(split, ALL, 0, 0, axis_index_groups=groups)


def scattered_sum(tiles, groups):
    count = len(groups[0])
    split = tiles.reshape((count, tiles.shape[0] // count) + tiles.shape[1:])
    return added(all_to_all(split, groups)).astype(jnp.bfloat16)


def exchanged(tiles, groups):
    return all_to_all(jnp.broadcast_to(tiles[None], (len(groups[0]),) + tiles.shape), groups)


def gathered(tiles, groups):
    return exchanged(tiles, groups).reshape((-1,) + tiles.shape[1:])


def untile_kernel(other, place, tiles, *refs):
    qkv_out, proj_out, qkv_held, proj_held, semaphores = refs[-5:]
    first = (1 - place[3] if other else place[3]) * (D // 2)
    chunk = D // 2 // CHUNKS
    copies = []
    for at in range(CHUNKS):
        rows = slice(at * chunk, (at + 1) * chunk)
        for col in range(4 * D // 128):
            strip = tiles[at * chunk // 16 : (at + 1) * chunk // 16, col].reshape(chunk, 128)
            if col < 3 * D // 128:
                qkv_held[rows, 128 * col : 128 * col + 128] = strip
            else:
                proj_held[rows, 128 * col - 3 * D : 128 * col - 3 * D + 128] = strip
        target = pl.ds(pl.multiple_of(first + at * chunk, chunk), chunk)
        for kind, (held, out) in enumerate(((qkv_held, qkv_out), (proj_held, proj_out))):
            copies.append(pltpu.make_async_copy(held.at[rows], out.at[target], semaphores.at[2 * at + kind]))
            copies[-1].start()
    for copy in copies:
        copy.wait()


CHUNKS = 4


def untile(place, tiles, other, so_far=()):
    return pl.pallas_call(
        functools.partial(untile_kernel, other),
        in_specs=[SMEM, VMEM] + [HBM] * len(so_far),
        out_specs=(HBM, HBM),
        out_shape=(rows_of(D, 3 * D), rows_of(D)),
        scratch_shapes=[
            pltpu.VMEM((D // 2, 3 * D), jnp.bfloat16),
            pltpu.VMEM((D // 2, D), jnp.bfloat16),
            pltpu.SemaphoreType.DMA((2 * CHUNKS,)),
        ],
        input_output_aliases={2: 0, 3: 1} if so_far else {},
        compiler_params=pltpu.CompilerParams(vmem_limit_bytes=32 * 2**20),
        cost_estimate=pl.CostEstimate(flops=0, bytes_accessed=2 * 2**20, transcendentals=0),
        name="untile_other" if other else "untile_own",
    )(place, tiles, *so_far)


def per_device(activations, cotangent, qkv_weight, proj_weight):
    lat, lon = lax.axis_index(LAT), lax.axis_index(LON)
    odd = lat % 2 == 1
    lon_edge = jnp.where(odd, lon == lax.axis_size(LON) - 1, lon == 0)
    place = jnp.stack([odd, lat == 0, lon_edge, lax.axis_index("core") == 1]).astype(jnp.int32)
    own, lon, lat, both = pack(place, activations, cotangent)
    own, qkv_weight, proj_weight = lax.optimization_barrier((own, qkv_weight, proj_weight))
    both, lon, lat = moved(both, 3, False), moved(lon, 1, False), moved(lat, 2, False)
    qkv_weight, proj_weight = near_weights(qkv_weight, proj_weight)
    theirs, mine, x_held, qkv_grad = block(place, (own, both, lon, lat), qkv_weight, proj_weight)
    own, lon, lat, both = rest(x_held, qkv_grad, qkv_weight)

    near, middle, far = near_groups(), middle_groups(), far_groups()
    lon = moved(lon, 1, True)
    tiles = (mine.astype(jnp.float32) + swapped(theirs).astype(jnp.float32)).astype(jnp.bfloat16)
    tiles, lat, both = lax.optimization_barrier((tiles.reshape(-1, 16, 128), lat, both))
    tiles, lon, lat = lax.optimization_barrier((scattered_sum(tiles, near), lon, moved(lat, 2, True)))
    tiles = scattered_sum(tiles, middle)
    factor = (LEVELS * ROWS * COLS * lax.axis_size(ALL)) ** (-0.5)
    tiles = (added(exchanged(tiles, far)) * factor).astype(jnp.bfloat16)
    tiles, both = lax.optimization_barrier((gathered(tiles, middle), both))
    tiles, both = lax.optimization_barrier((gathered(tiles, near), moved(both, 3, True)))
    tiles = tiles.reshape(HALF_TILES.shape)
    arrived = swapped(tiles)
    grads = untile(place, tiles, False)
    input_grad = unpack(place, cotangent, own, lon, lat, both)
    arrived, grads, input_grad = lax.optimization_barrier((arrived, grads, input_grad))
    qkv_weight_grad, proj_weight_grad = untile(place, arrived, True, grads)
    return (input_grad, qkv_weight_grad, proj_weight_grad)


def over(physical):
    spec = P(None, LAT, LON, None)
    return jax.shard_map(
        per_device,
        mesh=physical,
        in_specs=(spec, spec, P(), P()),
        out_specs=(spec, P(), P()),
        check_vma=False,
    )


def solution(mesh):
    return over(Mesh(mesh.devices.reshape(8, 4, 2, 4, 2), ALL))
```

```python
import itertools

import jax
import jax.numpy as jnp
from jax import lax
from jax.experimental import pallas as pl
from jax.experimental.pallas import tpu as pltpu
from jax.sharding import Mesh, PartitionSpec as P

D = 512
HEADS = 8
HEAD_DIM = 64
GROUP = 4
LEVELS = 4
HALF_LAT = 3
HALF_LON = 6
ROWS = 6
COLS = 12
PAIRS = ((1, 2), (3, 0))
QUARTER = 2 * HALF_LAT * HALF_LON
WINDOW = 4 * QUARTER
TOKENS = 2 * WINDOW

LON = ("z", "y_hi", "core")
LAT = ("x", "y_lo")
ALL = LON + LAT


def dot(a, b, a_dim, b_dim):
    return lax.dot_general(a, b, (((a_dim,), (b_dim,)), ((), ())), preferred_element_type=jnp.float32)


def owner_of(kind, lat, lon):
    lat = lat + kind // 2
    return lat, lon + kind % 2 * (-1 if lat % 2 == 1 else 1)


def moved(value, kind, back):
    lons, lats = lax.axis_size(LON), lax.axis_size(LAT)
    pairs = []
    for lon in range(lons):
        for lat in range(lats):
            to_lat, to_lon = owner_of(kind, lat, lon)
            pair = (lon * lats + lat, to_lon % lons * lats + to_lat % lats)
            pairs.append(pair[::-1] if back else pair)
    return lax.ppermute(value, ALL, pairs)


def token_labels(token, window, lat_edge, lon_edge):
    quarter = token // QUARTER
    level = token % QUARTER // (QUARTER // 2)
    return level * window + 2 * lat_edge * (quarter // 2) + 4 * lon_edge * (quarter % 2)


def fetched(sources, targets, semaphores):
    copies = [
        pltpu.make_async_copy(source, target, semaphores.at[at])
        for at, (source, target) in enumerate(zip(sources, targets))
    ]
    for copy in copies:
        copy.start()
    return copies


def pack_kernel(place, act_ref, cot_ref, own, lon, lat, both, lines):
    cuts = {(row_half, col_half): [] for row_half in range(2) for col_half in range(2)}
    for kind, ref in enumerate((act_ref, cot_ref)):
        for row_half, col_half in cuts:
            held = [lines.at[4 * (4 * kind + 2 * row_half + col_half) + part] for part in range(4)]
            for row in range(HALF_LAT):
                for col in range(HALF_LON):
                    token = ref[row_half * HALF_LAT + row, col_half * HALF_LON + col].astype(jnp.float32)
                    at = pl.ds(LEVELS * (row * HALF_LON + col), LEVELS)
                    for part in range(4):
                        held[part][at] = token[:, 128 * part : 128 * part + 128]
            for pair in PAIRS:
                for level in pair:
                    at = pl.ds(level, HALF_LAT * HALF_LON, stride=LEVELS)
                    cuts[row_half, col_half].append(jnp.concatenate([part[at] for part in held], axis=1))
    whole = {at: jnp.concatenate(pieces, axis=0).astype(jnp.bfloat16) for at, pieces in cuts.items()}

    def put(parity):
        own[...] = whole[0, parity]
        lon[...] = whole[0, 1 - parity]
        lat[...] = whole[1, 1 - parity]
        both[...] = whole[1, parity]

    for parity in range(2):
        pl.when(place[0] == parity)(lambda parity=parity: put(parity))


SMEM = pl.BlockSpec(memory_space=pltpu.SMEM)
VMEM = pl.BlockSpec(memory_space=pltpu.VMEM)
HBM = pl.BlockSpec(memory_space=pltpu.HBM)
LOCAL = (ROWS, COLS, LEVELS, D)


def pack(place, activations, cotangent):
    return pl.pallas_call(
        pack_kernel,
        out_shape=(jax.ShapeDtypeStruct((4 * QUARTER, D), jnp.bfloat16),) * 4,
        in_specs=[SMEM, VMEM, VMEM],
        out_specs=(VMEM,) * 4,
        scratch_shapes=[
            pltpu.VMEM((32, LEVELS * HALF_LAT * HALF_LON, 128), jnp.float32),
        ],
        compiler_params=pltpu.CompilerParams(vmem_limit_bytes=32 * 2**20),
        cost_estimate=pl.CostEstimate(flops=0, bytes_accessed=1200000, transcendentals=0),
        name="pack",
    )(place, activations.transpose(1, 2, 0, 3), cotangent.transpose(1, 2, 0, 3))


def unpack_kernel(place, own, lon, lat, both, cot, out, cot_ref, lines, semaphores):
    (copy,) = fetched((cot,), (cot_ref,), semaphores)
    own, lon, lat, both = (ref[...].astype(jnp.float32) for ref in (own, lon, lat, both))
    even = place[0] == 0
    whole = {
        (0, 0): jnp.where(even, own, lon),
        (0, 1): jnp.where(even, lon, own),
        (1, 0): jnp.where(even, both, lat),
        (1, 1): jnp.where(even, lat, both),
    }
    copy.wait()
    count = HALF_LAT * HALF_LON
    for (row_half, col_half), quarter in whole.items():
        held = [lines.at[4 * (2 * row_half + col_half) + part] for part in range(4)]
        for at, level in enumerate(PAIRS[0] + PAIRS[1]):
            for part in range(4):
                cut = quarter[at * count : (at + 1) * count, 128 * part : 128 * part + 128]
                held[part][pl.ds(level, count, stride=LEVELS)] = cut
        for row in range(HALF_LAT):
            for col in range(HALF_LON):
                at = pl.ds(LEVELS * (row * HALF_LON + col), LEVELS)
                token = jnp.concatenate([part[at] for part in held], axis=1)
                place_of = (row_half * HALF_LAT + row, col_half * HALF_LON + col)
                out[place_of] = (cot_ref[place_of].astype(jnp.float32) + token).astype(jnp.bfloat16)


def unpack(place, cotangent, *quarters):
    local = pl.pallas_call(
        unpack_kernel,
        out_shape=jax.ShapeDtypeStruct(LOCAL, jnp.bfloat16),
        in_specs=[SMEM] + [VMEM] * 4 + [HBM],
        out_specs=VMEM,
        scratch_shapes=[
            pltpu.VMEM(LOCAL, jnp.bfloat16),
            pltpu.VMEM((16, LEVELS * HALF_LAT * HALF_LON, 128), jnp.float32),
            pltpu.SemaphoreType.DMA((1,)),
        ],
        compiler_params=pltpu.CompilerParams(vmem_limit_bytes=32 * 2**20),
        cost_estimate=pl.CostEstimate(flops=0, bytes_accessed=900000, transcendentals=0),
        name="unpack",
    )(place, *quarters, cotangent.transpose(1, 2, 0, 3))
    return local.transpose(2, 0, 1, 3)


def weights_kernel(qkv_weight, proj_weight, qkv_held, proj_held, semaphores):
    for copy in fetched((qkv_weight, proj_weight), (qkv_held, proj_held), semaphores):
        copy.wait()


def near_weights(qkv_weight, proj_weight):
    return pl.pallas_call(
        weights_kernel,
        out_shape=(rows_of(D, 3 * D), rows_of(D)),
        in_specs=[HBM, HBM],
        out_specs=(VMEM, VMEM),
        scratch_shapes=[pltpu.SemaphoreType.DMA((2,))],
        compiler_params=pltpu.CompilerParams(vmem_limit_bytes=32 * 2**20),
        cost_estimate=pl.CostEstimate(flops=0, bytes_accessed=4 * 2**20, transcendentals=0),
        name="near_weights",
    )(qkv_weight, proj_weight)


def block_kernel(place, *refs):
    quarters, (qkv_weight, proj_weight), (theirs, mine, x_held, qkv_grad) = refs[:4], refs[4:6], refs[6:10]
    cot_held, normed, attended, qkv, upstream, tiles = refs[10:]
    own_ref, both_ref, lon_ref, lat_ref = quarters
    held = [ref[...].astype(jnp.float32) for ref in (own_ref, lon_ref, lat_ref, both_ref)]
    for kind, target in enumerate((x_held, cot_held)):
        chunks = [
            held[quarter][(2 * kind + window) * QUARTER : (2 * kind + window + 1) * QUARTER]
            for window in range(2)
            for quarter in range(4)
        ]
        target[...] = jnp.concatenate(chunks, axis=0).astype(jnp.bfloat16)
    x = x_held[...].astype(jnp.float32)
    centered = x - jnp.mean(x, axis=-1, keepdims=True)
    inverse = lax.rsqrt(jnp.mean(centered * centered, axis=-1, keepdims=True) + 1e-05)
    normed[...] = (centered * inverse).astype(jnp.bfloat16)

    for step in range(3 * D // 256):
        cols = slice(step * 256, (step + 1) * 256)
        gain = HEAD_DIM ** (-0.5) if step < D // 256 else 1.0
        qkv[:, cols] = (dot(normed[...], qkv_weight[:, cols], 1, 0) * gain).astype(jnp.bfloat16)
    for step in range(D // 256):
        cols = slice(step * 256, (step + 1) * 256)
        upstream[:, cols] = dot(cot_held[...], proj_weight[cols, :], 1, 1).astype(jnp.bfloat16)

    head_of = lax.broadcasted_iota(jnp.int32, (WINDOW, GROUP * HEAD_DIM), 1) // HEAD_DIM
    zero = jnp.zeros((WINDOW, GROUP * HEAD_DIM), jnp.bfloat16)

    def apart(slab):
        return jnp.concatenate([jnp.where(head_of == head, slab, zero) for head in range(GROUP)], axis=0)

    def together(tall):
        merged = tall[:WINDOW]
        for head in range(1, GROUP):
            merged = jnp.where(head_of == head, tall[head * WINDOW : (head + 1) * WINDOW], merged)
        return merged.astype(jnp.bfloat16)

    for window in range(2):
        rows = slice(window * WINDOW, (window + 1) * WINDOW)
        shape = (WINDOW, GROUP * WINDOW)
        key_label = token_labels(lax.broadcasted_iota(jnp.int32, shape, 0), window, place[1], place[2])
        query_label = token_labels(lax.broadcasted_iota(jnp.int32, shape, 1) % WINDOW, window, place[1], place[2])
        bias = jnp.where(key_label == query_label, 0.0, -1000000000.0)
        for group in range(HEADS // GROUP):
            cols = [slice(part * D + group * GROUP * HEAD_DIM, part * D + (group + 1) * GROUP * HEAD_DIM) for part in range(3)]
            query, keys, values = (qkv[rows, at] for at in cols)
            query, grad = apart(query), apart(upstream[rows, cols[0]])
            scores = dot(keys, query, 1, 1) + bias
            expo = jnp.exp(scores - jnp.max(scores, axis=0, keepdims=True))
            probs = expo * (1.0 / jnp.sum(expo, axis=0, keepdims=True))
            low = probs.astype(jnp.bfloat16)
            prob_grad = dot(values, grad, 1, 1)
            inner = jnp.sum(probs * prob_grad, axis=0, keepdims=True)
            score_grad = (probs * (prob_grad - inner)).astype(jnp.bfloat16)
            attended[rows, cols[0]] = together(dot(low, values, 0, 0))
            qkv_grad[rows, cols[0]] = together(dot(score_grad, keys, 0, 0) * HEAD_DIM ** (-0.5))
            qkv_grad[rows, cols[1]] = dot(score_grad, query, 1, 0).astype(jnp.bfloat16)
            qkv_grad[rows, cols[2]] = dot(low, grad, 1, 0).astype(jnp.bfloat16)

    def put(step, grads):
        grads = grads.astype(jnp.bfloat16)
        for half in range(2):
            rows = grads[half * (D // 2) : (half + 1) * (D // 2)]
            for part in range(2):
                tiles[half, :, 2 * step + part] = rows[:, 128 * part : 128 * part + 128].reshape(D // 32, 16, 128)

    tall = normed[...].T
    for step in range(3 * D // 256):
        put(step, dot(tall, qkv_grad[:, step * 256 : (step + 1) * 256], 1, 0))
    tall = attended[...].T
    for step in range(D // 256):
        put(step + 3 * D // 256, dot(tall, cot_held[:, step * 256 : (step + 1) * 256], 1, 0))
    theirs[...] = tiles[1 - place[3]]
    mine[...] = tiles[place[3]]


def rest_kernel(x_held, qkv_grad, qkv_weight, *branch):
    normed_grad = dot(qkv_grad[...], qkv_weight[...], 1, 1)
    x = x_held[...].astype(jnp.float32)
    centered = x - jnp.mean(x, axis=-1, keepdims=True)
    inverse = lax.rsqrt(jnp.mean(centered * centered, axis=-1, keepdims=True) + 1e-05)
    xhat = centered * inverse
    average = jnp.mean(normed_grad, axis=-1, keepdims=True)
    product = jnp.mean(normed_grad * xhat, axis=-1, keepdims=True)
    dx = inverse * (normed_grad - average - xhat * product)
    for kind, target in enumerate(branch):
        chunks = [dx[(4 * window + kind) * QUARTER : (4 * window + kind + 1) * QUARTER] for window in range(2)]
        target[...] = jnp.concatenate(chunks, axis=0).astype(jnp.bfloat16)


HALF_TILES = jax.ShapeDtypeStruct((D // 32, 4 * D // 128, 16, 128), jnp.bfloat16)


def rows_of(count, width=D):
    return jax.ShapeDtypeStruct((count, width), jnp.bfloat16)


def block(place, quarters, qkv_weight, proj_weight):
    return pl.pallas_call(
        block_kernel,
        out_shape=(HALF_TILES, HALF_TILES, rows_of(TOKENS), rows_of(TOKENS, 3 * D)),
        in_specs=[SMEM] + [VMEM] * 6,
        out_specs=(VMEM,) * 4,
        scratch_shapes=[
            pltpu.VMEM((TOKENS, D), jnp.bfloat16),
            pltpu.VMEM((TOKENS, D), jnp.bfloat16),
            pltpu.VMEM((TOKENS, D), jnp.bfloat16),
            pltpu.VMEM((TOKENS, 3 * D), jnp.bfloat16),
            pltpu.VMEM((TOKENS, D), jnp.bfloat16),
            pltpu.VMEM((2,) + HALF_TILES.shape, jnp.bfloat16),
        ],
        compiler_params=pltpu.CompilerParams(vmem_limit_bytes=48 * 2**20),
        cost_estimate=pl.CostEstimate(flops=2 * 10**9, bytes_accessed=6 * 10**6, transcendentals=6 * 10**5),
        name="block",
    )(place, *quarters, qkv_weight, proj_weight)


def rest(x_held, qkv_grad, qkv_weight):
    return pl.pallas_call(
        rest_kernel,
        out_shape=(rows_of(2 * QUARTER),) * 4,
        in_specs=[VMEM] * 3,
        out_specs=(VMEM,) * 4,
        compiler_params=pltpu.CompilerParams(vmem_limit_bytes=48 * 2**20),
        cost_estimate=pl.CostEstimate(flops=5 * 10**8, bytes_accessed=3 * 10**6, transcendentals=300),
        name="rest",
    )(x_held, qkv_grad, qkv_weight)


def added(arrived):
    total = arrived[0].astype(jnp.float32)
    for part in range(1, arrived.shape[0]):
        total = total + arrived[part].astype(jnp.float32)
    return total


def device_groups(members):
    tall, wide = lax.axis_size("y_hi"), lax.axis_size("x")
    cores, y_los = lax.axis_size("core"), lax.axis_size("y_lo")

    def index(z, y, x, core):
        return (((z * tall + y // y_los) * cores + core) * wide + x) * y_los + y % y_los

    return [[index(*at, core) for at in group] for core in range(cores) for group in members(core)]


def chips():
    return lax.axis_size("z"), lax.axis_size("y_hi") * lax.axis_size("y_lo"), lax.axis_size("x")


def near_groups():
    def along(size, core):
        if size == 1:
            return [[0]]
        return [[(2 * at + 2 * core) % size, 2 * at + 1] for at in range(size // 2)]

    def members(core):
        zs, ys, xs = (along(size, core) for size in chips())
        return [[(z, y, x) for z in za for y in ya for x in xa] for za in zs for ya in ys for xa in xs]

    return device_groups(members)


def strided(size):
    step = min(size, 2)
    return [list(range(parity, size, step)) for parity in range(step)]


def middle_groups():
    def members(core):
        z_size, y_size, x_size = chips()
        xs = strided(x_size)
        if core == 0:
            return [[(z, y, x) for x in xa for z in za] for xa in xs for za in strided(z_size) for y in range(y_size)]
        return [[(z, y, x) for x in xa for y in ya] for xa in xs for ya in strided(y_size) for z in range(z_size)]

    return device_groups(members)


def far_groups():
    def members(core):
        z_size, y_size, x_size = chips()
        if core == 0:
            return [[(z, y, x) for y in ya] for ya in strided(y_size) for z in range(z_size) for x in range(x_size)]
        return [[(z, y, x) for z in za] for za in strided(z_size) for y in range(y_size) for x in range(x_size)]

    return device_groups(members)


def swapped(value):
    at = [(z, y, x) for z, y, x in itertools.product(*(range(size) for size in chips()))]
    first, second = device_groups(lambda core: [at])
    return lax.ppermute(value, ALL, [*zip(first, second), *zip(second, first)])


def all_to_all(split, groups):
    return lax.all_to_all(split, ALL, 0, 0, axis_index_groups=groups)


def scattered_sum(tiles, groups):
    count = len(groups[0])
    split = tiles.reshape((count, tiles.shape[0] // count) + tiles.shape[1:])
    return added(all_to_all(split, groups)).astype(jnp.bfloat16)


def exchanged(tiles, groups):
    return all_to_all(jnp.broadcast_to(tiles[None], (len(groups[0]),) + tiles.shape), groups)


def gathered(tiles, groups):
    return exchanged(tiles, groups).reshape((-1,) + tiles.shape[1:])


def untile_kernel(place, mine, theirs, qkv_out, proj_out):
    for core, tiles in ((place[3], mine), (1 - place[3], theirs)):
        rows = pl.ds(pl.multiple_of(core * (D // 2), D // 2), D // 2)
        for col in range(4 * D // 128):
            strip = tiles[:, col].reshape(D // 2, 128)
            if col < 3 * D // 128:
                qkv_out[rows, 128 * col : 128 * col + 128] = strip
            else:
                proj_out[rows, 128 * col - 3 * D : 128 * col - 3 * D + 128] = strip


def untile(place, mine, theirs):
    return pl.pallas_call(
        untile_kernel,
        in_specs=[SMEM, VMEM, VMEM],
        out_specs=(VMEM, VMEM),
        out_shape=(rows_of(D, 3 * D), rows_of(D)),
        compiler_params=pltpu.CompilerParams(vmem_limit_bytes=32 * 2**20),
        cost_estimate=pl.CostEstimate(flops=0, bytes_accessed=4 * 2**20, transcendentals=0),
        name="untile",
    )(place, mine, theirs)


def per_device(activations, cotangent, qkv_weight, proj_weight):
    lat, lon = lax.axis_index(LAT), lax.axis_index(LON)
    odd = lat % 2 == 1
    lon_edge = jnp.where(odd, lon == lax.axis_size(LON) - 1, lon == 0)
    place = jnp.stack([odd, lat == 0, lon_edge, lax.axis_index("core") == 1]).astype(jnp.int32)
    own, lon, lat, both = pack(place, activations, cotangent)
    own, qkv_weight, proj_weight = lax.optimization_barrier((own, qkv_weight, proj_weight))
    both, lon, lat = moved(both, 3, False), moved(lon, 1, False), moved(lat, 2, False)
    qkv_weight, proj_weight = near_weights(qkv_weight, proj_weight)
    theirs, mine, x_held, qkv_grad = block(place, (own, both, lon, lat), qkv_weight, proj_weight)
    own, lon, lat, both = rest(x_held, qkv_grad, qkv_weight)

    near, middle, far = near_groups(), middle_groups(), far_groups()
    tiles = (mine.astype(jnp.float32) + swapped(theirs).astype(jnp.float32)).astype(jnp.bfloat16)
    tiles, lon, lat, both = lax.optimization_barrier((tiles.reshape(-1, 16, 128), lon, lat, both))
    tiles, lat, lon = lax.optimization_barrier((scattered_sum(tiles, near), moved(lat, 2, True), lon))
    tiles, lon = lax.optimization_barrier((scattered_sum(tiles, middle), moved(lon, 1, True)))
    factor = (LEVELS * ROWS * COLS * lax.axis_size(ALL)) ** (-0.5)
    tiles = (added(exchanged(tiles, far)) * factor).astype(jnp.bfloat16)
    tiles, both = lax.optimization_barrier((gathered(tiles, middle), both))
    tiles, both = lax.optimization_barrier((gathered(tiles, near), moved(both, 3, True)))
    tiles = tiles.reshape(HALF_TILES.shape)
    arrived = swapped(tiles)
    input_grad = unpack(place, cotangent, own, lon, lat, both)
    arrived, input_grad = lax.optimization_barrier((arrived, input_grad))
    qkv_weight_grad, proj_weight_grad = untile(place, tiles, arrived)
    return (input_grad, qkv_weight_grad, proj_weight_grad)


def over(physical):
    spec = P(None, LAT, LON, None)
    return jax.shard_map(
        per_device,
        mesh=physical,
        in_specs=(spec, spec, P(), P()),
        out_specs=(spec, P(), P()),
        check_vma=False,
    )


def solution(mesh):
    return over(Mesh(mesh.devices.reshape(8, 4, 2, 4, 2), ALL))
```

```python
import functools
import itertools

import jax
import jax.numpy as jnp
from jax import lax
from jax.experimental import pallas as pl
from jax.experimental.pallas import tpu as pltpu
from jax.sharding import Mesh, PartitionSpec as P

D = 512
HEADS = 8
HEAD_DIM = 64
GROUP = 4
LEVELS = 4
HALF_LAT = 3
HALF_LON = 6
ROWS = 6
COLS = 12
PAIRS = ((1, 2), (3, 0))
QUARTER = 2 * HALF_LAT * HALF_LON
WINDOW = 4 * QUARTER
TOKENS = 2 * WINDOW

LON = ("z", "y_hi", "core")
LAT = ("x", "y_lo")
ALL = LON + LAT


def dot(a, b, a_dim, b_dim):
    return lax.dot_general(a, b, (((a_dim,), (b_dim,)), ((), ())), preferred_element_type=jnp.float32)


def owner_of(kind, lat, lon):
    lat = lat + kind // 2
    return lat, lon + kind % 2 * (-1 if lat % 2 == 1 else 1)


def moved(value, kind, back):
    lons, lats = lax.axis_size(LON), lax.axis_size(LAT)
    pairs = []
    for lon in range(lons):
        for lat in range(lats):
            to_lat, to_lon = owner_of(kind, lat, lon)
            pair = (lon * lats + lat, to_lon % lons * lats + to_lat % lats)
            pairs.append(pair[::-1] if back else pair)
    return lax.ppermute(value, ALL, pairs)


def token_labels(token, window, lat_edge, lon_edge):
    quarter = token // QUARTER
    level = token % QUARTER // (QUARTER // 2)
    return level * window + 2 * lat_edge * (quarter // 2) + 4 * lon_edge * (quarter % 2)


def fetched(sources, targets, semaphores):
    copies = [
        pltpu.make_async_copy(source, target, semaphores.at[at])
        for at, (source, target) in enumerate(zip(sources, targets))
    ]
    for copy in copies:
        copy.start()
    return copies


def pack_kernel(place, act_ref, cot_ref, own, lon, lat, both, lines):
    cuts = {(row_half, col_half): [] for row_half in range(2) for col_half in range(2)}
    for kind, ref in enumerate((act_ref, cot_ref)):
        for row_half, col_half in cuts:
            held = [lines.at[4 * (4 * kind + 2 * row_half + col_half) + part] for part in range(4)]
            for row in range(HALF_LAT):
                for col in range(HALF_LON):
                    token = ref[row_half * HALF_LAT + row, col_half * HALF_LON + col].astype(jnp.float32)
                    at = pl.ds(LEVELS * (row * HALF_LON + col), LEVELS)
                    for part in range(4):
                        held[part][at] = token[:, 128 * part : 128 * part + 128]
            for pair in PAIRS:
                for level in pair:
                    at = pl.ds(level, HALF_LAT * HALF_LON, stride=LEVELS)
                    cuts[row_half, col_half].append(jnp.concatenate([part[at] for part in held], axis=1))
    whole = {at: jnp.concatenate(pieces, axis=0).astype(jnp.bfloat16) for at, pieces in cuts.items()}

    def put(parity):
        own[...] = whole[0, parity]
        lon[...] = whole[0, 1 - parity]
        lat[...] = whole[1, 1 - parity]
        both[...] = whole[1, parity]

    for parity in range(2):
        pl.when(place[0] == parity)(lambda parity=parity: put(parity))


SMEM = pl.BlockSpec(memory_space=pltpu.SMEM)
VMEM = pl.BlockSpec(memory_space=pltpu.VMEM)
HBM = pl.BlockSpec(memory_space=pltpu.HBM)
LOCAL = (ROWS, COLS, LEVELS, D)


def pack(place, activations, cotangent):
    return pl.pallas_call(
        pack_kernel,
        out_shape=(jax.ShapeDtypeStruct((4 * QUARTER, D), jnp.bfloat16),) * 4,
        in_specs=[SMEM, VMEM, VMEM],
        out_specs=(VMEM,) * 4,
        scratch_shapes=[
            pltpu.VMEM((32, LEVELS * HALF_LAT * HALF_LON, 128), jnp.float32),
        ],
        compiler_params=pltpu.CompilerParams(vmem_limit_bytes=32 * 2**20),
        cost_estimate=pl.CostEstimate(flops=0, bytes_accessed=1200000, transcendentals=0),
        name="pack",
    )(place, activations.transpose(1, 2, 0, 3), cotangent.transpose(1, 2, 0, 3))


def unpack_kernel(place, own, lon, lat, both, cot, out, cot_ref, lines, semaphores):
    (copy,) = fetched((cot,), (cot_ref,), semaphores)
    own, lon, lat, both = (ref[...].astype(jnp.float32) for ref in (own, lon, lat, both))
    even = place[0] == 0
    whole = {
        (0, 0): jnp.where(even, own, lon),
        (0, 1): jnp.where(even, lon, own),
        (1, 0): jnp.where(even, both, lat),
        (1, 1): jnp.where(even, lat, both),
    }
    copy.wait()
    count = HALF_LAT * HALF_LON
    for (row_half, col_half), quarter in whole.items():
        held = [lines.at[4 * (2 * row_half + col_half) + part] for part in range(4)]
        for at, level in enumerate(PAIRS[0] + PAIRS[1]):
            for part in range(4):
                cut = quarter[at * count : (at + 1) * count, 128 * part : 128 * part + 128]
                held[part][pl.ds(level, count, stride=LEVELS)] = cut
        for row in range(HALF_LAT):
            for col in range(HALF_LON):
                at = pl.ds(LEVELS * (row * HALF_LON + col), LEVELS)
                token = jnp.concatenate([part[at] for part in held], axis=1)
                place_of = (row_half * HALF_LAT + row, col_half * HALF_LON + col)
                out[place_of] = (cot_ref[place_of].astype(jnp.float32) + token).astype(jnp.bfloat16)


def unpack(place, cotangent, *quarters):
    local = pl.pallas_call(
        unpack_kernel,
        out_shape=jax.ShapeDtypeStruct(LOCAL, jnp.bfloat16),
        in_specs=[SMEM] + [VMEM] * 4 + [HBM],
        out_specs=VMEM,
        scratch_shapes=[
            pltpu.VMEM(LOCAL, jnp.bfloat16),
            pltpu.VMEM((16, LEVELS * HALF_LAT * HALF_LON, 128), jnp.float32),
            pltpu.SemaphoreType.DMA((1,)),
        ],
        compiler_params=pltpu.CompilerParams(vmem_limit_bytes=32 * 2**20),
        cost_estimate=pl.CostEstimate(flops=0, bytes_accessed=900000, transcendentals=0),
        name="unpack",
    )(place, *quarters, cotangent.transpose(1, 2, 0, 3))
    return local.transpose(2, 0, 1, 3)


def weights_kernel(qkv_weight, proj_weight, qkv_held, proj_held, semaphores):
    for copy in fetched((qkv_weight, proj_weight), (qkv_held, proj_held), semaphores):
        copy.wait()


def near_weights(qkv_weight, proj_weight):
    return pl.pallas_call(
        weights_kernel,
        out_shape=(rows_of(D, 3 * D), rows_of(D)),
        in_specs=[HBM, HBM],
        out_specs=(VMEM, VMEM),
        scratch_shapes=[pltpu.SemaphoreType.DMA((2,))],
        compiler_params=pltpu.CompilerParams(vmem_limit_bytes=32 * 2**20),
        cost_estimate=pl.CostEstimate(flops=0, bytes_accessed=4 * 2**20, transcendentals=0),
        name="near_weights",
    )(qkv_weight, proj_weight)


def block_kernel(place, *refs):
    quarters, (qkv_weight, proj_weight), (theirs, mine, x_held, qkv_grad) = refs[:4], refs[4:6], refs[6:10]
    cot_held, normed, attended, qkv, upstream, tiles = refs[10:]
    own_ref, both_ref, lon_ref, lat_ref = quarters
    held = [ref[...].astype(jnp.float32) for ref in (own_ref, lon_ref, lat_ref, both_ref)]
    for kind, target in enumerate((x_held, cot_held)):
        chunks = [
            held[quarter][(2 * kind + window) * QUARTER : (2 * kind + window + 1) * QUARTER]
            for window in range(2)
            for quarter in range(4)
        ]
        target[...] = jnp.concatenate(chunks, axis=0).astype(jnp.bfloat16)
    x = x_held[...].astype(jnp.float32)
    centered = x - jnp.mean(x, axis=-1, keepdims=True)
    inverse = lax.rsqrt(jnp.mean(centered * centered, axis=-1, keepdims=True) + 1e-05)
    normed[...] = (centered * inverse).astype(jnp.bfloat16)

    for step in range(3 * D // 256):
        cols = slice(step * 256, (step + 1) * 256)
        gain = HEAD_DIM ** (-0.5) if step < D // 256 else 1.0
        qkv[:, cols] = (dot(normed[...], qkv_weight[:, cols], 1, 0) * gain).astype(jnp.bfloat16)
    for step in range(D // 256):
        cols = slice(step * 256, (step + 1) * 256)
        upstream[:, cols] = dot(cot_held[...], proj_weight[cols, :], 1, 1).astype(jnp.bfloat16)

    head_of = lax.broadcasted_iota(jnp.int32, (WINDOW, GROUP * HEAD_DIM), 1) // HEAD_DIM
    zero = jnp.zeros((WINDOW, GROUP * HEAD_DIM), jnp.bfloat16)

    def apart(slab):
        return jnp.concatenate([jnp.where(head_of == head, slab, zero) for head in range(GROUP)], axis=0)

    def together(tall):
        merged = tall[:WINDOW]
        for head in range(1, GROUP):
            merged = jnp.where(head_of == head, tall[head * WINDOW : (head + 1) * WINDOW], merged)
        return merged.astype(jnp.bfloat16)

    for window in range(2):
        rows = slice(window * WINDOW, (window + 1) * WINDOW)
        shape = (WINDOW, GROUP * WINDOW)
        key_label = token_labels(lax.broadcasted_iota(jnp.int32, shape, 0), window, place[1], place[2])
        query_label = token_labels(lax.broadcasted_iota(jnp.int32, shape, 1) % WINDOW, window, place[1], place[2])
        bias = jnp.where(key_label == query_label, 0.0, -1000000000.0)
        for group in range(HEADS // GROUP):
            cols = [slice(part * D + group * GROUP * HEAD_DIM, part * D + (group + 1) * GROUP * HEAD_DIM) for part in range(3)]
            query, keys, values = (qkv[rows, at] for at in cols)
            query, grad = apart(query), apart(upstream[rows, cols[0]])
            scores = dot(keys, query, 1, 1) + bias
            expo = jnp.exp(scores - jnp.max(scores, axis=0, keepdims=True))
            probs = expo * (1.0 / jnp.sum(expo, axis=0, keepdims=True))
            low = probs.astype(jnp.bfloat16)
            prob_grad = dot(values, grad, 1, 1)
            inner = jnp.sum(probs * prob_grad, axis=0, keepdims=True)
            score_grad = (probs * (prob_grad - inner)).astype(jnp.bfloat16)
            attended[rows, cols[0]] = together(dot(low, values, 0, 0))
            qkv_grad[rows, cols[0]] = together(dot(score_grad, keys, 0, 0) * HEAD_DIM ** (-0.5))
            qkv_grad[rows, cols[1]] = dot(score_grad, query, 1, 0).astype(jnp.bfloat16)
            qkv_grad[rows, cols[2]] = dot(low, grad, 1, 0).astype(jnp.bfloat16)

    def put(step, grads):
        grads = grads.astype(jnp.bfloat16)
        for half in range(2):
            rows = grads[half * (D // 2) : (half + 1) * (D // 2)]
            for part in range(2):
                tiles[half, :, 2 * step + part] = rows[:, 128 * part : 128 * part + 128].reshape(D // 32, 16, 128)

    tall = normed[...].T
    for step in range(3 * D // 256):
        put(step, dot(tall, qkv_grad[:, step * 256 : (step + 1) * 256], 1, 0))
    tall = attended[...].T
    for step in range(D // 256):
        put(step + 3 * D // 256, dot(tall, cot_held[:, step * 256 : (step + 1) * 256], 1, 0))
    theirs[...] = tiles[1 - place[3]]
    mine[...] = tiles[place[3]]


def rest_kernel(x_held, qkv_grad, qkv_weight, *branch):
    normed_grad = dot(qkv_grad[...], qkv_weight[...], 1, 1)
    x = x_held[...].astype(jnp.float32)
    centered = x - jnp.mean(x, axis=-1, keepdims=True)
    inverse = lax.rsqrt(jnp.mean(centered * centered, axis=-1, keepdims=True) + 1e-05)
    xhat = centered * inverse
    average = jnp.mean(normed_grad, axis=-1, keepdims=True)
    product = jnp.mean(normed_grad * xhat, axis=-1, keepdims=True)
    dx = inverse * (normed_grad - average - xhat * product)
    for kind, target in enumerate(branch):
        chunks = [dx[(4 * window + kind) * QUARTER : (4 * window + kind + 1) * QUARTER] for window in range(2)]
        target[...] = jnp.concatenate(chunks, axis=0).astype(jnp.bfloat16)


HALF_TILES = jax.ShapeDtypeStruct((D // 32, 4 * D // 128, 16, 128), jnp.bfloat16)


def rows_of(count, width=D):
    return jax.ShapeDtypeStruct((count, width), jnp.bfloat16)


def block(place, quarters, qkv_weight, proj_weight):
    return pl.pallas_call(
        block_kernel,
        out_shape=(HALF_TILES, HALF_TILES, rows_of(TOKENS), rows_of(TOKENS, 3 * D)),
        in_specs=[SMEM] + [VMEM] * 6,
        out_specs=(VMEM,) * 4,
        scratch_shapes=[
            pltpu.VMEM((TOKENS, D), jnp.bfloat16),
            pltpu.VMEM((TOKENS, D), jnp.bfloat16),
            pltpu.VMEM((TOKENS, D), jnp.bfloat16),
            pltpu.VMEM((TOKENS, 3 * D), jnp.bfloat16),
            pltpu.VMEM((TOKENS, D), jnp.bfloat16),
            pltpu.VMEM((2,) + HALF_TILES.shape, jnp.bfloat16),
        ],
        compiler_params=pltpu.CompilerParams(vmem_limit_bytes=48 * 2**20),
        cost_estimate=pl.CostEstimate(flops=2 * 10**9, bytes_accessed=6 * 10**6, transcendentals=6 * 10**5),
        name="block",
    )(place, *quarters, qkv_weight, proj_weight)


def rest(x_held, qkv_grad, qkv_weight):
    return pl.pallas_call(
        rest_kernel,
        out_shape=(rows_of(2 * QUARTER),) * 4,
        in_specs=[VMEM] * 3,
        out_specs=(VMEM,) * 4,
        compiler_params=pltpu.CompilerParams(vmem_limit_bytes=48 * 2**20),
        cost_estimate=pl.CostEstimate(flops=5 * 10**8, bytes_accessed=3 * 10**6, transcendentals=300),
        name="rest",
    )(x_held, qkv_grad, qkv_weight)


def added(arrived):
    total = arrived[0].astype(jnp.float32)
    for part in range(1, arrived.shape[0]):
        total = total + arrived[part].astype(jnp.float32)
    return total


def device_groups(members):
    tall, wide = lax.axis_size("y_hi"), lax.axis_size("x")
    cores, y_los = lax.axis_size("core"), lax.axis_size("y_lo")

    def index(z, y, x, core):
        return (((z * tall + y // y_los) * cores + core) * wide + x) * y_los + y % y_los

    return [[index(*at, core) for at in group] for core in range(cores) for group in members(core)]


def chips():
    return lax.axis_size("z"), lax.axis_size("y_hi") * lax.axis_size("y_lo"), lax.axis_size("x")


def near_groups():
    def along(size, core):
        if size == 1:
            return [[0]]
        return [[(2 * at + 2 * core) % size, 2 * at + 1] for at in range(size // 2)]

    def members(core):
        zs, ys, xs = (along(size, core) for size in chips())
        return [[(z, y, x) for z in za for y in ya for x in xa] for za in zs for ya in ys for xa in xs]

    return device_groups(members)


def strided(size):
    step = min(size, 2)
    return [list(range(parity, size, step)) for parity in range(step)]


def middle_groups():
    def members(core):
        z_size, y_size, x_size = chips()
        xs = strided(x_size)
        if core == 0:
            return [[(z, y, x) for x in xa for z in za] for xa in xs for za in strided(z_size) for y in range(y_size)]
        return [[(z, y, x) for x in xa for y in ya] for xa in xs for ya in strided(y_size) for z in range(z_size)]

    return device_groups(members)


def far_groups():
    def members(core):
        z_size, y_size, x_size = chips()
        if core == 0:
            return [[(z, y, x) for y in ya] for ya in strided(y_size) for z in range(z_size) for x in range(x_size)]
        return [[(z, y, x) for z in za] for za in strided(z_size) for y in range(y_size) for x in range(x_size)]

    return device_groups(members)


def swapped(value):
    at = [(z, y, x) for z, y, x in itertools.product(*(range(size) for size in chips()))]
    first, second = device_groups(lambda core: [at])
    return lax.ppermute(value, ALL, [*zip(first, second), *zip(second, first)])


def all_to_all(split, groups):
    return lax.all_to_all(split, ALL, 0, 0, axis_index_groups=groups)


def scattered_sum(tiles, groups):
    count = len(groups[0])
    split = tiles.reshape((count, tiles.shape[0] // count) + tiles.shape[1:])
    return added(all_to_all(split, groups)).astype(jnp.bfloat16)


def exchanged(tiles, groups):
    return all_to_all(jnp.broadcast_to(tiles[None], (len(groups[0]),) + tiles.shape), groups)


def gathered(tiles, groups):
    return exchanged(tiles, groups).reshape((-1,) + tiles.shape[1:])


def untile_kernel(other, place, tiles, *refs):
    qkv_out, proj_out, qkv_held, proj_held, semaphores = refs[-5:]
    first = (1 - place[3] if other else place[3]) * (D // 2)
    chunk = D // 2 // CHUNKS
    copies = []
    for at in range(CHUNKS):
        rows = slice(at * chunk, (at + 1) * chunk)
        for col in range(4 * D // 128):
            strip = tiles[at * chunk // 16 : (at + 1) * chunk // 16, col].reshape(chunk, 128)
            if col < 3 * D // 128:
                qkv_held[rows, 128 * col : 128 * col + 128] = strip
            else:
                proj_held[rows, 128 * col - 3 * D : 128 * col - 3 * D + 128] = strip
        target = pl.ds(pl.multiple_of(first + at * chunk, chunk), chunk)
        for kind, (held, out) in enumerate(((qkv_held, qkv_out), (proj_held, proj_out))):
            copies.append(pltpu.make_async_copy(held.at[rows], out.at[target], semaphores.at[2 * at + kind]))
            copies[-1].start()
    for copy in copies:
        copy.wait()


CHUNKS = 4


def untile(place, tiles, other, so_far=()):
    return pl.pallas_call(
        functools.partial(untile_kernel, other),
        in_specs=[SMEM, VMEM] + [HBM] * len(so_far),
        out_specs=(HBM, HBM),
        out_shape=(rows_of(D, 3 * D), rows_of(D)),
        scratch_shapes=[
            pltpu.VMEM((D // 2, 3 * D), jnp.bfloat16),
            pltpu.VMEM((D // 2, D), jnp.bfloat16),
            pltpu.SemaphoreType.DMA((2 * CHUNKS,)),
        ],
        input_output_aliases={2: 0, 3: 1} if so_far else {},
        compiler_params=pltpu.CompilerParams(vmem_limit_bytes=32 * 2**20),
        cost_estimate=pl.CostEstimate(flops=0, bytes_accessed=2 * 2**20, transcendentals=0),
        name="untile_other" if other else "untile_own",
    )(place, tiles, *so_far)


def per_device(activations, cotangent, qkv_weight, proj_weight):
    lat, lon = lax.axis_index(LAT), lax.axis_index(LON)
    odd = lat % 2 == 1
    lon_edge = jnp.where(odd, lon == lax.axis_size(LON) - 1, lon == 0)
    place = jnp.stack([odd, lat == 0, lon_edge, lax.axis_index("core") == 1]).astype(jnp.int32)
    own, lon, lat, both = pack(place, activations, cotangent)
    own, qkv_weight, proj_weight = lax.optimization_barrier((own, qkv_weight, proj_weight))
    both, lon, lat = moved(both, 3, False), moved(lon, 1, False), moved(lat, 2, False)
    qkv_weight, proj_weight = near_weights(qkv_weight, proj_weight)
    theirs, mine, x_held, qkv_grad = block(place, (own, both, lon, lat), qkv_weight, proj_weight)
    own, lon, lat, both = rest(x_held, qkv_grad, qkv_weight)

    near, middle, far = near_groups(), middle_groups(), far_groups()
    lon = moved(lon, 1, True)
    tiles = (mine.astype(jnp.float32) + swapped(theirs).astype(jnp.float32)).astype(jnp.bfloat16)
    tiles, lat, both = lax.optimization_barrier((tiles.reshape(-1, 16, 128), lat, both))
    tiles, lon, lat = lax.optimization_barrier((scattered_sum(tiles, near), lon, lat))
    tiles, lat = lax.optimization_barrier((scattered_sum(tiles, middle), moved(lat, 2, True)))
    factor = (LEVELS * ROWS * COLS * lax.axis_size(ALL)) ** (-0.5)
    tiles = (added(exchanged(tiles, far)) * factor).astype(jnp.bfloat16)
    tiles, both = lax.optimization_barrier((gathered(tiles, middle), both))
    tiles, both = lax.optimization_barrier((gathered(tiles, near), moved(both, 3, True)))
    tiles = tiles.reshape(HALF_TILES.shape)
    arrived = swapped(tiles)
    grads = untile(place, tiles, False)
    input_grad = unpack(place, cotangent, own, lon, lat, both)
    arrived, grads, input_grad = lax.optimization_barrier((arrived, grads, input_grad))
    qkv_weight_grad, proj_weight_grad = untile(place, arrived, True, grads)
    return (input_grad, qkv_weight_grad, proj_weight_grad)


def over(physical):
    spec = P(None, LAT, LON, None)
    return jax.shard_map(
        per_device,
        mesh=physical,
        in_specs=(spec, spec, P(), P()),
        out_specs=(spec, P(), P()),
        check_vma=False,
    )


def solution(mesh):
    return over(Mesh(mesh.devices.reshape(8, 4, 2, 4, 2), ALL))
```
